32 devices in a mesh: group: 2 (over y), chan: 4 (over z), band: 2 (over x), beam: 2 (over core).
Axes of the slice: x: 2, y: 2, z: 4, core: 2. Of those that a mesh axis runs over, the one named last changes fastest.
Arguments:
- voltages: bfloat16 [2, 1024, 2, 8, 512], P(None, 'chan', 'band', None, 'group'), parts along dimension 4, may hold values from -6 to 6
- gains: float32 [2, 2, 8, 1024], P(None, 'band', 'chan'), may hold values from -5 to 5
- positions: float32 [3, 1024], replicated, may hold values from -4 to 4
- directions: float32 [3, 2048], P(None, ('group', 'beam')), parts along dimension 1, may hold values from -1 to 1
- antenna_row_lookup: int32 [1024], replicated, may hold values from 0 to 1023, each once
- chan_order: int32 [16], replicated, may hold values from 0 to 15, each once
- delays: int32 [4, 2, 8], replicated, may hold values from 0 to 31
Outputs:
- dedispersed: float32 [2, 8, 32, 2048], P('band', 'chan', None, ('group', 'beam')), parts along dimension 3
The draws below stay inside these ranges and needn't reach their ends.
There are 2 independent parts, one for each index of `group`. The reference program is written for one: setup_inputs(seed, part) draws one part's arguments, and reference() takes and returns one part's arrays. A program takes and returns all parts, laid end to end along the dimension named above; an argument that names none is the same for every part. Nothing has to cross between parts.
Inputs may be any that keep to these rules, and one draw needn't show every extreme that they name: `antenna_row_lookup`: each antenna appears once. `chan_order`: each frequency index appears once.
All inputs are finite; a program needn't handle non-finite values.
Results may differ from the reference program's by a relative error of at most 0.004.
Values may be sent and summed in bfloat16 or wider, within the bound.
No kernel may reach another device: no remote copies, remote signals or barrier semaphores. Data moves between devices by JAX's collectives and lax.ppermute only.
A program may use at most 64 MiB of HBM per device.

```python
import math
import jax
import jax.numpy as jnp
from jax import lax

ANTENNA_COUNT = 1024
BEAMS = 1024
SAMPLE_COUNT = 256
INTEG = 8
FREQ_BAND_COUNT = 2
CHANNELS_PER_BAND = 8
CHANNEL_COUNT = 16
TB = 32
ROUNDS = 4


def place_ends(values, key, low, largest):
    extent = values.shape
    index_at = [jax.random.randint(jax.random.fold_in(key, axis), (), 0, extent[axis]) for axis in range(len(extent))]
    values = values.at[tuple(index_at)].set(low)
    longest = extent.index(max(extent))
    index_at[longest] = (index_at[longest] + 1) % extent[longest]
    return values.at[tuple(index_at)].set(largest)


def block_scale(key, shape, cuts, smallest, top_value):
    gain, own = 1.0, jax.random.fold_in(key, 6)
    for position, shards_of in cuts:
        steps = jnp.exp(jax.random.uniform(jax.random.fold_in(own, position), (shards_of,), jnp.float32, smallest / len(cuts), top_value / len(cuts)))
        gain = gain * jnp.repeat(steps, shape[position] // shards_of).reshape([-1 if axis == position else 1 for axis in range(len(shape))])
    return gain


def bell_draw(stream_key, shape, scale, bound, split=(), dtype=jnp.bfloat16):
    values = scale * jax.random.normal(stream_key, shape, jnp.float32)
    if split:
        values = values * block_scale(stream_key, shape, split, -0.22, 0.18)
    return jnp.clip(values, -bound, bound).astype(dtype)


def setup_inputs(seed: int = 0, part: int = 0) -> dict:
    splits = jax.random.split(jax.random.key(seed), 8)
    part_keys = jax.random.split(jax.random.fold_in(splits[7], part), 8)
    voltages = bell_draw(part_keys[0], (2, ANTENNA_COUNT, FREQ_BAND_COUNT, CHANNELS_PER_BAND, SAMPLE_COUNT), 1.0, 6.0, ((1, 4), (2, 2)))
    gains = bell_draw(splits[1], (2, FREQ_BAND_COUNT, CHANNELS_PER_BAND, ANTENNA_COUNT), 0.7, 5.0, ((1, 2), (2, 4)), jnp.float32)
    positions = jnp.clip(jax.random.uniform(splits[2], (3, ANTENNA_COUNT), jnp.float32, -4.0, 4.0), -4.0, 4.0)
    directions = jnp.clip(jax.random.uniform(part_keys[3], (3, BEAMS), jnp.float32, -1.0, 1.0) * block_scale(part_keys[3], (3, BEAMS), ((1, 2),), -0.4, 0.0), -1.0, 1.0)
    antenna_row_lookup = jax.random.permutation(splits[4], ANTENNA_COUNT).astype(jnp.int32)
    chan_order = jax.random.permutation(splits[5], CHANNEL_COUNT).astype(jnp.int32)
    delays = place_ends(jax.random.randint(splits[6], (ROUNDS, FREQ_BAND_COUNT, CHANNELS_PER_BAND), 0, TB), jax.random.fold_in(splits[6], 1), 0, TB - 1).astype(jnp.int32)
    return {"voltages": voltages, "gains": gains, "positions": positions, "directions": directions, "antenna_row_lookup": antenna_row_lookup, "chan_order": chan_order, "delays": delays}


def roll_rows(state, shifts):
    length = state.shape[1]
    doubled = jnp.concatenate([state, state], axis=1)

    def one_row(row, shift):
        return lax.dynamic_slice_in_dim(row, length - shift, length, 0)
    return jax.vmap(one_row)(doubled, shifts)

def pair_round(state, shifts, stride):
    count, length, width = state.shape
    grouped = state.reshape(count // (2 * stride), 2, stride, length, width)
    lower = jnp.broadcast_to(grouped[:, 0:1], grouped.shape).reshape(state.shape)
    upper = jnp.broadcast_to(grouped[:, 1:2], grouped.shape).reshape(state.shape)
    return lower + roll_rows(upper, shifts)

def beam_weights(gain_pair, freq, pos_rows, dirs):
    geometry = pos_rows[0][:, None] * dirs[0][None, :]
    geometry = geometry + pos_rows[1][:, None] * dirs[1][None, :]
    geometry = geometry + pos_rows[2][:, None] * dirs[2][None, :]
    phase = (2.0 * math.pi * freq)[:, None, None] * geometry[None]
    cosine = jnp.cos(phase)
    sine = jnp.sin(phase)
    g_re = gain_pair[0][:, :, None]
    g_im = gain_pair[1][:, :, None]
    factor = 1.0 / math.sqrt(pos_rows.shape[1])
    w_re = ((g_re * cosine + g_im * sine) * factor).astype(jnp.bfloat16)
    w_im = ((g_im * cosine - g_re * sine) * factor).astype(jnp.bfloat16)
    upper_rows = jnp.concatenate([w_re, w_im], axis=2)
    lower_rows = jnp.concatenate([-w_im, w_re], axis=2)
    return jnp.stack([upper_rows, lower_rows], axis=1)

def integrate(power, chans):
    count, samples, width = power.shape
    binned = lax.optimization_barrier(jnp.mean(power.reshape(count, samples // INTEG, INTEG, width), axis=2))
    centred = binned - lax.optimization_barrier(jnp.mean(binned, axis=1, keepdims=True))
    return centred * (1.0 / math.sqrt(chans))

def reference(voltages, gains, positions, directions, antenna_row_lookup, chan_order, delays):
    pos_rows = positions[:, antenna_row_lookup]
    freq = 1.0 + chan_order.astype(jnp.float32) / CHANNEL_COUNT
    voltage_cube = jnp.moveaxis(voltages.reshape(2, ANTENNA_COUNT, CHANNEL_COUNT, SAMPLE_COUNT), 2, 0)
    gain_table_rows = jnp.moveaxis(gains.reshape(2, CHANNEL_COUNT, ANTENNA_COUNT), 1, 0)

    def one_channel(items):
        vol_c, gain_c, freq_c = items
        weights = beam_weights(gain_c[:, None, :], freq_c[None], pos_rows, directions)[0].astype(jnp.float32)
        beams = jnp.einsum('pat,paq->tq', vol_c.astype(jnp.float32), weights)
        half = beams.shape[1] // 2
        power = beams[:, :half] * beams[:, :half] + beams[:, half:] * beams[:, half:]
        return integrate(power[None], CHANNEL_COUNT)[0]
    level = lax.map(one_channel, (voltage_cube, gain_table_rows, freq))
    flat_delays = delays.reshape(ROUNDS, CHANNEL_COUNT)
    for bit in range(ROUNDS):
        level = pair_round(level, flat_delays[bit], 1 << bit)
    return level.reshape(FREQ_BAND_COUNT, CHANNELS_PER_BAND, TB, BEAMS)
```

```python
import math

import jax
import jax.numpy as jnp
from jax import lax
from jax.experimental import pallas as pl
from jax.experimental.pallas import tpu as pltpu
from jax.sharding import PartitionSpec as P

INTEG = 8
VMEM = pl.BlockSpec(memory_space=pltpu.VMEM)
SMEM = pl.BlockSpec(memory_space=pltpu.SMEM)
PARAMS = pltpu.CompilerParams(vmem_limit_bytes=40 * 1024 * 1024)
SIN = (6.283184915580925, -41.34158901325128, 81.59993513909575, -76.61436771142901, 41.342343389037076, -12.470285565721209)
COS = (0.9999992089426497, -19.738979914331107, 64.92864094416844, -85.27141067260794, 58.789407905427666, -21.069178520245686)
ROUNDER = 1.5 * 2.0**23
PHASE_ROWS = 32


def partner(value, axis, mask):
    pairs = [(source, source ^ mask) for source in range(lax.axis_size(axis))]
    return lax.ppermute(value, axis, pairs)


def split_channels(voltages, masks):
    parts, ants, _, chans, samples = voltages.shape
    per_dev = lax.axis_size("beam")

    def kernel(v_ref, *refs):
        outs, wide = refs[: len(masks)], refs[len(masks) :]
        for lane, half in enumerate(wide):
            half[...] = v_ref[0, :, pl.ds(lane * 128, 128)].astype(jnp.float32)
        z = lax.axis_index("chan")
        e = lax.axis_index("beam")
        for mask, out in zip(masks, outs):
            chan = (z ^ mask) * per_dev + e
            for lane, half in enumerate(wide):
                out[0, :, pl.ds(lane * 128, 128)] = half[pl.ds(chan, ants, stride=chans), :].astype(jnp.bfloat16)

    return pl.pallas_call(
        kernel,
        grid=(parts,),
        in_specs=[pl.BlockSpec((1, ants * chans, samples), lambda p: (p, 0, 0))],
        out_specs=[pl.BlockSpec((1, ants, samples), lambda p: (p, 0, 0))] * len(masks),
        out_shape=[jax.ShapeDtypeStruct((parts, ants, samples), jnp.bfloat16)] * len(masks),
        scratch_shapes=[pltpu.VMEM((ants * chans, 128), jnp.float32)] * (samples // 128),
        compiler_params=PARAMS,
        name="split_channels",
    )(voltages.reshape(parts, ants * chans, samples))


def horner(coefs, u):
    total = coefs[-1] * u + coefs[-2]
    for coef in coefs[-3::-1]:
        total = total * u + coef
    return total


def bf16_parts(x):
    first = x.astype(jnp.bfloat16).astype(jnp.float32)
    rest = x - first
    second = rest.astype(jnp.bfloat16).astype(jnp.float32)
    return first, second, rest - second


def make_weights(pos, gain, dirs, chan_order, total, in_band):
    ants, beams = pos.shape[1], dirs.shape[1]
    per_dev = lax.axis_size("beam")
    block = min(beams, 128)
    lanes = min(ants, 512)

    def kernel(order_ref, pos_ref, gain_ref, dir_ref, out, left, right, size, turns):
        @pl.when(pl.program_id(0) == 0)
        def _():
            slot = lax.axis_index("band") * in_band + lax.axis_index("chan") * per_dev + lax.axis_index("beam")
            freq = 1.0 + order_ref[slot].astype(jnp.float32) * (1.0 / total)
            g_re, g_im = gain_ref[0:1, :], gain_ref[1:2, :]
            top = jnp.maximum(jnp.abs(g_re), jnp.abs(g_im))
            low = jnp.minimum(jnp.abs(g_re), jnp.abs(g_im))
            ratio = low / jnp.where(top > 0.0, top, 1.0)
            size[...] = top * jnp.sqrt(1.0 + ratio * ratio) * (1.0 / math.sqrt(ants))
            right[...] = jnp.zeros_like(right)
            left[...] = jnp.zeros_like(left)
            pos_parts = bf16_parts(pos_ref[...] * -freq)
            dir_parts = bf16_parts(dir_ref[...])
            row = 0
            for pos_part in pos_parts:
                for dir_part in dir_parts:
                    right[row : row + 3, :] = pos_part
                    left[row : row + 3, :] = dir_part
                    row += 3
            for part in bf16_parts(jnp.arctan2(g_im, g_re) * (0.5 / math.pi)):
                right[row : row + 1, :] = part
                left[row : row + 1, :] = jnp.ones((1, beams), jnp.float32)
                row += 1

        start = pl.multiple_of(pl.program_id(0) * block, block)
        turns[...] = lax.dot_general(
            left[:, pl.ds(start, block)].astype(jnp.bfloat16),
            right[...].astype(jnp.bfloat16),
            (((0,), (0,)), ((), ())),
            preferred_element_type=jnp.float32,
        )

        def rows(step, carry):
            at = pl.ds(pl.multiple_of(step * 16, 16), 16)
            for lane in range(0, ants, lanes):
                cols = pl.ds(lane, lanes)
                x = turns[at, cols]
                t = x - ((x + ROUNDER) - ROUNDER)
                u = t * t
                scale = size[:, cols]
                out[0, at, cols] = (horner(COS, u) * scale).astype(jnp.bfloat16)
                out[1, at, cols] = (horner(SIN, u) * (t * scale)).astype(jnp.bfloat16)
            return carry

        lax.fori_loop(0, block // 16, rows, 0)

    return pl.pallas_call(
        kernel,
        grid=(beams // block,),
        in_specs=[
            SMEM,
            pl.BlockSpec((3, ants), lambda i: (0, 0)),
            pl.BlockSpec((2, ants), lambda i: (0, 0)),
            pl.BlockSpec((3, beams), lambda i: (0, 0)),
        ],
        out_specs=pl.BlockSpec((2, block, ants), lambda i: (0, i, 0)),
        out_shape=jax.ShapeDtypeStruct((2, beams, ants), jnp.bfloat16),
        scratch_shapes=[
            pltpu.VMEM((PHASE_ROWS, beams), jnp.float32),
            pltpu.VMEM((PHASE_ROWS, ants), jnp.float32),
            pltpu.VMEM((1, ants), jnp.float32),
            pltpu.VMEM((block, ants), jnp.float32),
        ],
        compiler_params=PARAMS,
        name="make_weights",
    )(chan_order, pos, gain, dirs)


def chunk_product(w_ref, chunks, first, beam_rows):
    re = jnp.concatenate([chunk[0] for chunk in chunks], axis=0)
    im = jnp.concatenate([chunk[1] for chunk in chunks], axis=0)
    straight = jnp.concatenate([re, im], axis=1)
    turned = jnp.concatenate([-im, re], axis=1)
    cols = pl.ds(first, re.shape[0])
    dot = lambda a, b: jnp.dot(a, b, preferred_element_type=jnp.float32)
    return dot(w_ref[0, beam_rows, cols], straight) + dot(w_ref[1, beam_rows, cols], turned)


def early_beams(weights, chunks):
    beams = weights.shape[1]
    samples = chunks[0].shape[2]
    step = min(beams, 256)

    def kernel(w_ref, *refs):
        for row in range(0, beams, step):
            rows = pl.ds(row, step)
            refs[-1][rows, :] = chunk_product(w_ref, refs[:-1], 0, rows)

    return pl.pallas_call(
        kernel,
        in_specs=[VMEM] * (1 + len(chunks)),
        out_specs=VMEM,
        out_shape=jax.ShapeDtypeStruct((beams, 2 * samples), jnp.float32),
        compiler_params=PARAMS,
        name="early_beams",
    )(weights, *chunks)


def last_levels(weights, chunks, first, partial, total):
    beams = weights.shape[1]
    samples = chunks[0].shape[2]
    bins = samples // INTEG
    step = min(beams // 2, 256)

    def kernel(w_ref, part_ref, *refs):
        ours, theirs = refs[-2:]
        bin_no = lax.broadcasted_iota(jnp.int32, (bins, samples), 0)
        time = lax.broadcasted_iota(jnp.int32, (bins, samples), 1)
        centre = jnp.where(time // INTEG == bin_no, 1.0 / INTEG, 0.0) - 1.0 / samples
        centre = centre.astype(jnp.bfloat16)
        for row in range(0, beams, step):
            rows = pl.ds(row, step)
            beam = part_ref[rows, :] + chunk_product(w_ref, refs[:-2], first, rows)
            re, im = beam[:, :samples], beam[:, samples:]
            power = re * re + im * im
            high = power.astype(jnp.bfloat16)
            low = (power - high.astype(jnp.float32)).astype(jnp.bfloat16)
            dot = lambda b: lax.dot_general(centre, b, (((1,), (1,)), ((), ())), preferred_element_type=jnp.float32)
            level = (dot(high) + dot(low)) * (1.0 / math.sqrt(total))
            if row < beams // 2:
                ours[:, pl.ds(row, step)] = level
            else:
                theirs[:, pl.ds(row - beams // 2, step)] = level

    return pl.pallas_call(
        kernel,
        in_specs=[VMEM] * (2 + len(chunks)),
        out_specs=[VMEM, VMEM],
        out_shape=[jax.ShapeDtypeStruct((bins, beams // 2), jnp.float32)] * 2,
        compiler_params=PARAMS,
        name="last_levels",
    )(weights, partial, *chunks)


def pick(cond, a, b):
    return jnp.where(cond, a, b), jnp.where(cond, b, a)


def tree_call(kernel, delays, arrays, shape, final, name):
    outs = [jax.ShapeDtypeStruct(shape, jnp.float32)]
    if not final:
        outs.append(jax.ShapeDtypeStruct(shape, jnp.bfloat16))
    return pl.pallas_call(
        kernel,
        in_specs=[SMEM] + [VMEM] * len(arrays),
        out_specs=[VMEM] * len(outs),
        out_shape=outs,
        compiler_params=PARAMS,
        name=name,
    )(delays, *arrays)


def store(outs, slot, value):
    for out in outs:
        out[slot] = value.astype(out.dtype)


def core_round(own, other, delays, in_band):
    per_dev = lax.axis_size("beam")

    def kernel(delay_ref, own_ref, other_ref, *outs):
        base = lax.axis_index("band") * in_band + lax.axis_index("chan") * per_dev
        lower, upper = pick(lax.axis_index("beam") == 0, own_ref[...], other_ref[...])
        for slot in range(per_dev):
            store(outs, slot, lower + pltpu.roll(upper, delay_ref[0, base + slot], 0))

    return tree_call(kernel, delays, [own, other], (per_dev,) + own.shape, False, "core_round")


def axis_rounds(own, sent, axis, bits, level_no, delays, in_band, final):
    per_dev = own.shape[0]
    masks = [1 << bits[0]]
    if len(bits) == 2:
        masks += [2 << bits[0], 3 << bits[0]]
    others = [partner(sent, axis, mask) for mask in masks]

    def kernel(delay_ref, *refs):
        states, outs = refs[: 1 + len(masks)], refs[1 + len(masks) :]
        here = lax.axis_index(axis)
        first_bit = (here >> bits[0]) & 1 == 0
        second_bit = (here >> (bits[0] + 1)) & 1 == 0

        def base(index):
            if axis == "chan":
                return lax.axis_index("band") * in_band + index * per_dev
            return index * in_band + lax.axis_index("chan") * per_dev

        def one_round(a, b, cond, round_no, slot):
            lower, upper = pick(cond, a, b)
            return lower + pltpu.roll(upper, delay_ref[round_no, slot], 0)

        for slot in range(per_dev):
            load = lambda m: states[m][slot].astype(jnp.float32)
            value = one_round(load(0), load(1), first_bit, level_no, base(here) + slot)
            if len(bits) == 2:
                far = base(here ^ masks[1]) + slot
                other = one_round(load(2), load(3), first_bit, level_no, far)
                value = one_round(value, other, second_bit, level_no + 1, base(here) + slot)
            store(outs, slot, value)

    return tree_call(kernel, delays, [own] + others, own.shape, final, "rounds_" + axis)


def shards(voltages, gains, positions, directions, antenna_row_lookup, chan_order, delays):
    chan_count = lax.axis_size("chan")
    band_count = lax.axis_size("band")
    per_dev = gains.shape[2]
    assert per_dev == lax.axis_size("beam") == 2
    in_band = per_dev * chan_count
    total = in_band * band_count
    ants = voltages.shape[1]
    chan_index = lax.axis_index("chan")
    beam_index = lax.axis_index("beam")

    masks = [0] + [m for m in range(1, chan_count) if m != chan_count // 2] + [chan_count // 2]
    blocks = split_channels(voltages, masks)
    far = {m: partner(blocks[masks.index(m)], "chan", m) for m in reversed(masks[1:])}
    chunks = [blocks[0]] + [far[m] for m in masks[1:]]

    order = chan_index ^ jnp.array(masks, jnp.int32)
    rows = antenna_row_lookup.reshape(chan_count, ants)[order].reshape(-1)
    gain = lax.dynamic_index_in_dim(gains[:, 0], beam_index, 1, keepdims=False)
    gain = gain.reshape(2, chan_count, ants)[:, order].reshape(2, -1)
    dirs = jnp.concatenate([directions, partner(directions, "beam", 1)], axis=1)
    weights = make_weights(positions[:, rows], gain, dirs, chan_order, total, in_band)

    partial = early_beams(weights, chunks[:-1])
    ours, theirs = last_levels(weights, chunks[-1:], ants * (chan_count - 1), partial, total)

    flat_delays = delays.reshape(delays.shape[0], total)
    state, sent = core_round(ours, partner(theirs, "beam", 1), flat_delays, in_band)
    level_no = 1
    steps = []
    for axis, count in (("chan", chan_count), ("band", band_count)):
        bits = list(range(count.bit_length() - 1))
        steps += [(axis, bits[i : i + 2]) for i in range(0, len(bits), 2)]
    for number, (axis, bits) in enumerate(steps):
        final = number == len(steps) - 1
        result = axis_rounds(state, sent, axis, bits, level_no, flat_delays, in_band, final)
        if final:
            state = result[0]
        else:
            state, sent = result
        level_no += len(bits)
    return state.reshape(1, per_dev, state.shape[1], state.shape[2])


def solution(mesh):
    placed = (
        P(None, "chan", "band", None, "group"),
        P(None, "band", "chan", None),
        P(),
        P(None, ("group", "beam")),
        P(),
        P(),
        P(),
    )
    return jax.shard_map(
        shards,
        mesh=mesh,
        in_specs=placed,
        out_specs=P("band", "chan", None, ("group", "beam")),
        check_vma=False,
    )
```

```python
import math

import jax
import jax.numpy as jnp
from jax import lax
from jax.experimental import pallas as pl
from jax.experimental.pallas import tpu as pltpu
from jax.sharding import PartitionSpec as P

INTEG = 8
VMEM = pl.BlockSpec(memory_space=pltpu.VMEM)
SMEM = pl.BlockSpec(memory_space=pltpu.SMEM)
PARAMS = pltpu.CompilerParams(vmem_limit_bytes=40 * 1024 * 1024)
SIN = (6.283184915580925, -41.34158901325128, 81.59993513909575, -76.61436771142901, 41.342343389037076, -12.470285565721209)
COS = (0.9999992089426497, -19.738979914331107, 64.92864094416844, -85.27141067260794, 58.789407905427666, -21.069178520245686)
ROUNDER = 1.5 * 2.0**23
PHASE_ROWS = 32


def partner(value, axis, mask):
    pairs = [(source, source ^ mask) for source in range(lax.axis_size(axis))]
    return lax.ppermute(value, axis, pairs)


def split_channels(voltages, pieces, token=None):
    parts, ants, _, chans, samples = voltages.shape
    per_dev = lax.axis_size("beam")
    start = min(first for _, first, _ in pieces)
    stop = max(last for _, _, last in pieces)
    group = max(16, (stop - start) // 4)
    jobs = [(p, first) for first in range(start, stop, group) for p in range(parts)]

    def kernel(v_hbm, *refs):
        outs = refs[-len(pieces) - 4 : -4]
        raw, low, high, sems = refs[-4:]
        z = lax.axis_index("chan")
        e = lax.axis_index("beam")

        def fetch(number):
            p, first = jobs[number]
            rows = v_hbm.at[p, pl.ds(first * chans, group * chans), :]
            return pltpu.make_async_copy(rows, raw.at[number], sems.at[number])

        for number in range(len(jobs)):
            fetch(number).start()
        for number, (p, first) in enumerate(jobs):
            fetch(number).wait()
            slot = number % 2
            for lane, wide in enumerate((low, high)):
                wide[slot] = raw[number, :, pl.ds(lane * 128, 128)].astype(jnp.float32)
            for (mask, piece_first, piece_last), out in zip(pieces, outs):
                if piece_first <= first < piece_last:
                    chan = (z ^ mask) * per_dev + e
                    at = pl.ds(first - piece_first, group)
                    for lane, wide in enumerate((low, high)):
                        rows = wide[slot, pl.ds(chan, group, stride=chans), :]
                        out[p, at, pl.ds(lane * 128, 128)] = rows.astype(jnp.bfloat16)

    assert samples == 256
    tokens = [] if token is None else [token]
    in_hbm = pltpu.with_memory_space_constraint(voltages.reshape(parts, ants * chans, samples), pltpu.HBM)
    return pl.pallas_call(
        kernel,
        in_specs=[pl.BlockSpec(memory_space=pltpu.HBM)] + [pl.BlockSpec(memory_space=pl.ANY)] * len(tokens),
        out_specs=[VMEM] * len(pieces),
        out_shape=[
            jax.ShapeDtypeStruct((parts, last - first, samples), jnp.bfloat16) for _, first, last in pieces
        ],
        scratch_shapes=[
            pltpu.VMEM((len(jobs), group * chans, samples), jnp.bfloat16),
            pltpu.VMEM((2, group * chans, 128), jnp.float32),
            pltpu.VMEM((2, group * chans, 128), jnp.float32),
            pltpu.SemaphoreType.DMA((len(jobs),)),
        ],
        compiler_params=PARAMS,
        name="split_channels",
    )(in_hbm, *tokens)


def horner(coefs, u):
    total = coefs[-1] * u + coefs[-2]
    for coef in coefs[-3::-1]:
        total = total * u + coef
    return total


def bf16_parts(x):
    first = x.astype(jnp.bfloat16).astype(jnp.float32)
    rest = x - first
    second = rest.astype(jnp.bfloat16).astype(jnp.float32)
    return first, second, rest - second


def make_weights(pos, gain, dirs, chan_order, total, in_band):
    ants, beams = pos.shape[1], dirs.shape[1]
    per_dev = lax.axis_size("beam")
    block = min(beams, 128)
    lanes = min(ants, 512)

    def kernel(order_ref, pos_ref, gain_ref, dir_ref, out, left, right, size, turns):
        @pl.when(pl.program_id(0) == 0)
        def _():
            slot = lax.axis_index("band") * in_band + lax.axis_index("chan") * per_dev + lax.axis_index("beam")
            freq = 1.0 + order_ref[slot].astype(jnp.float32) * (1.0 / total)
            g_re, g_im = gain_ref[0:1, :], gain_ref[1:2, :]
            top = jnp.maximum(jnp.abs(g_re), jnp.abs(g_im))
            low = jnp.minimum(jnp.abs(g_re), jnp.abs(g_im))
            ratio = low / jnp.where(top > 0.0, top, 1.0)
            size[...] = top * jnp.sqrt(1.0 + ratio * ratio) * (1.0 / math.sqrt(ants))
            right[...] = jnp.zeros_like(right)
            left[...] = jnp.zeros_like(left)
            pos_parts = bf16_parts(pos_ref[...] * -freq)
            dir_parts = bf16_parts(dir_ref[...])
            row = 0
            for pos_part in pos_parts:
                for dir_part in dir_parts:
                    right[row : row + 3, :] = pos_part
                    left[row : row + 3, :] = dir_part
                    row += 3
            for part in bf16_parts(jnp.arctan2(g_im, g_re) * (0.5 / math.pi)):
                right[row : row + 1, :] = part
                left[row : row + 1, :] = jnp.ones((1, beams), jnp.float32)
                row += 1

        start = pl.multiple_of(pl.program_id(0) * block, block)
        turns[...] = lax.dot_general(
            left[:, pl.ds(start, block)].astype(jnp.bfloat16),
            right[...].astype(jnp.bfloat16),
            (((0,), (0,)), ((), ())),
            preferred_element_type=jnp.float32,
        )

        def rows(step, carry):
            at = pl.ds(pl.multiple_of(step * 16, 16), 16)
            for lane in range(0, ants, lanes):
                cols = pl.ds(lane, lanes)
                x = turns[at, cols]
                t = x - ((x + ROUNDER) - ROUNDER)
                u = t * t
                scale = size[:, cols]
                out[0, at, cols] = (horner(COS, u) * scale).astype(jnp.bfloat16)
                out[1, at, cols] = (horner(SIN, u) * (t * scale)).astype(jnp.bfloat16)
            return carry

        lax.fori_loop(0, block // 16, rows, 0)

    return pl.pallas_call(
        kernel,
        grid=(beams // block,),
        in_specs=[
            SMEM,
            pl.BlockSpec((3, ants), lambda i: (0, 0)),
            pl.BlockSpec((2, ants), lambda i: (0, 0)),
            pl.BlockSpec((3, beams), lambda i: (0, 0)),
        ],
        out_specs=pl.BlockSpec((2, block, ants), lambda i: (0, i, 0)),
        out_shape=jax.ShapeDtypeStruct((2, beams, ants), jnp.bfloat16),
        scratch_shapes=[
            pltpu.VMEM((PHASE_ROWS, beams), jnp.float32),
            pltpu.VMEM((PHASE_ROWS, ants), jnp.float32),
            pltpu.VMEM((1, ants), jnp.float32),
            pltpu.VMEM((block, ants), jnp.float32),
        ],
        compiler_params=PARAMS,
        name="make_weights",
    )(pltpu.with_memory_space_constraint(chan_order, pltpu.SMEM), pos, gain, dirs)


def chunk_product(w_ref, chunks, first, beam_rows):
    re = jnp.concatenate([chunk[0] for chunk in chunks], axis=0)
    im = jnp.concatenate([chunk[1] for chunk in chunks], axis=0)
    straight = jnp.concatenate([re, im], axis=1)
    turned = jnp.concatenate([-im, re], axis=1)
    cols = pl.ds(first, re.shape[0])
    dot = lambda a, b: jnp.dot(a, b, preferred_element_type=jnp.float32)
    return dot(w_ref[0, beam_rows, cols], straight) + dot(w_ref[1, beam_rows, cols], turned)


def early_beams(weights, chunks):
    beams = weights.shape[1]
    samples = chunks[0].shape[2]
    step = min(beams, 256)

    def kernel(w_ref, *refs):
        for row in range(0, beams, step):
            rows = pl.ds(row, step)
            refs[-1][rows, :] = chunk_product(w_ref, refs[:-1], 0, rows)

    return pl.pallas_call(
        kernel,
        in_specs=[VMEM] * (1 + len(chunks)),
        out_specs=VMEM,
        out_shape=jax.ShapeDtypeStruct((beams, 2 * samples), jnp.float32),
        compiler_params=PARAMS,
        name="early_beams",
    )(weights, *chunks)


def last_levels(weights, chunks, first, partial, total):
    beams = weights.shape[1]
    samples = chunks[0].shape[2]
    bins = samples // INTEG
    step = min(beams // 2, 256)

    def kernel(w_ref, part_ref, *refs):
        ours, theirs = refs[-2:]
        bin_no = lax.broadcasted_iota(jnp.int32, (bins, samples), 0)
        time = lax.broadcasted_iota(jnp.int32, (bins, samples), 1)
        centre = jnp.where(time // INTEG == bin_no, 1.0 / INTEG, 0.0) - 1.0 / samples
        centre = centre.astype(jnp.bfloat16)
        for row in range(0, beams, step):
            rows = pl.ds(row, step)
            beam = part_ref[rows, :] + chunk_product(w_ref, refs[:-2], first, rows)
            re, im = beam[:, :samples], beam[:, samples:]
            power = re * re + im * im
            high = power.astype(jnp.bfloat16)
            low = (power - high.astype(jnp.float32)).astype(jnp.bfloat16)
            dot = lambda b: lax.dot_general(centre, b, (((1,), (1,)), ((), ())), preferred_element_type=jnp.float32)
            level = (dot(high) + dot(low)) * (1.0 / math.sqrt(total))
            if row < beams // 2:
                ours[:, pl.ds(row, step)] = level
            else:
                theirs[:, pl.ds(row - beams // 2, step)] = level

    return pl.pallas_call(
        kernel,
        in_specs=[VMEM] * (2 + len(chunks)),
        out_specs=[VMEM, VMEM],
        out_shape=[jax.ShapeDtypeStruct((bins, beams // 2), jnp.float32)] * 2,
        compiler_params=PARAMS,
        name="last_levels",
    )(weights, partial, *chunks)


def pick(cond, a, b):
    return jnp.where(cond, a, b), jnp.where(cond, b, a)


def tree_call(kernel, delays, arrays, shape, final, name):
    outs = [jax.ShapeDtypeStruct(shape, jnp.float32)]
    if not final:
        outs.append(jax.ShapeDtypeStruct(shape, jnp.bfloat16))
    return pl.pallas_call(
        kernel,
        in_specs=[SMEM] + [VMEM] * len(arrays),
        out_specs=[VMEM] * len(outs),
        out_shape=outs,
        compiler_params=PARAMS,
        name=name,
    )(pltpu.with_memory_space_constraint(delays, pltpu.SMEM), *arrays)


def store(outs, slot, value):
    for out in outs:
        out[slot] = value.astype(out.dtype)


def core_round(own, other, delays, in_band):
    per_dev = lax.axis_size("beam")

    def kernel(delay_ref, own_ref, other_ref, *outs):
        base = lax.axis_index("band") * in_band + lax.axis_index("chan") * per_dev
        lower, upper = pick(lax.axis_index("beam") == 0, own_ref[...], other_ref[...])
        for slot in range(per_dev):
            store(outs, slot, lower + pltpu.roll(upper, delay_ref[0, base + slot], 0))

    return tree_call(kernel, delays, [own, other], (per_dev,) + own.shape, False, "core_round")


def axis_rounds(own, sent, axis, bits, level_no, delays, in_band, final):
    per_dev = own.shape[0]
    masks = [1 << bits[0]]
    if len(bits) == 2:
        masks += [2 << bits[0], 3 << bits[0]]
    others = [partner(sent, axis, mask) for mask in masks]

    def kernel(delay_ref, *refs):
        states, outs = refs[: 1 + len(masks)], refs[1 + len(masks) :]
        here = lax.axis_index(axis)
        first_bit = (here >> bits[0]) & 1 == 0
        second_bit = (here >> (bits[0] + 1)) & 1 == 0

        def base(index):
            if axis == "chan":
                return lax.axis_index("band") * in_band + index * per_dev
            return index * in_band + lax.axis_index("chan") * per_dev

        def one_round(a, b, cond, round_no, slot):
            lower, upper = pick(cond, a, b)
            return lower + pltpu.roll(upper, delay_ref[round_no, slot], 0)

        for slot in range(per_dev):
            load = lambda m: states[m][slot].astype(jnp.float32)
            value = one_round(load(0), load(1), first_bit, level_no, base(here) + slot)
            if len(bits) == 2:
                far = base(here ^ masks[1]) + slot
                other = one_round(load(2), load(3), first_bit, level_no, far)
                value = one_round(value, other, second_bit, level_no + 1, base(here) + slot)
            store(outs, slot, value)

    return tree_call(kernel, delays, [own] + others, own.shape, final, "rounds_" + axis)


def shards(voltages, gains, positions, directions, antenna_row_lookup, chan_order, delays):
    chan_count = lax.axis_size("chan")
    band_count = lax.axis_size("band")
    per_dev = gains.shape[2]
    assert per_dev == lax.axis_size("beam") == 2
    in_band = per_dev * chan_count
    total = in_band * band_count
    ants = voltages.shape[1]
    chan_index = lax.axis_index("chan")
    beam_index = lax.axis_index("beam")

    middle = chan_count // 2
    near = list(range(middle))
    distant = list(range(chan_count - 1, middle, -1))
    masks = near + distant + [middle]
    first = split_channels(voltages, [(middle, 0, ants // 2)])
    across = split_channels(voltages, [(m, 0, ants) for m in distant] + [(middle, ants // 2, ants)], first[0])
    beside = split_channels(voltages, [(m, 0, ants) for m in near], across[0])
    first = [partner(first[0], "chan", middle)]
    across = [partner(v, "chan", m) for v, m in zip(across, distant + [middle])]
    beside = [beside[0]] + [partner(v, "chan", m) for v, m in zip(beside[1:], near[1:])]
    chunks = beside + across[:-1] + first + across[-1:]

    order = chan_index ^ jnp.array(masks, jnp.int32)
    rows = antenna_row_lookup.reshape(chan_count, ants)[order].reshape(-1)
    gain = lax.dynamic_index_in_dim(gains[:, 0], beam_index, 1, keepdims=False)
    gain = gain.reshape(2, chan_count, ants)[:, order].reshape(2, -1)
    held, _ = lax.optimization_barrier((directions, chunks[0]))
    dirs = jnp.concatenate([directions, partner(held, "beam", 1)], axis=1)
    weights = make_weights(positions[:, rows], gain, dirs, chan_order, total, in_band)

    partial = early_beams(weights, chunks[:-1])
    ours, theirs = last_levels(weights, chunks[-1:], ants * chan_count - ants // 2, partial, total)

    flat_delays = delays.reshape(delays.shape[0], total)
    state, sent = core_round(ours, partner(theirs, "beam", 1), flat_delays, in_band)
    level_no = 1
    steps = []
    for axis, count in (("chan", chan_count), ("band", band_count)):
        bits = list(range(count.bit_length() - 1))
        steps += [(axis, bits[i : i + 2]) for i in range(0, len(bits), 2)]
    for number, (axis, bits) in enumerate(steps):
        final = number == len(steps) - 1
        result = axis_rounds(state, sent, axis, bits, level_no, flat_delays, in_band, final)
        if final:
            state = result[0]
        else:
            state, sent = result
        level_no += len(bits)
    return state.reshape(1, per_dev, state.shape[1], state.shape[2])


def solution(mesh):
    placed = (
        P(None, "chan", "band", None, "group"),
        P(None, "band", "chan", None),
        P(),
        P(None, ("group", "beam")),
        P(),
        P(),
        P(),
    )
    return jax.shard_map(
        shards,
        mesh=mesh,
        in_specs=placed,
        out_specs=P("band", "chan", None, ("group", "beam")),
        check_vma=False,
    )
```

```python
import math

import jax
import jax.numpy as jnp
from jax import lax
from jax.experimental import pallas as pl
from jax.experimental.pallas import tpu as pltpu
from jax.sharding import PartitionSpec as P

INTEG = 8
VMEM = pl.BlockSpec(memory_space=pltpu.VMEM)
SMEM = pl.BlockSpec(memory_space=pltpu.SMEM)
PARAMS = pltpu.CompilerParams(vmem_limit_bytes=40 * 1024 * 1024)
SIN = (6.283184915580925, -41.34158901325128, 81.59993513909575, -76.61436771142901, 41.342343389037076, -12.470285565721209)
COS = (0.9999992089426497, -19.738979914331107, 64.92864094416844, -85.27141067260794, 58.789407905427666, -21.069178520245686)
ROUNDER = 1.5 * 2.0**23
PHASE_ROWS = 32
LONG = pl.CostEstimate(flops=10**10, bytes_accessed=10**8, transcendentals=10**8)
SHORT = pl.CostEstimate(flops=0, bytes_accessed=0, transcendentals=0)


def partner(value, flips):
    axes = tuple(axis for axis in ("chan", "band", "beam") if axis in dict(flips))
    sizes = [lax.axis_size(axis) for axis in axes]
    flip = 0
    for axis, bit in flips:
        flip ^= (1 << bit) * math.prod(sizes[axes.index(axis) + 1 :])
    pairs = [(source, source ^ flip) for source in range(math.prod(sizes))]
    return lax.ppermute(value, axes, pairs)


def chan_partner(value, mask):
    return partner(value, [("chan", bit) for bit in range(mask.bit_length()) if mask >> bit & 1])


def split_channels(voltages, pieces, from_hbm, token=None):
    parts, ants, _, chans, samples = voltages.shape
    per_dev = lax.axis_size("beam")
    start = min(first for _, first, _ in pieces)
    stop = max(last for _, _, last in pieces)
    group = max(16, (stop - start) // 4)
    jobs = [(p, first) for first in range(start, stop, group) for p in range(parts)]
    lanes = range(0, samples, 128)
    tokens = [] if token is None else [token]

    def kernel(v_ref, *refs):
        refs = refs[len(tokens) :]
        outs, wide, (raw, sems) = refs[: len(pieces)], refs[len(pieces) : -2], refs[-2:]
        z = lax.axis_index("chan")
        e = lax.axis_index("beam")

        def rows(number):
            p, first = jobs[number]
            return v_ref.at[p, pl.ds(first * chans, group * chans), :]

        def fetch(number):
            return pltpu.make_async_copy(rows(number), raw.at[number], sems.at[number])

        if from_hbm:
            for number in range(len(jobs)):
                fetch(number).start()
        for number, (p, first) in enumerate(jobs):
            if from_hbm:
                fetch(number).wait()
            block = raw.at[number] if from_hbm else rows(number)
            slot = number % 2
            for lane, half in zip(lanes, wide):
                half[slot] = block[:, pl.ds(lane, 128)].astype(jnp.float32)
            for (mask, piece_first, piece_last), out in zip(pieces, outs):
                if piece_first <= first < piece_last:
                    chan = (z ^ mask) * per_dev + e
                    at = pl.ds(first - piece_first, group)
                    for lane, half in zip(lanes, wide):
                        out[p, at, pl.ds(lane, 128)] = half[slot, pl.ds(chan, group, stride=chans), :].astype(jnp.bfloat16)

    place = pltpu.HBM if from_hbm else pltpu.VMEM
    raw_slots = len(jobs) if from_hbm else 1
    return pl.pallas_call(
        kernel,
        in_specs=[pl.BlockSpec(memory_space=place)] + [pl.BlockSpec(memory_space=pl.ANY)] * len(tokens),
        out_specs=[VMEM] * len(pieces),
        out_shape=[
            jax.ShapeDtypeStruct((parts, last - first, samples), jnp.bfloat16) for _, first, last in pieces
        ],
        scratch_shapes=[pltpu.VMEM((2, group * chans, 128), jnp.float32)] * len(lanes)
        + [
            pltpu.VMEM((raw_slots, group * chans, samples), jnp.bfloat16),
            pltpu.SemaphoreType.DMA((raw_slots,)),
        ],
        compiler_params=PARAMS,
        name="split_channels",
    )(pltpu.with_memory_space_constraint(voltages.reshape(parts, ants * chans, samples), place), *tokens)


def horner(coefs, u):
    total = coefs[-1] * u + coefs[-2]
    for coef in coefs[-3::-1]:
        total = total * u + coef
    return total


def bf16_parts(x):
    first = x.astype(jnp.bfloat16).astype(jnp.float32)
    rest = x - first
    second = rest.astype(jnp.bfloat16).astype(jnp.float32)
    return first, second, rest - second


def xor_blocks(x, index, count):
    size = x.shape[-1] // count
    for bit in range(count.bit_length() - 1):
        swapped = [x[..., (i ^ (1 << bit)) * size : (i ^ (1 << bit)) * size + size] for i in range(count)]
        x = jnp.where((index >> bit) & 1 == 1, jnp.concatenate(swapped, axis=-1), x)
    return x


def phase_rows(dirs):
    parts = jnp.concatenate(bf16_parts(dirs), axis=0)
    rows = [parts, parts, parts, jnp.ones((3, dirs.shape[1]), jnp.float32)]
    rows.append(jnp.zeros((PHASE_ROWS - 30, dirs.shape[1]), jnp.float32))
    return jnp.concatenate(rows, axis=0).astype(jnp.bfloat16)


def fill_weights(left_ref, right_ref, length_ref, turns, out):
    _, beams, ants = out.shape
    block = turns.shape[0]
    lanes = min(ants, 512)

    def block_of_beams(number, carry):
        start = pl.multiple_of(number * block, block)
        turns[...] = lax.dot_general(
            left_ref[:, pl.ds(start, block)],
            right_ref[...],
            (((0,), (0,)), ((), ())),
            preferred_element_type=jnp.float32,
        )

        def rows(step, carry):
            at = pl.ds(pl.multiple_of(step * 16, 16), 16)
            to = pl.ds(pl.multiple_of(start + step * 16, 16), 16)
            for lane in range(0, ants, lanes):
                cols = pl.ds(lane, lanes)
                x = turns[at, cols]
                t = x - ((x + ROUNDER) - ROUNDER)
                u = t * t
                scale = length_ref[:, cols]
                out[0, to, cols] = (horner(COS, u) * scale).astype(jnp.bfloat16)
                out[1, to, cols] = (horner(SIN, u) * (t * scale)).astype(jnp.bfloat16)
            return carry

        return lax.fori_loop(0, block // 16, rows, carry)

    lax.fori_loop(0, beams // block, block_of_beams, 0)


def our_weights(positions, lookup, gains, dirs, chan_order, masks, total, in_band):
    ants, beams = positions.shape[1], dirs.shape[1]
    per_dev = lax.axis_size("beam")
    size = ants // len(masks)
    lanes = min(ants, 512)

    def in_order(x, z):
        x = xor_blocks(x, z, len(masks))
        return jnp.concatenate([x[..., m * size : m * size + size] for m in masks], axis=-1)

    def kernel(order_ref, pos_ref, look_ref, gain_ref, dir_ref, out, right_ref, length_ref, left, turns):
        z = lax.axis_index("chan")
        e = lax.axis_index("beam")
        slot = lax.axis_index("band") * in_band + z * per_dev + e
        freq = 1.0 + order_ref[slot].astype(jnp.float32) * (1.0 / total)

        g_re = in_order(jnp.where(e == 0, gain_ref[0, 0:1, :], gain_ref[0, 1:2, :]), z)
        g_im = in_order(jnp.where(e == 0, gain_ref[1, 0:1, :], gain_ref[1, 1:2, :]), z)
        top = jnp.maximum(jnp.abs(g_re), jnp.abs(g_im))
        low = jnp.minimum(jnp.abs(g_re), jnp.abs(g_im))
        ratio = low / jnp.where(top > 0.0, top, 1.0)
        length_ref[...] = top * jnp.sqrt(1.0 + ratio * ratio) * (1.0 / math.sqrt(ants))

        parts = [jnp.concatenate([part] * 3, axis=0) for part in bf16_parts(pos_ref[...] * -freq)]
        parts.append(jnp.zeros((PHASE_ROWS - 27, ants), jnp.float32))
        table = jnp.concatenate(parts, axis=0).astype(jnp.bfloat16)
        look = in_order(look_ref[...], z)
        antenna = lax.broadcasted_iota(jnp.int32, (ants, lanes), 0)
        turn_parts = jnp.concatenate(
            [jnp.zeros((27, ants), jnp.float32)]
            + list(bf16_parts(jnp.arctan2(g_im, g_re) * (0.5 / math.pi)))
            + [jnp.zeros((PHASE_ROWS - 30, ants), jnp.float32)],
            axis=0,
        )
        for lane in range(0, ants, lanes):
            chosen = jnp.where(antenna == look[:, lane : lane + lanes], 1.0, 0.0).astype(jnp.bfloat16)
            rows = jnp.dot(table, chosen, preferred_element_type=jnp.float32)
            right_ref[:, pl.ds(lane, lanes)] = (rows + turn_parts[:, lane : lane + lanes]).astype(jnp.bfloat16)
        left[...] = phase_rows(dir_ref[...])
        fill_weights(left, right_ref, length_ref, turns, out)

    return pl.pallas_call(
        kernel,
        in_specs=[SMEM] + [VMEM] * 4,
        out_specs=[VMEM] * 3,
        out_shape=[
            jax.ShapeDtypeStruct((2, beams, ants), jnp.bfloat16),
            jax.ShapeDtypeStruct((PHASE_ROWS, ants), jnp.bfloat16),
            jax.ShapeDtypeStruct((1, ants), jnp.float32),
        ],
        scratch_shapes=[
            pltpu.VMEM((PHASE_ROWS, beams), jnp.bfloat16),
            pltpu.VMEM((min(beams, 128), ants), jnp.float32),
        ],
        compiler_params=PARAMS,
        cost_estimate=LONG,
        name="our_weights",
    )(chan_order, positions, lookup, gains, dirs)


def their_weights(right, length, dirs):
    ants, beams = right.shape[1], dirs.shape[1]

    def kernel(right_ref, length_ref, dir_ref, out, left, turns):
        left[...] = phase_rows(dir_ref[...])
        fill_weights(left, right_ref, length_ref, turns, out)

    return pl.pallas_call(
        kernel,
        in_specs=[VMEM] * 3,
        out_specs=VMEM,
        out_shape=jax.ShapeDtypeStruct((2, beams, ants), jnp.bfloat16),
        scratch_shapes=[
            pltpu.VMEM((PHASE_ROWS, beams), jnp.bfloat16),
            pltpu.VMEM((min(beams, 128), ants), jnp.float32),
        ],
        compiler_params=PARAMS,
        cost_estimate=SHORT,
        name="their_weights",
    )(right, length, dirs)


def chunk_product(w_ref, blocks, first, beam_rows):
    re = jnp.concatenate([re for re, _ in blocks], axis=0)
    im = jnp.concatenate([im for _, im in blocks], axis=0)
    straight = jnp.concatenate([re, im], axis=1)
    turned = jnp.concatenate([-im, re], axis=1)
    cols = pl.ds(first, re.shape[0])
    dot = lambda a, b: jnp.dot(a, b, preferred_element_type=jnp.float32)
    return dot(w_ref[0, beam_rows, cols], straight) + dot(w_ref[1, beam_rows, cols], turned)


def filled(ref, before, after):
    zeros = lambda count: [jnp.zeros((count, ref.shape[2]), ref.dtype)] if count else []
    return [jnp.concatenate(zeros(before) + [ref[p]] + zeros(after), axis=0) for p in range(2)]


def early_beams(weights, chunks, rest):
    half = weights[0].shape[1]
    samples = chunks[0].shape[2]
    step = min(half, 256)

    def kernel(ours_ref, theirs_ref, *refs):
        blocks = [filled(ref, 0, 0) for ref in refs[:-2]] + [filled(refs[-2], 0, rest)]
        for number, w_ref in enumerate((ours_ref, theirs_ref)):
            for row in range(0, half, step):
                product = chunk_product(w_ref, blocks, 0, pl.ds(row, step))
                refs[-1][pl.ds(number * half + row, step), :] = product

    return pl.pallas_call(
        kernel,
        in_specs=[VMEM] * (2 + len(chunks)),
        out_specs=VMEM,
        out_shape=jax.ShapeDtypeStruct((2 * half, 2 * samples), jnp.float32),
        compiler_params=PARAMS,
        cost_estimate=SHORT,
        name="early_beams",
    )(*weights, *chunks)


def two_parts(x):
    high = x.astype(jnp.bfloat16)
    return high, (x - high.astype(jnp.float32)).astype(jnp.bfloat16)


def last_levels(weights, chunk, done, partial, total):
    _, half, ants = weights[0].shape
    samples = chunk.shape[2]
    bins = samples // INTEG
    step = min(half, 256)
    first = ants - chunk.shape[1] - done

    def kernel(ours_ref, theirs_ref, part_ref, chunk_ref, high_ref, low_ref, sent_ref):
        blocks = [filled(chunk_ref, done, 0)]
        bin_no = lax.broadcasted_iota(jnp.int32, (bins, samples), 0)
        time = lax.broadcasted_iota(jnp.int32, (bins, samples), 1)
        centre = jnp.where(time // INTEG == bin_no, 1.0 / INTEG, 0.0) - 1.0 / samples
        centre = centre.astype(jnp.bfloat16)
        for number, w_ref in enumerate((ours_ref, theirs_ref)):
            for row in range(0, half, step):
                rows = pl.ds(row, step)
                beam = part_ref[pl.ds(number * half + row, step), :] + chunk_product(w_ref, blocks, first, rows)
                re, im = beam[:, :samples], beam[:, samples:]
                high, low = two_parts(re * re + im * im)
                dot = lambda b: lax.dot_general(centre, b, (((1,), (1,)), ((), ())), preferred_element_type=jnp.float32)
                high, low = two_parts((dot(high) + dot(low)) * (1.0 / math.sqrt(total)))
                if number == 0:
                    high_ref[:, rows] = high
                    low_ref[:, rows] = low
                else:
                    sent_ref[:, rows] = high

    return pl.pallas_call(
        kernel,
        in_specs=[VMEM] * 4,
        out_specs=[VMEM] * 3,
        out_shape=[jax.ShapeDtypeStruct((bins, half), jnp.bfloat16)] * 3,
        compiler_params=PARAMS,
        name="last_levels",
    )(*weights, partial, chunk)


def tree_maps(delays, steps, bins, in_band):
    per_dev = lax.axis_size("beam")
    sources = [[0] + list(range(1 << len(bits))) for bits in steps]

    def kernel(delay_ref, *outs):
        def place(flips):
            at = {axis: lax.axis_index(axis) for axis in ("band", "chan", "beam")}
            for axis, bit in flips:
                at[axis] = at[axis] ^ (1 << bit)
            return at

        round_no = 0
        for bits, srcs, out in zip(steps, sources, outs):
            row = lax.broadcasted_iota(jnp.int32, out.shape[1:], 0)
            col = lax.broadcasted_iota(jnp.int32, out.shape[1:], 1)
            for slot in range(per_dev):
                shift = jnp.zeros_like(col)
                for number, source in enumerate(srcs):
                    moved = 0
                    for k, (axis, bit) in enumerate(bits):
                        later = [bits[j] for j in range(k + 1, len(bits)) if source >> j & 1]
                        end = place(later)
                        start = place(later + ([bits[k]] if source >> k & 1 else []))
                        delay = delay_ref[round_no + k, end["band"] * in_band + end["chan"] * per_dev + slot]
                        moved = moved + ((start[axis] >> bit) & 1) * delay
                    shift = jnp.where(col // bins == number, moved, shift)
                hit = lax.rem(row - col + len(bits) * bins + out.shape[2] - shift, bins) == 0
                out[slot] = jnp.where(hit, 1.0, 0.0).astype(jnp.bfloat16)
            round_no += len(bits)

    return pl.pallas_call(
        kernel,
        in_specs=[SMEM],
        out_specs=[VMEM] * len(steps),
        out_shape=[jax.ShapeDtypeStruct((per_dev, bins, len(srcs) * bins), jnp.bfloat16) for srcs in sources],
        compiler_params=PARAMS,
        name="tree_maps",
    )(delays)


def tree_step(matrix, states, final):
    slots, bins, _ = matrix.shape
    width = states[0].shape[-1]

    def kernel(map_ref, *refs):
        ins, outs = refs[: len(states)], refs[len(states) :]
        for slot in range(slots):
            column = [ref[...] if len(ref.shape) == 2 else ref[slot] for ref in ins]
            value = jnp.dot(map_ref[slot], jnp.concatenate(column, axis=0), preferred_element_type=jnp.float32)
            for out, part in zip(outs, [value] if final else two_parts(value)):
                out[slot] = part

    dtypes = [jnp.float32] if final else [jnp.bfloat16] * 2
    return pl.pallas_call(
        kernel,
        in_specs=[VMEM] * (1 + len(states)),
        out_specs=[VMEM] * len(dtypes),
        out_shape=[jax.ShapeDtypeStruct((slots, bins, width), dtype) for dtype in dtypes],
        compiler_params=PARAMS,
        name="tree_step",
    )(matrix, *states)


def shards(voltages, gains, positions, directions, antenna_row_lookup, chan_order, delays):
    chan_count = lax.axis_size("chan")
    band_count = lax.axis_size("band")
    per_dev = gains.shape[2]
    assert per_dev == lax.axis_size("beam") == 2
    in_band = per_dev * chan_count
    total = in_band * band_count
    ants, samples = voltages.shape[1], voltages.shape[4]
    bins = samples // INTEG

    middle = chan_count // 2
    near = list(range(middle))
    distant = list(range(chan_count - 1, middle, -1))
    masks = near + distant + [middle]
    cut = ants // 4
    first = split_channels(voltages, [(middle, 0, cut)], True)
    across = split_channels(voltages, [(m, 0, ants) for m in distant] + [(middle, cut, ants)], False, first[0])
    beside = split_channels(voltages, [(m, 0, ants) for m in near], False, across[0])
    first = [chan_partner(first[0], middle)]
    across = [chan_partner(v, m) for v, m in zip(across, distant + [middle])]
    chunks = [beside[0]] + [chan_partner(v, m) for v, m in zip(beside[1:], near[1:])]
    chunks += across[:-1] + first

    lookup = antenna_row_lookup.reshape(1, -1)
    placed, _ = lax.optimization_barrier((positions, beside[0]))
    ours, right, length = our_weights(placed, lookup, gains[:, 0], directions, chan_order, masks, total, in_band)
    held, _ = lax.optimization_barrier((directions, length))
    weights = [ours, their_weights(right, length, partner(held, [("beam", 0)]))]
    partial = early_beams(weights, chunks, ants - cut)

    bits = [("beam", 0)]
    for axis, count in (("chan", chan_count), ("band", band_count)):
        bits += [(axis, bit) for bit in range(count.bit_length() - 1)]
    steps = [bits[i : i + 2] for i in range(0, len(bits), 2)]
    maps = tree_maps(delays.reshape(delays.shape[0], total), steps, bins, in_band)
    partial, *maps = lax.optimization_barrier((partial, *maps))

    high, low, other = last_levels(weights, across[-1], cut, partial, total)
    for number, (step, matrix) in enumerate(zip(steps, maps)):
        states = [high, low]
        for source in range(1, 1 << len(step)):
            flips = [place for k, place in enumerate(step) if source >> k & 1]
            states.append(partner(other if ("beam", 0) in flips else high, flips))
        if number == len(steps) - 1:
            (state,) = tree_step(matrix, states, True)
        else:
            high, low = tree_step(matrix, states, False)
    return state.reshape(1, per_dev, bins, state.shape[2])


def solution(mesh):
    placed = (
        P(None, "chan", "band", None, "group"),
        P(None, "band", "chan", None),
        P(),
        P(None, ("group", "beam")),
        P(),
        P(),
        P(),
    )
    return jax.shard_map(
        shards,
        mesh=mesh,
        in_specs=placed,
        out_specs=P("band", "chan", None, ("group", "beam")),
        check_vma=False,
    )
```

```python
import math

import jax
import jax.numpy as jnp
from jax import lax
from jax.experimental import pallas as pl
from jax.experimental.pallas import tpu as pltpu
from jax.sharding import PartitionSpec as P

INTEG = 8
VMEM = pl.BlockSpec(memory_space=pltpu.VMEM)
SMEM = pl.BlockSpec(memory_space=pltpu.SMEM)
PARAMS = pltpu.CompilerParams(vmem_limit_bytes=40 * 1024 * 1024)
SIN = (6.283184915580925, -41.34158901325128, 81.59993513909575, -76.61436771142901, 41.342343389037076, -12.470285565721209)
COS = (0.9999992089426497, -19.738979914331107, 64.92864094416844, -85.27141067260794, 58.789407905427666, -21.069178520245686)
ROUNDER = 1.5 * 2.0**23
PHASE_ROWS = 32
LONG = pl.CostEstimate(flops=10**10, bytes_accessed=10**8, transcendentals=10**8)
SHORT = pl.CostEstimate(flops=0, bytes_accessed=0, transcendentals=0)


def partner(value, flips):
    axes = tuple(axis for axis in ("chan", "band", "beam") if axis in dict(flips))
    sizes = [lax.axis_size(axis) for axis in axes]
    flip = 0
    for axis, bit in flips:
        flip ^= (1 << bit) * math.prod(sizes[axes.index(axis) + 1 :])
    pairs = [(source, source ^ flip) for source in range(math.prod(sizes))]
    return lax.ppermute(value, axes, pairs)


def chan_partner(value, mask):
    return partner(value, [("chan", bit) for bit in range(mask.bit_length()) if mask >> bit & 1])


def split_channels(voltages, pieces, from_hbm, token=None):
    parts, ants, _, chans, samples = voltages.shape
    per_dev = lax.axis_size("beam")
    start = min(first for _, first, _ in pieces)
    stop = max(last for _, _, last in pieces)
    group = max(16, (stop - start) // 4)
    jobs = [(p, first) for first in range(start, stop, group) for p in range(parts)]
    lanes = range(0, samples, 128)
    tokens = [] if token is None else [token]

    def kernel(v_ref, *refs):
        refs = refs[len(tokens) :]
        outs, wide, (raw, sems) = refs[: len(pieces)], refs[len(pieces) : -2], refs[-2:]
        z = lax.axis_index("chan")
        e = lax.axis_index("beam")

        def rows(number):
            p, first = jobs[number]
            return v_ref.at[p, pl.ds(first * chans, group * chans), :]

        def fetch(number):
            return pltpu.make_async_copy(rows(number), raw.at[number], sems.at[number])

        if from_hbm:
            for number in range(len(jobs)):
                fetch(number).start()
        for number, (p, first) in enumerate(jobs):
            if from_hbm:
                fetch(number).wait()
            block = raw.at[number] if from_hbm else rows(number)
            slot = number % 2
            for lane, half in zip(lanes, wide):
                half[slot] = block[:, pl.ds(lane, 128)].astype(jnp.float32)
            for (mask, piece_first, piece_last), out in zip(pieces, outs):
                if piece_first <= first < piece_last:
                    chan = (z ^ mask) * per_dev + e
                    at = pl.ds(first - piece_first, group)
                    for lane, half in zip(lanes, wide):
                        out[p, at, pl.ds(lane, 128)] = half[slot, pl.ds(chan, group, stride=chans), :].astype(jnp.bfloat16)

    place = pltpu.HBM if from_hbm else pltpu.VMEM
    raw_slots = len(jobs) if from_hbm else 1
    return pl.pallas_call(
        kernel,
        in_specs=[pl.BlockSpec(memory_space=place)] + [pl.BlockSpec(memory_space=pl.ANY)] * len(tokens),
        out_specs=[VMEM] * len(pieces),
        out_shape=[
            jax.ShapeDtypeStruct((parts, last - first, samples), jnp.bfloat16) for _, first, last in pieces
        ],
        scratch_shapes=[pltpu.VMEM((2, group * chans, 128), jnp.float32)] * len(lanes)
        + [
            pltpu.VMEM((raw_slots, group * chans, samples), jnp.bfloat16),
            pltpu.SemaphoreType.DMA((raw_slots,)),
        ],
        compiler_params=PARAMS,
        name="split_channels",
    )(pltpu.with_memory_space_constraint(voltages.reshape(parts, ants * chans, samples), place), *tokens)


def horner(coefs, u):
    total = coefs[-1] * u + coefs[-2]
    for coef in coefs[-3::-1]:
        total = total * u + coef
    return total


def bf16_parts(x):
    first = x.astype(jnp.bfloat16).astype(jnp.float32)
    rest = x - first
    second = rest.astype(jnp.bfloat16).astype(jnp.float32)
    return first, second, rest - second


def xor_blocks(x, index, count):
    size = x.shape[-1] // count
    for bit in range(count.bit_length() - 1):
        swapped = [x[..., (i ^ (1 << bit)) * size : (i ^ (1 << bit)) * size + size] for i in range(count)]
        x = jnp.where((index >> bit) & 1 == 1, jnp.concatenate(swapped, axis=-1), x)
    return x


def phase_rows(dirs):
    parts = jnp.concatenate(bf16_parts(dirs), axis=0)
    rows = [parts, parts, parts, jnp.ones((3, dirs.shape[1]), jnp.float32)]
    rows.append(jnp.zeros((PHASE_ROWS - 30, dirs.shape[1]), jnp.float32))
    return jnp.concatenate(rows, axis=0).astype(jnp.bfloat16)


def fill_weights(left_ref, right_ref, length_ref, turns, out):
    _, beams, ants = out.shape
    block = turns.shape[0]
    lanes = min(ants, 512)

    def block_of_beams(number, carry):
        start = pl.multiple_of(number * block, block)
        turns[...] = lax.dot_general(
            left_ref[:, pl.ds(start, block)],
            right_ref[...],
            (((0,), (0,)), ((), ())),
            preferred_element_type=jnp.float32,
        )

        def rows(step, carry):
            at = pl.ds(pl.multiple_of(step * 16, 16), 16)
            to = pl.ds(pl.multiple_of(start + step * 16, 16), 16)
            for lane in range(0, ants, lanes):
                cols = pl.ds(lane, lanes)
                x = turns[at, cols]
                t = x - ((x + ROUNDER) - ROUNDER)
                u = t * t
                scale = length_ref[:, cols]
                out[0, to, cols] = (horner(COS, u) * scale).astype(jnp.bfloat16)
                out[1, to, cols] = (horner(SIN, u) * (t * scale)).astype(jnp.bfloat16)
            return carry

        return lax.fori_loop(0, block // 16, rows, carry)

    lax.fori_loop(0, beams // block, block_of_beams, 0)


def our_weights(positions, lookup, gains, dirs, chan_order, masks, total, in_band):
    ants, beams = positions.shape[1], dirs.shape[1]
    per_dev = lax.axis_size("beam")
    size = ants // len(masks)
    lanes = min(ants, 512)

    def in_order(x, z):
        x = xor_blocks(x, z, len(masks))
        return jnp.concatenate([x[..., m * size : m * size + size] for m in masks], axis=-1)

    def kernel(order_ref, pos_ref, look_ref, gain_ref, dir_ref, out, right_ref, length_ref, left, turns):
        z = lax.axis_index("chan")
        e = lax.axis_index("beam")
        slot = lax.axis_index("band") * in_band + z * per_dev + e
        freq = 1.0 + order_ref[slot].astype(jnp.float32) * (1.0 / total)

        g_re = in_order(jnp.where(e == 0, gain_ref[0, 0:1, :], gain_ref[0, 1:2, :]), z)
        g_im = in_order(jnp.where(e == 0, gain_ref[1, 0:1, :], gain_ref[1, 1:2, :]), z)
        top = jnp.maximum(jnp.abs(g_re), jnp.abs(g_im))
        low = jnp.minimum(jnp.abs(g_re), jnp.abs(g_im))
        ratio = low / jnp.where(top > 0.0, top, 1.0)
        length_ref[...] = top * jnp.sqrt(1.0 + ratio * ratio) * (1.0 / math.sqrt(ants))

        parts = [jnp.concatenate([part] * 3, axis=0) for part in bf16_parts(pos_ref[...] * -freq)]
        parts.append(jnp.zeros((PHASE_ROWS - 27, ants), jnp.float32))
        table = jnp.concatenate(parts, axis=0).astype(jnp.bfloat16)
        look = in_order(look_ref[...], z)
        antenna = lax.broadcasted_iota(jnp.int32, (ants, lanes), 0)
        turn_parts = jnp.concatenate(
            [jnp.zeros((27, ants), jnp.float32)]
            + list(bf16_parts(jnp.arctan2(g_im, g_re) * (0.5 / math.pi)))
            + [jnp.zeros((PHASE_ROWS - 30, ants), jnp.float32)],
            axis=0,
        )
        for lane in range(0, ants, lanes):
            chosen = jnp.where(antenna == look[:, lane : lane + lanes], 1.0, 0.0).astype(jnp.bfloat16)
            rows = jnp.dot(table, chosen, preferred_element_type=jnp.float32)
            right_ref[:, pl.ds(lane, lanes)] = (rows + turn_parts[:, lane : lane + lanes]).astype(jnp.bfloat16)
        left[...] = phase_rows(dir_ref[...])
        fill_weights(left, right_ref, length_ref, turns, out)

    return pl.pallas_call(
        kernel,
        in_specs=[SMEM] + [VMEM] * 4,
        out_specs=[VMEM] * 3,
        out_shape=[
            jax.ShapeDtypeStruct((2, beams, ants), jnp.bfloat16),
            jax.ShapeDtypeStruct((PHASE_ROWS, ants), jnp.bfloat16),
            jax.ShapeDtypeStruct((1, ants), jnp.float32),
        ],
        scratch_shapes=[
            pltpu.VMEM((PHASE_ROWS, beams), jnp.bfloat16),
            pltpu.VMEM((min(beams, 128), ants), jnp.float32),
        ],
        compiler_params=PARAMS,
        cost_estimate=LONG,
        name="our_weights",
    )(chan_order, positions, lookup, gains, dirs)


def their_weights(right, length, dirs):
    ants, beams = right.shape[1], dirs.shape[1]

    def kernel(right_ref, length_ref, dir_ref, out, left, turns):
        left[...] = phase_rows(dir_ref[...])
        fill_weights(left, right_ref, length_ref, turns, out)

    return pl.pallas_call(
        kernel,
        in_specs=[VMEM] * 3,
        out_specs=VMEM,
        out_shape=jax.ShapeDtypeStruct((2, beams, ants), jnp.bfloat16),
        scratch_shapes=[
            pltpu.VMEM((PHASE_ROWS, beams), jnp.bfloat16),
            pltpu.VMEM((min(beams, 128), ants), jnp.float32),
        ],
        compiler_params=PARAMS,
        cost_estimate=SHORT,
        name="their_weights",
    )(right, length, dirs)


def chunk_product(w_ref, blocks, first, beam_rows):
    re = jnp.concatenate([re for re, _ in blocks], axis=0)
    im = jnp.concatenate([im for _, im in blocks], axis=0)
    straight = jnp.concatenate([re, im], axis=1)
    turned = jnp.concatenate([-im, re], axis=1)
    cols = pl.ds(first, re.shape[0])
    dot = lambda a, b: jnp.dot(a, b, preferred_element_type=jnp.float32)
    return dot(w_ref[0, beam_rows, cols], straight) + dot(w_ref[1, beam_rows, cols], turned)


def filled(ref, before, after):
    zeros = lambda count: [jnp.zeros((count, ref.shape[2]), ref.dtype)] if count else []
    return [jnp.concatenate(zeros(before) + [ref[p]] + zeros(after), axis=0) for p in range(2)]


def early_beams(weights, chunks, rest):
    half = weights[0].shape[1]
    samples = chunks[0].shape[2]
    step = min(half, 512)

    def kernel(ours_ref, theirs_ref, *refs):
        blocks = [filled(ref, 0, 0) for ref in refs[:-2]] + [filled(refs[-2], 0, rest)]
        for number, w_ref in enumerate((ours_ref, theirs_ref)):
            for row in range(0, half, step):
                product = chunk_product(w_ref, blocks, 0, pl.ds(row, step))
                refs[-1][pl.ds(number * half + row, step), :] = product

    return pl.pallas_call(
        kernel,
        in_specs=[VMEM] * (2 + len(chunks)),
        out_specs=VMEM,
        out_shape=jax.ShapeDtypeStruct((2 * half, 2 * samples), jnp.float32),
        compiler_params=PARAMS,
        cost_estimate=SHORT,
        name="early_beams",
    )(*weights, *chunks)


def two_parts(x):
    high = x.astype(jnp.bfloat16)
    return high, (x - high.astype(jnp.float32)).astype(jnp.bfloat16)


def last_levels(weights, chunk, done, partial, total):
    _, half, ants = weights[0].shape
    samples = chunk.shape[2]
    bins = samples // INTEG
    step = min(half, 512)
    first = ants - chunk.shape[1] - done

    def kernel(ours_ref, theirs_ref, part_ref, chunk_ref, high_ref, low_ref, sent_ref):
        blocks = [filled(chunk_ref, done, 0)]
        bin_no = lax.broadcasted_iota(jnp.int32, (bins, samples), 0)
        time = lax.broadcasted_iota(jnp.int32, (bins, samples), 1)
        centre = jnp.where(time // INTEG == bin_no, 1.0 / INTEG, 0.0) - 1.0 / samples
        centre = centre.astype(jnp.bfloat16)
        for number, w_ref in enumerate((ours_ref, theirs_ref)):
            for row in range(0, half, step):
                rows = pl.ds(row, step)
                beam = part_ref[pl.ds(number * half + row, step), :] + chunk_product(w_ref, blocks, first, rows)
                re, im = beam[:, :samples], beam[:, samples:]
                high, low = two_parts(re * re + im * im)
                dot = lambda b: lax.dot_general(centre, b, (((1,), (1,)), ((), ())), preferred_element_type=jnp.float32)
                high, low = two_parts((dot(high) + dot(low)) * (1.0 / math.sqrt(total)))
                if number == 0:
                    high_ref[:, rows] = high
                    low_ref[:, rows] = low
                else:
                    sent_ref[:, rows] = high

    return pl.pallas_call(
        kernel,
        in_specs=[VMEM] * 4,
        out_specs=[VMEM] * 3,
        out_shape=[jax.ShapeDtypeStruct((bins, half), jnp.bfloat16)] * 3,
        compiler_params=PARAMS,
        name="last_levels",
    )(*weights, partial, chunk)


def subsets(bits):
    return [[bit for k, bit in enumerate(bits) if pick >> k & 1] for pick in range(1 << len(bits))]


def tree_maps(delays, stages, bins, in_band):
    per_dev = lax.axis_size("beam")
    shapes = [(per_dev, bins << len(sent), bins * (1 + (1 << len(got)))) for _, got, sent in stages]

    def kernel(delay_ref, *outs):
        def place(flips):
            at = {axis: lax.axis_index(axis) for axis in ("band", "chan", "beam")}
            for axis, bit in flips:
                at[axis] = at[axis] ^ (1 << bit)
            return at

        def total_delay(bits, first_round, target, source, slot):
            moved = 0
            for k, (axis, bit) in enumerate(bits):
                later = [b for b in bits[k + 1 :] if b in target or b in source]
                end = place(target + later)
                start = place(target + later + [b for b in bits[k : k + 1] if b in target or b in source])
                delay = delay_ref[first_round + k, end["band"] * in_band + end["chan"] * per_dev + slot]
                moved = moved + ((start[axis] >> bit) & 1) * delay
            return moved

        first_round = 0
        for (bits, got, sent), out in zip(stages, outs):
            sources = [[]] + subsets(got)
            shape = (bins, out.shape[2])
            row = lax.broadcasted_iota(jnp.int32, shape, 0)
            col = lax.broadcasted_iota(jnp.int32, shape, 1)
            for slot in range(per_dev):
                for number, target in enumerate(subsets(sent)):
                    shift = jnp.zeros_like(col)
                    for place_no, source in enumerate(sources):
                        moved = total_delay(bits, first_round, target, source, slot)
                        shift = jnp.where(col // bins == place_no, moved, shift)
                    hit = lax.rem(row - col + len(bits) * bins + shape[1] - shift, bins) == 0
                    out[slot, pl.ds(number * bins, bins), :] = jnp.where(hit, 1.0, 0.0).astype(jnp.bfloat16)
            first_round += len(bits)

    return pl.pallas_call(
        kernel,
        in_specs=[SMEM],
        out_specs=[VMEM] * len(stages),
        out_shape=[jax.ShapeDtypeStruct(shape, jnp.bfloat16) for shape in shapes],
        compiler_params=PARAMS,
        name="tree_maps",
    )(delays)


def tree_stage(matrix, states, bins, final):
    slots, rows, _ = matrix.shape
    width = states[0].shape[-1]
    targets = rows // bins
    dtypes = [jnp.float32] + [jnp.bfloat16] * (targets - 1) if final else [jnp.bfloat16] * 2

    def kernel(map_ref, *refs):
        ins, outs = refs[: len(states)], refs[len(states) :]
        for slot in range(slots):
            column = [ref[...] if len(ref.shape) == 2 else ref[slot] for ref in ins]
            value = jnp.dot(map_ref[slot], jnp.concatenate(column, axis=0), preferred_element_type=jnp.float32)
            parts = [value[t * bins : t * bins + bins] for t in range(targets)] if final else two_parts(value)
            for out, part in zip(outs, parts):
                out[slot] = part.astype(out.dtype)

    return pl.pallas_call(
        kernel,
        in_specs=[VMEM] * (1 + len(states)),
        out_specs=[VMEM] * len(dtypes),
        out_shape=[jax.ShapeDtypeStruct((slots, bins, width), dtype) for dtype in dtypes],
        compiler_params=PARAMS,
        name="tree_stage",
    )(matrix, *states)


def tree_sum(values):
    def kernel(*refs):
        total = refs[0][...]
        for ref in refs[1:-1]:
            total = total + ref[...].astype(jnp.float32)
        refs[-1][...] = total

    return pl.pallas_call(
        kernel,
        in_specs=[VMEM] * len(values),
        out_specs=VMEM,
        out_shape=jax.ShapeDtypeStruct(values[0].shape, jnp.float32),
        compiler_params=PARAMS,
        name="tree_sum",
    )(*values)


def shards(voltages, gains, positions, directions, antenna_row_lookup, chan_order, delays):
    chan_count = lax.axis_size("chan")
    band_count = lax.axis_size("band")
    per_dev = gains.shape[2]
    assert per_dev == lax.axis_size("beam") == 2
    in_band = per_dev * chan_count
    total = in_band * band_count
    ants, samples = voltages.shape[1], voltages.shape[4]
    bins = samples // INTEG

    middle = chan_count // 2
    near = list(range(middle))
    distant = list(range(chan_count - 1, middle, -1))
    masks = near + distant + [middle]
    cut = ants // 2
    first = list(split_channels(voltages, [(middle, 0, cut)], True))
    copied, first[0] = lax.optimization_barrier((voltages, first[0]))
    across = split_channels(copied, [(m, 0, ants) for m in distant] + [(middle, cut, ants)], False, first[0])
    beside = split_channels(copied, [(m, 0, ants) for m in near], False, across[0])
    first = [chan_partner(first[0], middle)]
    across = [chan_partner(v, m) for v, m in zip(across, distant + [middle])]
    chunks = [beside[0]] + [chan_partner(v, m) for v, m in zip(beside[1:], near[1:])]
    chunks += across[:-1] + first

    lookup = antenna_row_lookup.reshape(1, -1)
    placed, _ = lax.optimization_barrier((positions, beside[0]))
    ours, right, length = our_weights(placed, lookup, gains[:, 0], directions, chan_order, masks, total, in_band)
    held, _ = lax.optimization_barrier((directions, length))
    weights = [ours, their_weights(right, length, partner(held, [("beam", 0)]))]
    partial = early_beams(weights, chunks, ants - cut)

    bits = [("beam", 0)]
    for axis, count in (("chan", chan_count), ("band", band_count)):
        bits += [(axis, bit) for bit in range(count.bit_length() - 1)]
    last = bits[-4:]
    got = [bit for bit in last if bit in (("beam", 0), ("chan", chan_count.bit_length() - 2))]
    got += [bit for bit in last[::-1] if bit not in got][: 2 - len(got)]
    stages = [(pair, pair, []) for pair in (bits[i : i + 2] for i in range(0, len(bits) - 4, 2))]
    stages.append((last, got, [bit for bit in last if bit not in got]))
    maps = tree_maps(delays.reshape(delays.shape[0], total), stages, bins, in_band)
    partial, *maps = lax.optimization_barrier((partial, *maps))

    high, low, other = last_levels(weights, across[-1], cut, partial, total)
    for (_, got, sent), matrix in zip(stages, maps):
        states = [high, low]
        for flips in subsets(got)[1:]:
            states.append(partner(other if ("beam", 0) in flips else high, flips))
        result = tree_stage(matrix, states, bins, bool(sent))
        if not sent:
            high, low = result
    sums = [result[0]] + [partner(value, flips) for value, flips in zip(result[1:], subsets(sent)[1:])]
    return tree_sum(sums).reshape(1, per_dev, bins, high.shape[-1])


def solution(mesh):
    placed = (
        P(None, "chan", "band", None, "group"),
        P(None, "band", "chan", None),
        P(),
        P(None, ("group", "beam")),
        P(),
        P(),
        P(),
    )
    return jax.shard_map(
        shards,
        mesh=mesh,
        in_specs=placed,
        out_specs=P("band", "chan", None, ("group", "beam")),
        check_vma=False,
    )
```

```python
import math

import jax
import jax.numpy as jnp
from jax import lax
from jax.experimental import pallas as pl
from jax.experimental.pallas import tpu as pltpu
from jax.sharding import PartitionSpec as P

INTEG = 8
VMEM = pl.BlockSpec(memory_space=pltpu.VMEM)
SMEM = pl.BlockSpec(memory_space=pltpu.SMEM)
PARAMS = pltpu.CompilerParams(vmem_limit_bytes=40 * 1024 * 1024)
SIN = (6.283184915580925, -41.34158901325128, 81.59993513909575, -76.61436771142901, 41.342343389037076, -12.470285565721209)
COS = (0.9999992089426497, -19.738979914331107, 64.92864094416844, -85.27141067260794, 58.789407905427666, -21.069178520245686)
ROUNDER = 1.5 * 2.0**23
PHASE_ROWS = 32
LONG = pl.CostEstimate(flops=10**10, bytes_accessed=10**8, transcendentals=10**8)
SHORT = pl.CostEstimate(flops=0, bytes_accessed=0, transcendentals=0)


def partner(value, flips):
    axes = tuple(axis for axis in ("chan", "band", "beam") if axis in dict(flips))
    sizes = [lax.axis_size(axis) for axis in axes]
    flip = 0
    for axis, bit in flips:
        flip ^= (1 << bit) * math.prod(sizes[axes.index(axis) + 1 :])
    pairs = [(source, source ^ flip) for source in range(math.prod(sizes))]
    return lax.ppermute(value, axes, pairs)


def chan_partner(value, mask):
    return partner(value, [("chan", bit) for bit in range(mask.bit_length()) if mask >> bit & 1])


def split_channels(voltages, pieces, from_hbm, token=None):
    parts, ants, _, chans, samples = voltages.shape
    per_dev = lax.axis_size("beam")
    start = min(first for _, first, _ in pieces)
    stop = max(last for _, _, last in pieces)
    group = max(16, (stop - start) // 4)
    jobs = [(p, first) for first in range(start, stop, group) for p in range(parts)]
    lanes = range(0, samples, 128)
    tokens = [] if token is None else [token]

    def kernel(v_ref, *refs):
        refs = refs[len(tokens) :]
        outs, wide, (raw, sems) = refs[: len(pieces)], refs[len(pieces) : -2], refs[-2:]
        z = lax.axis_index("chan")
        e = lax.axis_index("beam")

        def rows(number):
            p, first = jobs[number]
            return v_ref.at[p, pl.ds(first * chans, group * chans), :]

        def fetch(number):
            return pltpu.make_async_copy(rows(number), raw.at[number], sems.at[number])

        if from_hbm:
            for number in range(len(jobs)):
                fetch(number).start()
        for number, (p, first) in enumerate(jobs):
            if from_hbm:
                fetch(number).wait()
            block = raw.at[number] if from_hbm else rows(number)
            slot = number % 2
            for lane, half in zip(lanes, wide):
                half[slot] = block[:, pl.ds(lane, 128)].astype(jnp.float32)
            for (mask, piece_first, piece_last), out in zip(pieces, outs):
                if piece_first <= first < piece_last:
                    chan = (z ^ mask) * per_dev + e
                    at = pl.ds(first - piece_first, group)
                    for lane, half in zip(lanes, wide):
                        out[p, at, pl.ds(lane, 128)] = half[slot, pl.ds(chan, group, stride=chans), :].astype(jnp.bfloat16)

    place = pltpu.HBM if from_hbm else pltpu.VMEM
    raw_slots = len(jobs) if from_hbm else 1
    return pl.pallas_call(
        kernel,
        in_specs=[pl.BlockSpec(memory_space=place)] + [pl.BlockSpec(memory_space=pl.ANY)] * len(tokens),
        out_specs=[VMEM] * len(pieces),
        out_shape=[
            jax.ShapeDtypeStruct((parts, last - first, samples), jnp.bfloat16) for _, first, last in pieces
        ],
        scratch_shapes=[pltpu.VMEM((2, group * chans, 128), jnp.float32)] * len(lanes)
        + [
            pltpu.VMEM((raw_slots, group * chans, samples), jnp.bfloat16),
            pltpu.SemaphoreType.DMA((raw_slots,)),
        ],
        compiler_params=PARAMS,
        name="split_channels",
    )(pltpu.with_memory_space_constraint(voltages.reshape(parts, ants * chans, samples), place), *tokens)


def horner(coefs, u):
    total = coefs[-1] * u + coefs[-2]
    for coef in coefs[-3::-1]:
        total = total * u + coef
    return total


def bf16_parts(x):
    first = x.astype(jnp.bfloat16).astype(jnp.float32)
    rest = x - first
    second = rest.astype(jnp.bfloat16).astype(jnp.float32)
    return first, second, rest - second


def xor_blocks(x, index, count):
    size = x.shape[-1] // count
    for bit in range(count.bit_length() - 1):
        swapped = [x[..., (i ^ (1 << bit)) * size : (i ^ (1 << bit)) * size + size] for i in range(count)]
        x = jnp.where((index >> bit) & 1 == 1, jnp.concatenate(swapped, axis=-1), x)
    return x


def phase_rows(dirs):
    parts = jnp.concatenate(bf16_parts(dirs), axis=0)
    rows = [parts, parts, parts, jnp.ones((3, dirs.shape[1]), jnp.float32)]
    rows.append(jnp.zeros((PHASE_ROWS - 30, dirs.shape[1]), jnp.float32))
    return jnp.concatenate(rows, axis=0).astype(jnp.bfloat16)


def fill_weights(left_ref, right_ref, length_ref, turns, out):
    _, beams, ants = out.shape
    block = turns.shape[0]
    lanes = min(ants, 512)

    def block_of_beams(number, carry):
        start = pl.multiple_of(number * block, block)
        turns[...] = lax.dot_general(
            left_ref[:, pl.ds(start, block)],
            right_ref[...],
            (((0,), (0,)), ((), ())),
            preferred_element_type=jnp.float32,
        )

        def rows(step, carry):
            at = pl.ds(pl.multiple_of(step * 16, 16), 16)
            to = pl.ds(pl.multiple_of(start + step * 16, 16), 16)
            for lane in range(0, ants, lanes):
                cols = pl.ds(lane, lanes)
                x = turns[at, cols]
                t = x - ((x + ROUNDER) - ROUNDER)
                u = t * t
                scale = length_ref[:, cols]
                out[0, to, cols] = (horner(COS, u) * scale).astype(jnp.bfloat16)
                out[1, to, cols] = (horner(SIN, u) * (t * scale)).astype(jnp.bfloat16)
            return carry

        return lax.fori_loop(0, block // 16, rows, carry)

    lax.fori_loop(0, beams // block, block_of_beams, 0)


def our_weights(positions, lookup, gains, dirs, chan_order, masks, total, in_band):
    ants, beams = positions.shape[1], dirs.shape[1]
    per_dev = lax.axis_size("beam")
    size = ants // len(masks)
    lanes = min(ants, 512)

    def in_order(x, z):
        x = xor_blocks(x, z, len(masks))
        return jnp.concatenate([x[..., m * size : m * size + size] for m in masks], axis=-1)

    def kernel(order_ref, pos_ref, look_ref, gain_ref, dir_ref, out, right_ref, length_ref, left, turns):
        z = lax.axis_index("chan")
        e = lax.axis_index("beam")
        slot = lax.axis_index("band") * in_band + z * per_dev + e
        freq = 1.0 + order_ref[slot].astype(jnp.float32) * (1.0 / total)

        g_re = in_order(jnp.where(e == 0, gain_ref[0, 0:1, :], gain_ref[0, 1:2, :]), z)
        g_im = in_order(jnp.where(e == 0, gain_ref[1, 0:1, :], gain_ref[1, 1:2, :]), z)
        top = jnp.maximum(jnp.abs(g_re), jnp.abs(g_im))
        low = jnp.minimum(jnp.abs(g_re), jnp.abs(g_im))
        ratio = low / jnp.where(top > 0.0, top, 1.0)
        length_ref[...] = top * jnp.sqrt(1.0 + ratio * ratio) * (1.0 / math.sqrt(ants))

        parts = [jnp.concatenate([part] * 3, axis=0) for part in bf16_parts(pos_ref[...] * -freq)]
        parts.append(jnp.zeros((PHASE_ROWS - 27, ants), jnp.float32))
        table = jnp.concatenate(parts, axis=0).astype(jnp.bfloat16)
        look = in_order(look_ref[...], z)
        antenna = lax.broadcasted_iota(jnp.int32, (ants, lanes), 0)
        turn_parts = jnp.concatenate(
            [jnp.zeros((27, ants), jnp.float32)]
            + list(bf16_parts(jnp.arctan2(g_im, g_re) * (0.5 / math.pi)))
            + [jnp.zeros((PHASE_ROWS - 30, ants), jnp.float32)],
            axis=0,
        )
        for lane in range(0, ants, lanes):
            chosen = jnp.where(antenna == look[:, lane : lane + lanes], 1.0, 0.0).astype(jnp.bfloat16)
            rows = jnp.dot(table, chosen, preferred_element_type=jnp.float32)
            right_ref[:, pl.ds(lane, lanes)] = (rows + turn_parts[:, lane : lane + lanes]).astype(jnp.bfloat16)
        left[...] = phase_rows(dir_ref[...])
        fill_weights(left, right_ref, length_ref, turns, out)

    return pl.pallas_call(
        kernel,
        in_specs=[SMEM] + [VMEM] * 4,
        out_specs=[VMEM] * 3,
        out_shape=[
            jax.ShapeDtypeStruct((2, beams, ants), jnp.bfloat16),
            jax.ShapeDtypeStruct((PHASE_ROWS, ants), jnp.bfloat16),
            jax.ShapeDtypeStruct((1, ants), jnp.float32),
        ],
        scratch_shapes=[
            pltpu.VMEM((PHASE_ROWS, beams), jnp.bfloat16),
            pltpu.VMEM((min(beams, 128), ants), jnp.float32),
        ],
        compiler_params=PARAMS,
        cost_estimate=LONG,
        name="our_weights",
    )(chan_order, positions, lookup, gains, dirs)


def their_weights(right, length, dirs):
    ants, beams = right.shape[1], dirs.shape[1]

    def kernel(right_ref, length_ref, dir_ref, out, left, turns):
        left[...] = phase_rows(dir_ref[...])
        fill_weights(left, right_ref, length_ref, turns, out)

    return pl.pallas_call(
        kernel,
        in_specs=[VMEM] * 3,
        out_specs=VMEM,
        out_shape=jax.ShapeDtypeStruct((2, beams, ants), jnp.bfloat16),
        scratch_shapes=[
            pltpu.VMEM((PHASE_ROWS, beams), jnp.bfloat16),
            pltpu.VMEM((min(beams, 128), ants), jnp.float32),
        ],
        compiler_params=PARAMS,
        cost_estimate=SHORT,
        name="their_weights",
    )(right, length, dirs)


def chunk_product(w_ref, blocks, first, beam_rows):
    re = jnp.concatenate([re for re, _ in blocks], axis=0)
    im = jnp.concatenate([im for _, im in blocks], axis=0)
    straight = jnp.concatenate([re, im], axis=1)
    turned = jnp.concatenate([-im, re], axis=1)
    cols = pl.ds(first, re.shape[0])
    dot = lambda a, b: jnp.dot(a, b, preferred_element_type=jnp.float32)
    return dot(w_ref[0, beam_rows, cols], straight) + dot(w_ref[1, beam_rows, cols], turned)


HIGH_EXTRA, OTHER_EXTRA = 1, 0
SUM_EXTRA = (1, 0, 2)


def filled(ref, before, after):
    zeros = lambda count: [jnp.zeros((count, ref.shape[2]), ref.dtype)] if count else []
    return [jnp.concatenate(zeros(before) + [ref[p]] + zeros(after), axis=0) for p in range(2)]


def early_beams(weights, chunks, first, rest, partial=None):
    half = weights[0].shape[1]
    samples = chunks[0].shape[2]
    step = min(half, 256)
    before = [] if partial is None else [partial]

    def kernel(ours_ref, theirs_ref, *refs):
        refs, out = refs[:-1], refs[-1]
        blocks = [filled(ref, 0, 0) for ref in refs[len(before) : -1]] + [filled(refs[-1], 0, rest)]
        for number, w_ref in enumerate((ours_ref, theirs_ref)):
            for row in range(0, half, step):
                product = chunk_product(w_ref, blocks, first, pl.ds(row, step))
                at = pl.ds(number * half + row, step)
                out[at, :] = product + refs[0][at, :] if before else product

    return pl.pallas_call(
        kernel,
        in_specs=[VMEM] * (2 + len(before) + len(chunks)),
        out_specs=VMEM,
        out_shape=jax.ShapeDtypeStruct((2 * half, 2 * samples), jnp.float32),
        compiler_params=PARAMS,
        cost_estimate=SHORT,
        name="early_beams",
    )(*weights, *before, *chunks)


def two_parts(x):
    high = x.astype(jnp.bfloat16)
    return high, (x - high.astype(jnp.float32)).astype(jnp.bfloat16)


def message(blocks, width, extra):
    return jax.ShapeDtypeStruct((blocks * width // 128 + 16 * extra, 128), jnp.bfloat16)


def put(ref, first, value):
    bins, width = value.shape
    for lane in range(0, width, 128):
        ref[pl.ds(first, bins), :] = value[:, lane : lane + 128].astype(ref.dtype)
        first += bins
    return first


def take(ref, number, bins, width):
    first = number * bins * width // 128
    pieces = [ref[pl.ds(first + lane // 128 * bins, bins), :] for lane in range(0, width, 128)]
    return jnp.concatenate(pieces, axis=1)


def pad(ref, first):
    if first < ref.shape[0]:
        ref[pl.ds(first, ref.shape[0] - first), :] = jnp.zeros((ref.shape[0] - first, 128), ref.dtype)


def last_levels(weights, chunk, partial, total):
    _, half, ants = weights[0].shape
    samples = chunk.shape[2]
    bins = samples // INTEG
    count = chunk.shape[1]
    first = ants - count

    def kernel(ours_ref, theirs_ref, part_ref, chunk_ref, high_ref, low_ref, sent_ref):
        re, im = chunk_ref[0], chunk_ref[1]
        antennas = jnp.concatenate(
            [jnp.concatenate([re, im], axis=1), jnp.concatenate([-im, re], axis=1)], axis=0
        )
        bin_no = lax.broadcasted_iota(jnp.int32, (bins, samples), 0)
        time = lax.broadcasted_iota(jnp.int32, (bins, samples), 1)
        centre = jnp.where(time // INTEG == bin_no, 1.0 / INTEG, 0.0) - 1.0 / samples
        centre = jnp.concatenate([centre, centre], axis=1).astype(jnp.bfloat16)
        for number, w_ref in enumerate((ours_ref, theirs_ref)):
            both = jnp.concatenate([w_ref[0, :, pl.ds(first, count)], w_ref[1, :, pl.ds(first, count)]], axis=1)
            beam = part_ref[pl.ds(number * half, half), :] + jnp.dot(both, antennas, preferred_element_type=jnp.float32)
            re, im = beam[:, :samples], beam[:, samples:]
            high, low = two_parts(re * re + im * im)
            parts = jnp.concatenate([high, low], axis=1)
            level = lax.dot_general(centre, parts, (((1,), (1,)), ((), ())), preferred_element_type=jnp.float32)
            high, low = two_parts(level * (1.0 / math.sqrt(total)))
            if number == 0:
                pad(high_ref, put(high_ref, 0, high))
                put(low_ref, 0, low)
            else:
                pad(sent_ref, put(sent_ref, 0, high))

    return pl.pallas_call(
        kernel,
        in_specs=[VMEM] * 4,
        out_specs=[VMEM] * 3,
        out_shape=[message(bins, half, HIGH_EXTRA), message(bins, half, 0), message(bins, half, OTHER_EXTRA)],
        compiler_params=PARAMS,
        name="last_levels",
    )(*weights, partial, chunk)


def subsets(bits):
    return [[bit for k, bit in enumerate(bits) if pick >> k & 1] for pick in range(1 << len(bits))]


def tree_maps(delays, stages, bins, in_band):
    per_dev = lax.axis_size("beam")
    shapes = [(per_dev, bins << len(sent), bins * (1 + (1 << len(got)))) for _, got, sent in stages]

    def kernel(delay_ref, *outs):
        def place(flips):
            at = {axis: lax.axis_index(axis) for axis in ("band", "chan", "beam")}
            for axis, bit in flips:
                at[axis] = at[axis] ^ (1 << bit)
            return at

        def total_delay(bits, first_round, target, source, slot):
            moved = 0
            for k, (axis, bit) in enumerate(bits):
                later = [b for b in bits[k + 1 :] if b in target or b in source]
                end = place(target + later)
                start = place(target + later + [b for b in bits[k : k + 1] if b in target or b in source])
                delay = delay_ref[first_round + k, end["band"] * in_band + end["chan"] * per_dev + slot]
                moved = moved + ((start[axis] >> bit) & 1) * delay
            return moved

        first_round = 0
        for (bits, got, sent), out in zip(stages, outs):
            sources = [[]] + subsets(got)
            shape = (bins, out.shape[2])
            row = lax.broadcasted_iota(jnp.int32, shape, 0)
            col = lax.broadcasted_iota(jnp.int32, shape, 1)
            for slot in range(per_dev):
                for number, target in enumerate(subsets(sent)):
                    shift = jnp.zeros_like(col)
                    for place_no, source in enumerate(sources):
                        moved = total_delay(bits, first_round, target, source, slot)
                        shift = jnp.where(col // bins == place_no, moved, shift)
                    hit = lax.rem(row - col + len(bits) * bins + shape[1] - shift, bins) == 0
                    out[slot, pl.ds(number * bins, bins), :] = jnp.where(hit, 1.0, 0.0).astype(jnp.bfloat16)
            first_round += len(bits)

    return pl.pallas_call(
        kernel,
        in_specs=[SMEM],
        out_specs=[VMEM] * len(stages),
        out_shape=[jax.ShapeDtypeStruct(shape, jnp.bfloat16) for shape in shapes],
        compiler_params=PARAMS,
        name="tree_maps",
    )(delays)


def tree_stage(matrix, states, bins, width, final):
    slots, rows, _ = matrix.shape
    targets = rows // bins
    blocks = bins * slots
    if final:
        shapes = [jax.ShapeDtypeStruct((slots, bins, width), jnp.float32)]
        shapes += [message(blocks, width, extra) for extra in SUM_EXTRA[: targets - 1]]
    else:
        shapes = [message(blocks, width, 0)] * 2

    def kernel(map_ref, *refs):
        ins, outs = refs[: len(states)], refs[len(states) :]
        row = 0
        for slot in range(slots):
            column = [take(ref, slot if ref.shape[0] >= blocks * width // 128 else 0, bins, width) for ref in ins]
            value = jnp.dot(map_ref[slot], jnp.concatenate(column, axis=0), preferred_element_type=jnp.float32)
            if final:
                outs[0][slot] = value[:bins]
                parts = [value[t * bins : t * bins + bins] for t in range(1, targets)]
            else:
                parts = two_parts(value)
            for out, part in zip(outs[-len(parts) :], parts):
                after = put(out, row, part)
            row = after
        for out in outs[-len(parts) :]:
            pad(out, row)

    return pl.pallas_call(
        kernel,
        in_specs=[VMEM] * (1 + len(states)),
        out_specs=[VMEM] * len(shapes),
        out_shape=shapes,
        compiler_params=PARAMS,
        name="tree_stage",
    )(matrix, *states)


def tree_sum(own, received):
    slots, bins, width = own.shape

    def kernel(own_ref, *refs):
        for slot in range(slots):
            total = own_ref[slot]
            for ref in refs[:-1]:
                total = total + take(ref, slot, bins, width).astype(jnp.float32)
            refs[-1][slot] = total

    return pl.pallas_call(
        kernel,
        in_specs=[VMEM] * (1 + len(received)),
        out_specs=VMEM,
        out_shape=jax.ShapeDtypeStruct(own.shape, jnp.float32),
        compiler_params=PARAMS,
        name="tree_sum",
    )(own, *received)


def shards(voltages, gains, positions, directions, antenna_row_lookup, chan_order, delays):
    chan_count = lax.axis_size("chan")
    band_count = lax.axis_size("band")
    per_dev = gains.shape[2]
    assert per_dev == lax.axis_size("beam") == 2
    in_band = per_dev * chan_count
    total = in_band * band_count
    ants, samples = voltages.shape[1], voltages.shape[4]
    bins = samples // INTEG

    middle = chan_count // 2
    near = list(range(middle))
    distant = list(range(chan_count - 1, middle, -1))
    masks = distant + near + [middle]
    cut = ants // 2
    first = list(split_channels(voltages, [(middle, 0, cut)], True))
    across = split_channels(voltages, [(m, 0, ants) for m in distant] + [(middle, cut, ants)], True, first[0])
    beside = split_channels(voltages, [(m, 0, ants) for m in near], True, across[0])
    first = [chan_partner(first[0], middle)]
    across = [chan_partner(v, m) for v, m in zip(across, distant + [middle])]
    chunks = [beside[0]] + [chan_partner(v, m) for v, m in zip(beside[1:], near[1:])]
    chunks += first

    lookup = antenna_row_lookup.reshape(1, -1)
    placed, _ = lax.optimization_barrier((positions, beside[0]))
    ours, right, length = our_weights(placed, lookup, gains[:, 0], directions, chan_order, masks, total, in_band)
    held, _ = lax.optimization_barrier((directions, length))
    weights = [ours, their_weights(right, length, partner(held, [("beam", 0)]))]
    partial = early_beams(weights, chunks, ants * len(distant), ants - cut)
    partial = early_beams(weights, across[:-1], 0, 0, partial) if distant else partial

    bits = [("beam", 0)]
    for axis, count in (("chan", chan_count), ("band", band_count)):
        bits += [(axis, bit) for bit in range(count.bit_length() - 1)]
    last = bits[-4:]
    got = [bit for bit in last if bit in (("beam", 0), ("chan", chan_count.bit_length() - 2))]
    got += [bit for bit in last[::-1] if bit not in got][: 2 - len(got)]
    stages = [(pair, pair, []) for pair in (bits[i : i + 2] for i in range(0, len(bits) - 4, 2))]
    stages.append((last, got, [bit for bit in last if bit not in got]))
    maps = tree_maps(delays.reshape(delays.shape[0], total), stages, bins, in_band)
    partial, *maps = lax.optimization_barrier((partial, *maps))

    high, low, other = last_levels(weights, across[-1], partial, total)
    for (_, got, sent), matrix in zip(stages, maps):
        states = [high, low]
        for flips in subsets(got)[1:]:
            states.append(partner(other if ("beam", 0) in flips else high, flips))
        result = tree_stage(matrix, states, bins, directions.shape[1], bool(sent))
        if not sent:
            high, low = result
    received = [partner(value, flips) for value, flips in zip(result[1:], subsets(sent)[1:])]
    return tree_sum(result[0], received).reshape(1, per_dev, bins, directions.shape[1])


def solution(mesh):
    placed = (
        P(None, "chan", "band", None, "group"),
        P(None, "band", "chan", None),
        P(),
        P(None, ("group", "beam")),
        P(),
        P(),
        P(),
    )
    return jax.shard_map(
        shards,
        mesh=mesh,
        in_specs=placed,
        out_specs=P("band", "chan", None, ("group", "beam")),
        check_vma=False,
    )
```

```python
import math

import jax
import jax.numpy as jnp
from jax import lax
from jax.experimental import pallas as pl
from jax.experimental.pallas import tpu as pltpu
from jax.sharding import PartitionSpec as P

INTEG = 8
VMEM = pl.BlockSpec(memory_space=pltpu.VMEM)
SMEM = pl.BlockSpec(memory_space=pltpu.SMEM)
PARAMS = pltpu.CompilerParams(vmem_limit_bytes=40 * 1024 * 1024)
SIN = (6.283184915580925, -41.34158901325128, 81.59993513909575, -76.61436771142901, 41.342343389037076, -12.470285565721209)
COS = (0.9999992089426497, -19.738979914331107, 64.92864094416844, -85.27141067260794, 58.789407905427666, -21.069178520245686)
ROUNDER = 1.5 * 2.0**23
PHASE_ROWS = 32
LONG = pl.CostEstimate(flops=10**10, bytes_accessed=10**8, transcendentals=10**8)
SHORT = pl.CostEstimate(flops=0, bytes_accessed=0, transcendentals=0)


def partner(value, flips):
    axes = tuple(axis for axis in ("chan", "band", "beam") if axis in dict(flips))
    sizes = [lax.axis_size(axis) for axis in axes]
    flip = 0
    for axis, bit in flips:
        flip ^= (1 << bit) * math.prod(sizes[axes.index(axis) + 1 :])
    pairs = [(source, source ^ flip) for source in range(math.prod(sizes))]
    return lax.ppermute(value, axes, pairs)


def chan_partner(value, mask):
    return partner(value, [("chan", bit) for bit in range(mask.bit_length()) if mask >> bit & 1])


def split_channels(voltages, pieces, from_hbm, token=None):
    parts, ants, _, chans, samples = voltages.shape
    per_dev = lax.axis_size("beam")
    start = min(first for _, first, _ in pieces)
    stop = max(last for _, _, last in pieces)
    group = max(16, (stop - start) // 4)
    jobs = [(p, first) for first in range(start, stop, group) for p in range(parts)]
    lanes = range(0, samples, 128)
    tokens = [] if token is None else [token]

    def kernel(v_ref, *refs):
        refs = refs[len(tokens) :]
        outs, wide, (raw, sems) = refs[: len(pieces)], refs[len(pieces) : -2], refs[-2:]
        z = lax.axis_index("chan")
        e = lax.axis_index("beam")

        def rows(number):
            p, first = jobs[number]
            return v_ref.at[p, pl.ds(first * chans, group * chans), :]

        def fetch(number):
            return pltpu.make_async_copy(rows(number), raw.at[number], sems.at[number])

        if from_hbm:
            for number in range(len(jobs)):
                fetch(number).start()
        for number, (p, first) in enumerate(jobs):
            if from_hbm:
                fetch(number).wait()
            block = raw.at[number] if from_hbm else rows(number)
            slot = number % 2
            for lane, half in zip(lanes, wide):
                half[slot] = block[:, pl.ds(lane, 128)].astype(jnp.float32)
            for (mask, piece_first, piece_last), out in zip(pieces, outs):
                if piece_first <= first < piece_last:
                    chan = (z ^ mask) * per_dev + e
                    at = pl.ds(first - piece_first, group)
                    for lane, half in zip(lanes, wide):
                        out[p, at, pl.ds(lane, 128)] = half[slot, pl.ds(chan, group, stride=chans), :].astype(jnp.bfloat16)

    place = pltpu.HBM if from_hbm else pltpu.VMEM
    raw_slots = len(jobs) if from_hbm else 1
    return pl.pallas_call(
        kernel,
        in_specs=[pl.BlockSpec(memory_space=place)] + [pl.BlockSpec(memory_space=pl.ANY)] * len(tokens),
        out_specs=[VMEM] * len(pieces),
        out_shape=[
            jax.ShapeDtypeStruct((parts, last - first, samples), jnp.bfloat16) for _, first, last in pieces
        ],
        scratch_shapes=[pltpu.VMEM((2, group * chans, 128), jnp.float32)] * len(lanes)
        + [
            pltpu.VMEM((raw_slots, group * chans, samples), jnp.bfloat16),
            pltpu.SemaphoreType.DMA((raw_slots,)),
        ],
        compiler_params=PARAMS,
        name="split_channels",
    )(pltpu.with_memory_space_constraint(voltages.reshape(parts, ants * chans, samples), place), *tokens)


def horner(coefs, u):
    total = coefs[-1] * u + coefs[-2]
    for coef in coefs[-3::-1]:
        total = total * u + coef
    return total


def bf16_parts(x):
    first = x.astype(jnp.bfloat16).astype(jnp.float32)
    rest = x - first
    second = rest.astype(jnp.bfloat16).astype(jnp.float32)
    return first, second, rest - second


def xor_blocks(x, index, count):
    size = x.shape[-1] // count
    for bit in range(count.bit_length() - 1):
        swapped = [x[..., (i ^ (1 << bit)) * size : (i ^ (1 << bit)) * size + size] for i in range(count)]
        x = jnp.where((index >> bit) & 1 == 1, jnp.concatenate(swapped, axis=-1), x)
    return x


def phase_rows(dirs):
    parts = jnp.concatenate(bf16_parts(dirs), axis=0)
    rows = [parts, parts, parts, jnp.ones((3, dirs.shape[1]), jnp.float32)]
    rows.append(jnp.zeros((PHASE_ROWS - 30, dirs.shape[1]), jnp.float32))
    return jnp.concatenate(rows, axis=0).astype(jnp.bfloat16)


def fill_weights(left_ref, right_ref, length_ref, turns, out):
    _, beams, ants = out.shape
    block = turns.shape[0]
    lanes = min(ants, 512)

    def block_of_beams(number, carry):
        start = pl.multiple_of(number * block, block)
        turns[...] = lax.dot_general(
            left_ref[:, pl.ds(start, block)],
            right_ref[...],
            (((0,), (0,)), ((), ())),
            preferred_element_type=jnp.float32,
        )

        def rows(step, carry):
            at = pl.ds(pl.multiple_of(step * 16, 16), 16)
            to = pl.ds(pl.multiple_of(start + step * 16, 16), 16)
            for lane in range(0, ants, lanes):
                cols = pl.ds(lane, lanes)
                x = turns[at, cols]
                t = x - ((x + ROUNDER) - ROUNDER)
                u = t * t
                scale = length_ref[:, cols]
                out[0, to, cols] = (horner(COS, u) * scale).astype(jnp.bfloat16)
                out[1, to, cols] = (horner(SIN, u) * (t * scale)).astype(jnp.bfloat16)
            return carry

        return lax.fori_loop(0, block // 16, rows, carry)

    lax.fori_loop(0, beams // block, block_of_beams, 0)


def subsets(bits):
    return [[bit for k, bit in enumerate(bits) if pick >> k & 1] for pick in range(1 << len(bits))]


def map_shapes(stages, per_dev, bins):
    return [(per_dev, bins << len(sent), bins * (1 + (1 << len(got)))) for _, got, sent in stages]


def fill_maps(delay_ref, outs, stages, bins):
    per_dev = lax.axis_size("beam")

    def place(flips):
        at = {axis: lax.axis_index(axis) for axis in ("band", "chan", "beam")}
        for axis, bit in flips:
            at[axis] = at[axis] ^ (1 << bit)
        return at

    def total_delay(bits, first_round, target, source, slot):
        moved = 0
        for k, (axis, bit) in enumerate(bits):
            later = [b for b in bits[k + 1 :] if b in target or b in source]
            end = place(target + later)
            start = place(target + later + [b for b in bits[k : k + 1] if b in target or b in source])
            delay = delay_ref[first_round + k, end["band"], end["chan"] * per_dev + slot]
            moved = moved + ((start[axis] >> bit) & 1) * delay
        return moved

    first_round = 0
    for (bits, got, sent), out in zip(stages, outs):
        sources = [[]] + subsets(got)
        shape = (bins, out.shape[2])
        row = lax.broadcasted_iota(jnp.int32, shape, 0)
        col = lax.broadcasted_iota(jnp.int32, shape, 1)
        for slot in range(per_dev):
            for number, target in enumerate(subsets(sent)):
                shift = jnp.zeros_like(col)
                for place_no, source in enumerate(sources):
                    moved = total_delay(bits, first_round, target, source, slot)
                    shift = jnp.where(col // bins == place_no, moved, shift)
                hit = lax.rem(row - col + len(bits) * bins + shape[1] - shift, bins) == 0
                out[slot, pl.ds(number * bins, bins), :] = jnp.where(hit, 1.0, 0.0).astype(jnp.bfloat16)
        first_round += len(bits)


def our_weights(positions, lookup, gains, dirs, chan_order, delays, masks, stages, bins):
    ants, beams = positions.shape[1], dirs.shape[1]
    per_dev = lax.axis_size("beam")
    size = ants // len(masks)
    lanes = min(ants, 512)
    _, band_count, in_band = delays.shape
    shapes = map_shapes(stages, per_dev, bins)

    def in_order(x, z):
        x = xor_blocks(x, z, len(masks))
        return jnp.concatenate([x[..., m * size : m * size + size] for m in masks], axis=-1)

    def kernel(order_ref, delay_ref, pos_ref, look_ref, gain_ref, dir_ref, out, right_ref, length_ref, copy_ref, *refs):
        maps, (left, turns) = refs[:-2], refs[-2:]
        copy_ref[...] = dir_ref[...]
        z = lax.axis_index("chan")
        e = lax.axis_index("beam")
        slot = lax.axis_index("band") * in_band + z * per_dev + e
        freq = 1.0 + order_ref[slot].astype(jnp.float32) * (1.0 / (band_count * in_band))

        g_re = in_order(jnp.where(e == 0, gain_ref[0, 0:1, :], gain_ref[0, 1:2, :]), z)
        g_im = in_order(jnp.where(e == 0, gain_ref[1, 0:1, :], gain_ref[1, 1:2, :]), z)
        top = jnp.maximum(jnp.abs(g_re), jnp.abs(g_im))
        low = jnp.minimum(jnp.abs(g_re), jnp.abs(g_im))
        ratio = low / jnp.where(top > 0.0, top, 1.0)
        length_ref[...] = top * jnp.sqrt(1.0 + ratio * ratio) * (1.0 / math.sqrt(ants))

        parts = [jnp.concatenate([part] * 3, axis=0) for part in bf16_parts(pos_ref[...] * -freq)]
        parts.append(jnp.zeros((PHASE_ROWS - 27, ants), jnp.float32))
        table = jnp.concatenate(parts, axis=0).astype(jnp.bfloat16)
        look = in_order(look_ref[...], z)
        antenna = lax.broadcasted_iota(jnp.int32, (ants, lanes), 0)
        turn_parts = jnp.concatenate(
            [jnp.zeros((27, ants), jnp.float32)]
            + list(bf16_parts(jnp.arctan2(g_im, g_re) * (0.5 / math.pi)))
            + [jnp.zeros((PHASE_ROWS - 30, ants), jnp.float32)],
            axis=0,
        )
        for lane in range(0, ants, lanes):
            chosen = jnp.where(antenna == look[:, lane : lane + lanes], 1.0, 0.0).astype(jnp.bfloat16)
            rows = jnp.dot(table, chosen, preferred_element_type=jnp.float32)
            right_ref[:, pl.ds(lane, lanes)] = (rows + turn_parts[:, lane : lane + lanes]).astype(jnp.bfloat16)
        left[...] = phase_rows(dir_ref[...])
        fill_weights(left, right_ref, length_ref, turns, out)
        fill_maps(delay_ref, maps, stages, bins)

    return pl.pallas_call(
        kernel,
        in_specs=[SMEM] * 2 + [VMEM] * 4,
        out_specs=[VMEM] * (4 + len(shapes)),
        out_shape=[
            jax.ShapeDtypeStruct((2, beams, ants), jnp.bfloat16),
            jax.ShapeDtypeStruct((PHASE_ROWS, ants), jnp.bfloat16),
            jax.ShapeDtypeStruct((1, ants), jnp.float32),
            jax.ShapeDtypeStruct(dirs.shape, jnp.float32),
        ]
        + [jax.ShapeDtypeStruct(shape, jnp.bfloat16) for shape in shapes],
        scratch_shapes=[
            pltpu.VMEM((PHASE_ROWS, beams), jnp.bfloat16),
            pltpu.VMEM((min(beams, 128), ants), jnp.float32),
        ],
        compiler_params=PARAMS,
        cost_estimate=LONG,
        name="our_weights",
    )(chan_order, delays, positions, lookup, gains, dirs)


def their_weights(right, length, dirs):
    ants, beams = right.shape[1], dirs.shape[1]

    def kernel(right_ref, length_ref, dir_ref, out, left, turns):
        left[...] = phase_rows(dir_ref[...])
        fill_weights(left, right_ref, length_ref, turns, out)

    return pl.pallas_call(
        kernel,
        in_specs=[VMEM] * 3,
        out_specs=VMEM,
        out_shape=jax.ShapeDtypeStruct((2, beams, ants), jnp.bfloat16),
        scratch_shapes=[
            pltpu.VMEM((PHASE_ROWS, beams), jnp.bfloat16),
            pltpu.VMEM((min(beams, 128), ants), jnp.float32),
        ],
        compiler_params=PARAMS,
        cost_estimate=SHORT,
        name="their_weights",
    )(right, length, dirs)


def chunk_product(w_ref, blocks, first, beam_rows):
    re = jnp.concatenate([re for re, _ in blocks], axis=0)
    im = jnp.concatenate([im for _, im in blocks], axis=0)
    straight = jnp.concatenate([re, im], axis=1)
    turned = jnp.concatenate([-im, re], axis=1)
    cols = pl.ds(first, re.shape[0])
    dot = lambda a, b: jnp.dot(a, b, preferred_element_type=jnp.float32)
    return dot(w_ref[0, beam_rows, cols], straight) + dot(w_ref[1, beam_rows, cols], turned)


HIGH_EXTRA, OTHER_EXTRA = 1, (0, 2)
SUM_EXTRA = (1, 0, 2)


def filled(ref, before, after):
    zeros = lambda count: [jnp.zeros((count, ref.shape[2]), ref.dtype)] if count else []
    return [jnp.concatenate(zeros(before) + [ref[p]] + zeros(after), axis=0) for p in range(2)]


def early_beams(weights, chunks, first, rest, partial=None):
    half = weights[0].shape[1]
    samples = chunks[0].shape[2]
    step = min(half, 256)
    before = [] if partial is None else [partial]

    def kernel(ours_ref, theirs_ref, *refs):
        refs, out = refs[:-1], refs[-1]
        blocks = [filled(ref, 0, 0) for ref in refs[len(before) : -1]] + [filled(refs[-1], 0, rest)]
        for number, w_ref in enumerate((ours_ref, theirs_ref)):
            for row in range(0, half, step):
                product = chunk_product(w_ref, blocks, first, pl.ds(row, step))
                at = pl.ds(number * half + row, step)
                out[at, :] = product + refs[0][at, :] if before else product

    return pl.pallas_call(
        kernel,
        in_specs=[VMEM] * (2 + len(before) + len(chunks)),
        out_specs=VMEM,
        out_shape=jax.ShapeDtypeStruct((2 * half, 2 * samples), jnp.float32),
        compiler_params=PARAMS,
        cost_estimate=SHORT,
        name="early_beams",
    )(*weights, *before, *chunks)


def two_parts(x):
    high = x.astype(jnp.bfloat16)
    return high, (x - high.astype(jnp.float32)).astype(jnp.bfloat16)


def message(blocks, width, extra):
    return jax.ShapeDtypeStruct((blocks * width // 128 + 16 * extra, 128), jnp.bfloat16)


def put(ref, first, value):
    bins, width = value.shape
    for lane in range(0, width, 128):
        ref[pl.ds(first, bins), :] = value[:, lane : lane + 128].astype(ref.dtype)
        first += bins
    return first


def take(ref, number, bins, width):
    first = number * bins * width // 128
    pieces = [ref[pl.ds(first + lane // 128 * bins, bins), :] for lane in range(0, width, 128)]
    return jnp.concatenate(pieces, axis=1)


def pad(ref, first):
    if first < ref.shape[0]:
        ref[pl.ds(first, ref.shape[0] - first), :] = jnp.zeros((ref.shape[0] - first, 128), ref.dtype)


def last_levels(weights, chunk, partial, total):
    _, half, ants = weights[0].shape
    samples = chunk.shape[2]
    bins = samples // INTEG
    count = chunk.shape[1]
    first = ants - count

    def kernel(ours_ref, theirs_ref, part_ref, chunk_ref, high_ref, low_ref, *sent_refs):
        re, im = chunk_ref[0], chunk_ref[1]
        antennas = jnp.concatenate(
            [jnp.concatenate([re, im], axis=1), jnp.concatenate([-im, re], axis=1)], axis=0
        )
        bin_no = lax.broadcasted_iota(jnp.int32, (bins, samples), 0)
        time = lax.broadcasted_iota(jnp.int32, (bins, samples), 1)
        centre = jnp.where(time // INTEG == bin_no, 1.0 / INTEG, 0.0) - 1.0 / samples
        centre = jnp.concatenate([centre, centre], axis=1).astype(jnp.bfloat16)
        for number, w_ref in enumerate((ours_ref, theirs_ref)):
            both = jnp.concatenate([w_ref[0, :, pl.ds(first, count)], w_ref[1, :, pl.ds(first, count)]], axis=1)
            beam = part_ref[pl.ds(number * half, half), :] + jnp.dot(both, antennas, preferred_element_type=jnp.float32)
            re, im = beam[:, :samples], beam[:, samples:]
            high, low = two_parts(re * re + im * im)
            parts = jnp.concatenate([high, low], axis=1)
            level = lax.dot_general(centre, parts, (((1,), (1,)), ((), ())), preferred_element_type=jnp.float32)
            high, low = two_parts(level * (1.0 / math.sqrt(total)))
            if number == 0:
                pad(high_ref, put(high_ref, 0, high))
                put(low_ref, 0, low)
            else:
                for sent_ref in sent_refs:
                    pad(sent_ref, put(sent_ref, 0, high))

    return pl.pallas_call(
        kernel,
        in_specs=[VMEM] * 4,
        out_specs=[VMEM] * 4,
        out_shape=[message(bins, half, extra) for extra in (HIGH_EXTRA, 0, *OTHER_EXTRA)],
        compiler_params=PARAMS,
        name="last_levels",
    )(*weights, partial, chunk)


def tree_stage(matrix, states, bins, width, first, final):
    slots, rows, _ = matrix.shape
    targets = rows // bins
    blocks = bins * slots
    if final:
        shapes = [jax.ShapeDtypeStruct((slots, bins, width), jnp.float32)]
        shapes += [message(blocks, width, extra) for extra in SUM_EXTRA[: targets - 1]]
    else:
        shapes = [message(blocks, width, 0)] * 2

    def kernel(map_ref, *refs):
        ins, outs = refs[: len(states)], refs[len(states) :]
        row = 0
        for slot in range(slots):
            column = [take(ref, 0 if first else slot, bins, width) for ref in ins]
            value = jnp.dot(map_ref[slot], jnp.concatenate(column, axis=0), preferred_element_type=jnp.float32)
            if final:
                outs[0][slot] = value[:bins]
                parts = [value[t * bins : t * bins + bins] for t in range(1, targets)]
            else:
                parts = two_parts(value)
            for out, part in zip(outs[-len(parts) :], parts):
                after = put(out, row, part)
            row = after
        for out in outs[-len(parts) :]:
            pad(out, row)

    return pl.pallas_call(
        kernel,
        in_specs=[VMEM] * (1 + len(states)),
        out_specs=[VMEM] * len(shapes),
        out_shape=shapes,
        compiler_params=PARAMS,
        name="tree_stage",
    )(matrix, *states)


def tree_sum(own, received):
    slots, bins, width = own.shape

    def kernel(own_ref, *refs):
        out, total, sems = refs[-3:]
        copies = [pltpu.make_async_copy(total.at[slot], out.at[slot], sems.at[slot]) for slot in range(slots)]
        for slot, copy in enumerate(copies):
            value = own_ref[slot]
            for ref in refs[:-3]:
                value = value + take(ref, slot, bins, width).astype(jnp.float32)
            total[slot] = value
            copy.start()
        for copy in copies:
            copy.wait()

    return pl.pallas_call(
        kernel,
        in_specs=[VMEM] * (1 + len(received)),
        out_specs=pl.BlockSpec(memory_space=pltpu.HBM),
        out_shape=jax.ShapeDtypeStruct(own.shape, jnp.float32),
        scratch_shapes=[pltpu.VMEM(own.shape, jnp.float32), pltpu.SemaphoreType.DMA((slots,))],
        compiler_params=PARAMS,
        name="tree_sum",
    )(own, *received)


def shards(voltages, gains, positions, directions, antenna_row_lookup, chan_order, delays):
    chan_count = lax.axis_size("chan")
    band_count = lax.axis_size("band")
    per_dev = gains.shape[2]
    assert per_dev == lax.axis_size("beam") == 2
    in_band = per_dev * chan_count
    total = in_band * band_count
    ants, samples = voltages.shape[1], voltages.shape[4]
    bins = samples // INTEG

    middle = chan_count // 2
    near = list(range(middle))
    distant = list(range(chan_count - 2, middle - 1, -1))
    middle = chan_count - 1
    masks = distant + near[1:] + [0, middle]
    cut = ants // 2
    first = split_channels(voltages, [(middle, 0, cut)], True)
    across = split_channels(voltages, [(m, 0, ants) for m in distant], True, first[0])
    *beside, rest = split_channels(voltages, [(m, 0, ants) for m in near] + [(middle, cut, ants)], True, across[0])
    first = [chan_partner(first[0], middle)]
    across = [chan_partner(v, m) for v, m in zip(across, distant)]
    rest = chan_partner(rest, middle)
    beside = [beside[0]] + [chan_partner(v, m) for v, m in zip(beside[1:], near[1:])]

    bits = [("beam", 0)]
    for axis, count in (("chan", chan_count), ("band", band_count)):
        bits += [(axis, bit) for bit in range(count.bit_length() - 1)]
    last = bits[-4:]
    got = [bit for bit in last if bit in (("beam", 0), ("chan", chan_count.bit_length() - 2))]
    got += [bit for bit in last[::-1] if bit not in got][: 2 - len(got)]
    stages = [(pair, pair, []) for pair in (bits[:-4][i : i + 2] for i in range(0, len(bits) - 4, 2))]
    stages.append((last, got, [bit for bit in last if bit not in got]))

    lookup = antenna_row_lookup.reshape(1, -1)
    placed, _ = lax.optimization_barrier((positions, beside[0]))
    ours, right, length, dirs, *maps = our_weights(
        placed, lookup, gains[:, 0], directions, chan_order, delays, masks, stages, bins
    )
    weights = [ours, their_weights(right, length, partner(dirs, [("beam", 0)]))]
    partial = early_beams(weights, [beside[0]] + first, ants * (chan_count - 2), ants - cut)
    partial = early_beams(weights, beside[1:], ants * len(distant), 0, partial)
    partial = early_beams(weights, across, 0, 0, partial)

    high, low, *other = last_levels(weights, rest, partial, total)
    for number, ((_, got, sent), matrix) in enumerate(zip(stages, maps)):
        states = [high, low]
        for flips in subsets(got)[1:]:
            states.append(partner(other[len(flips) - 1] if ("beam", 0) in flips else high, flips))
        result = tree_stage(matrix, states, bins, directions.shape[1], number == 0, bool(sent))
        if not sent:
            high, low = result
    received = [partner(value, flips) for value, flips in zip(result[1:], subsets(sent)[1:])]
    return tree_sum(result[0], received).reshape(1, per_dev, bins, directions.shape[1])


def solution(mesh):
    placed = (
        P(None, "chan", "band", None, "group"),
        P(None, "band", "chan", None),
        P(),
        P(None, ("group", "beam")),
        P(),
        P(),
        P(),
    )
    return jax.shard_map(
        shards,
        mesh=mesh,
        in_specs=placed,
        out_specs=P("band", "chan", None, ("group", "beam")),
        check_vma=False,
    )
```

```python
import math

import jax
import jax.numpy as jnp
from jax import lax
from jax.experimental import pallas as pl
from jax.experimental.pallas import tpu as pltpu
from jax.sharding import PartitionSpec as P

INTEG = 8
VMEM = pl.BlockSpec(memory_space=pltpu.VMEM)
SMEM = pl.BlockSpec(memory_space=pltpu.SMEM)
PARAMS = pltpu.CompilerParams(vmem_limit_bytes=40 * 1024 * 1024)
SIN = (6.283184915580925, -41.34158901325128, 81.59993513909575, -76.61436771142901, 41.342343389037076, -12.470285565721209)
COS = (0.9999992089426497, -19.738979914331107, 64.92864094416844, -85.27141067260794, 58.789407905427666, -21.069178520245686)
PHASE_ROWS = 32
LONG = pl.CostEstimate(flops=10**10, bytes_accessed=10**8, transcendentals=10**8)
SHORT = pl.CostEstimate(flops=0, bytes_accessed=0, transcendentals=0)


def partner(value, flips):
    axes = tuple(axis for axis in ("chan", "band", "beam") if axis in dict(flips))
    sizes = [lax.axis_size(axis) for axis in axes]
    flip = 0
    for axis, bit in flips:
        flip ^= (1 << bit) * math.prod(sizes[axes.index(axis) + 1 :])
    pairs = [(source, source ^ flip) for source in range(math.prod(sizes))]
    return lax.ppermute(value, axes, pairs)


def chan_partner(value, mask):
    return partner(value, [("chan", bit) for bit in range(mask.bit_length()) if mask >> bit & 1])


def split_channels(voltages, pieces, from_hbm, token=None):
    parts, ants, _, chans, samples = voltages.shape
    per_dev = lax.axis_size("beam")
    start = min(first for _, first, _ in pieces)
    stop = max(last for _, _, last in pieces)
    group = max(16, (stop - start) // 4)
    jobs = [(p, first) for first in range(start, stop, group) for p in range(parts)]
    lanes = range(0, samples, 128)
    tokens = [] if token is None else [token]

    def kernel(v_ref, *refs):
        refs = refs[len(tokens) :]
        outs, wide, (raw, sems) = refs[: len(pieces)], refs[len(pieces) : -2], refs[-2:]
        z = lax.axis_index("chan")
        e = lax.axis_index("beam")

        def rows(number):
            p, first = jobs[number]
            return v_ref.at[p, pl.ds(first * chans, group * chans), :]

        def fetch(number):
            return pltpu.make_async_copy(rows(number), raw.at[number], sems.at[number])

        if from_hbm:
            for number in range(len(jobs)):
                fetch(number).start()
        for number, (p, first) in enumerate(jobs):
            if from_hbm:
                fetch(number).wait()
            block = raw.at[number] if from_hbm else rows(number)
            slot = number % 2
            for lane, half in zip(lanes, wide):
                half[slot] = block[:, pl.ds(lane, 128)].astype(jnp.float32)
            for (mask, piece_first, piece_last), out in zip(pieces, outs):
                if piece_first <= first < piece_last:
                    chan = (z ^ mask) * per_dev + e
                    at = pl.ds(first - piece_first, group)
                    for lane, half in zip(lanes, wide):
                        out[p, at, pl.ds(lane, 128)] = half[slot, pl.ds(chan, group, stride=chans), :].astype(jnp.bfloat16)

    place = pltpu.HBM if from_hbm else pltpu.VMEM
    raw_slots = len(jobs) if from_hbm else 1
    return pl.pallas_call(
        kernel,
        in_specs=[pl.BlockSpec(memory_space=place)] + [pl.BlockSpec(memory_space=pl.ANY)] * len(tokens),
        out_specs=[VMEM] * len(pieces),
        out_shape=[
            jax.ShapeDtypeStruct((parts, last - first, samples), jnp.bfloat16) for _, first, last in pieces
        ],
        scratch_shapes=[pltpu.VMEM((2, group * chans, 128), jnp.float32)] * len(lanes)
        + [
            pltpu.VMEM((raw_slots, group * chans, samples), jnp.bfloat16),
            pltpu.SemaphoreType.DMA((raw_slots,)),
        ],
        compiler_params=PARAMS,
        name="split_channels",
    )(pltpu.with_memory_space_constraint(voltages.reshape(parts, ants * chans, samples), place), *tokens)


def horner(coefs, u):
    total = coefs[-1] * u + coefs[-2]
    for coef in coefs[-3::-1]:
        total = total * u + coef
    return total


def bf16_parts(x):
    first = x.astype(jnp.bfloat16).astype(jnp.float32)
    rest = x - first
    second = rest.astype(jnp.bfloat16).astype(jnp.float32)
    return first, second, rest - second


def xor_blocks(x, index, count):
    size = x.shape[-1] // count
    for bit in range(count.bit_length() - 1):
        swapped = [x[..., (i ^ (1 << bit)) * size : (i ^ (1 << bit)) * size + size] for i in range(count)]
        x = jnp.where((index >> bit) & 1 == 1, jnp.concatenate(swapped, axis=-1), x)
    return x


def phase_rows(dirs):
    parts = jnp.concatenate(bf16_parts(dirs), axis=0)
    rows = [parts, parts, parts, jnp.ones((3, dirs.shape[1]), jnp.float32)]
    rows.append(jnp.zeros((PHASE_ROWS - 30, dirs.shape[1]), jnp.float32))
    return jnp.concatenate(rows, axis=0).astype(jnp.bfloat16)


def fill_weights(left_ref, right_ref, length_ref, turns, out):
    _, beams, ants = out.shape
    block = turns.shape[0]
    lanes = min(ants, 512)

    def block_of_beams(number, carry):
        start = pl.multiple_of(number * block, block)
        turns[...] = lax.dot_general(
            left_ref[:, pl.ds(start, block)],
            right_ref[...],
            (((0,), (0,)), ((), ())),
            preferred_element_type=jnp.float32,
        )

        def rows(step, carry):
            at = pl.ds(pl.multiple_of(step * 16, 16), 16)
            to = pl.ds(pl.multiple_of(start + step * 16, 16), 16)
            for lane in range(0, ants, lanes):
                cols = pl.ds(lane, lanes)
                x = turns[at, cols]
                t = x - jnp.round(x)
                u = t * t
                scale = length_ref[:, cols]
                out[0, to, cols] = (horner(COS, u) * scale).astype(jnp.bfloat16)
                out[1, to, cols] = (horner(SIN, u) * (t * scale)).astype(jnp.bfloat16)
            return carry

        return lax.fori_loop(0, block // 16, rows, carry)

    lax.fori_loop(0, beams // block, block_of_beams, 0)


def subsets(bits):
    return [[bit for k, bit in enumerate(bits) if pick >> k & 1] for pick in range(1 << len(bits))]


def map_shapes(stages, per_dev, bins):
    return [(per_dev, bins << len(sent), bins * (1 + (1 << len(got)))) for _, got, sent in stages]


def fill_maps(delay_ref, outs, stages, bins):
    per_dev = lax.axis_size("beam")

    def place(flips):
        at = {axis: lax.axis_index(axis) for axis in ("band", "chan", "beam")}
        for axis, bit in flips:
            at[axis] = at[axis] ^ (1 << bit)
        return at

    def total_delay(bits, first_round, target, source, slot):
        moved = 0
        for k, (axis, bit) in enumerate(bits):
            later = [b for b in bits[k + 1 :] if b in target or b in source]
            end = place(target + later)
            start = place(target + later + [b for b in bits[k : k + 1] if b in target or b in source])
            delay = delay_ref[first_round + k, end["band"], end["chan"] * per_dev + slot]
            moved = moved + ((start[axis] >> bit) & 1) * delay
        return moved

    first_round = 0
    for (bits, got, sent), out in zip(stages, outs):
        sources = [[]] + subsets(got)
        shape = (bins, out.shape[2])
        row = lax.broadcasted_iota(jnp.int32, shape, 0)
        col = lax.broadcasted_iota(jnp.int32, shape, 1)
        for slot in range(per_dev):
            for number, target in enumerate(subsets(sent)):
                shift = jnp.zeros_like(col)
                for place_no, source in enumerate(sources):
                    moved = total_delay(bits, first_round, target, source, slot)
                    shift = jnp.where(col // bins == place_no, moved, shift)
                hit = lax.rem(row - col + len(bits) * bins + shape[1] - shift, bins) == 0
                out[slot, pl.ds(number * bins, bins), :] = jnp.where(hit, 1.0, 0.0).astype(jnp.bfloat16)
        first_round += len(bits)


def our_weights(positions, lookup, gains, dirs, chan_order, delays, masks, stages, bins):
    ants, beams = positions.shape[1], dirs.shape[1]
    per_dev = lax.axis_size("beam")
    size = ants // len(masks)
    lanes = min(ants, 512)
    _, band_count, in_band = delays.shape
    shapes = map_shapes(stages, per_dev, bins)

    def in_order(x, z):
        x = xor_blocks(x, z, len(masks))
        return jnp.concatenate([x[..., m * size : m * size + size] for m in masks], axis=-1)

    def kernel(order_ref, delay_ref, pos_ref, look_ref, gain_ref, dir_ref, out, right_ref, length_ref, copy_ref, *refs):
        maps, (left, turns) = refs[:-2], refs[-2:]
        copy_ref[...] = dir_ref[...]
        z = lax.axis_index("chan")
        e = lax.axis_index("beam")
        slot = lax.axis_index("band") * in_band + z * per_dev + e
        freq = 1.0 + order_ref[slot].astype(jnp.float32) * (1.0 / (band_count * in_band))

        g_re = in_order(jnp.where(e == 0, gain_ref[0, 0:1, :], gain_ref[0, 1:2, :]), z)
        g_im = in_order(jnp.where(e == 0, gain_ref[1, 0:1, :], gain_ref[1, 1:2, :]), z)
        top = jnp.maximum(jnp.abs(g_re), jnp.abs(g_im))
        low = jnp.minimum(jnp.abs(g_re), jnp.abs(g_im))
        ratio = low / jnp.where(top > 0.0, top, 1.0)
        length_ref[...] = top * jnp.sqrt(1.0 + ratio * ratio) * (1.0 / math.sqrt(ants))

        parts = [jnp.concatenate([part] * 3, axis=0) for part in bf16_parts(pos_ref[...] * -freq)]
        parts.append(jnp.zeros((PHASE_ROWS - 27, ants), jnp.float32))
        table = jnp.concatenate(parts, axis=0).astype(jnp.bfloat16)
        look = in_order(look_ref[...], z)
        antenna = lax.broadcasted_iota(jnp.int32, (ants, lanes), 0)
        turn_parts = jnp.concatenate(
            [jnp.zeros((27, ants), jnp.float32)]
            + list(bf16_parts(jnp.arctan2(g_im, g_re) * (0.5 / math.pi)))
            + [jnp.zeros((PHASE_ROWS - 30, ants), jnp.float32)],
            axis=0,
        )
        for lane in range(0, ants, lanes):
            chosen = jnp.where(antenna == look[:, lane : lane + lanes], 1.0, 0.0).astype(jnp.bfloat16)
            rows = jnp.dot(table, chosen, preferred_element_type=jnp.float32)
            right_ref[:, pl.ds(lane, lanes)] = (rows + turn_parts[:, lane : lane + lanes]).astype(jnp.bfloat16)
        left[...] = phase_rows(dir_ref[...])
        fill_weights(left, right_ref, length_ref, turns, out)
        fill_maps(delay_ref, maps, stages, bins)

    return pl.pallas_call(
        kernel,
        in_specs=[SMEM] * 2 + [VMEM] * 4,
        out_specs=[VMEM] * (4 + len(shapes)),
        out_shape=[
            jax.ShapeDtypeStruct((2, beams, ants), jnp.bfloat16),
            jax.ShapeDtypeStruct((PHASE_ROWS, ants), jnp.bfloat16),
            jax.ShapeDtypeStruct((1, ants), jnp.float32),
            jax.ShapeDtypeStruct(dirs.shape, jnp.float32),
        ]
        + [jax.ShapeDtypeStruct(shape, jnp.bfloat16) for shape in shapes],
        scratch_shapes=[
            pltpu.VMEM((PHASE_ROWS, beams), jnp.bfloat16),
            pltpu.VMEM((min(beams, 128), ants), jnp.float32),
        ],
        compiler_params=PARAMS,
        cost_estimate=LONG,
        name="our_weights",
    )(chan_order, delays, positions, lookup, gains, dirs)


def their_weights(right, length, dirs):
    ants, beams = right.shape[1], dirs.shape[1]

    def kernel(right_ref, length_ref, dir_ref, out, left, turns):
        left[...] = phase_rows(dir_ref[...])
        fill_weights(left, right_ref, length_ref, turns, out)

    return pl.pallas_call(
        kernel,
        in_specs=[VMEM] * 3,
        out_specs=VMEM,
        out_shape=jax.ShapeDtypeStruct((2, beams, ants), jnp.bfloat16),
        scratch_shapes=[
            pltpu.VMEM((PHASE_ROWS, beams), jnp.bfloat16),
            pltpu.VMEM((min(beams, 128), ants), jnp.float32),
        ],
        compiler_params=PARAMS,
        cost_estimate=SHORT,
        name="their_weights",
    )(right, length, dirs)


def chunk_product(w_ref, blocks, first, beam_rows):
    re = jnp.concatenate([re for re, _ in blocks], axis=0)
    im = jnp.concatenate([im for _, im in blocks], axis=0)
    straight = jnp.concatenate([re, im], axis=1)
    turned = jnp.concatenate([-im, re], axis=1)
    cols = pl.ds(first, re.shape[0])
    dot = lambda a, b: jnp.dot(a, b, preferred_element_type=jnp.float32)
    return dot(w_ref[0, beam_rows, cols], straight) + dot(w_ref[1, beam_rows, cols], turned)


HIGH_EXTRA, OTHER_EXTRA = 1, (0, 2)
SUM_EXTRA = (1, 0, 2)


def filled(ref, before, after):
    zeros = lambda count: [jnp.zeros((count, ref.shape[2]), ref.dtype)] if count else []
    return [jnp.concatenate(zeros(before) + [ref[p]] + zeros(after), axis=0) for p in range(2)]


def early_beams(weights, chunks, first, rest, partial=None):
    half = weights[0].shape[1]
    samples = chunks[0].shape[2]
    step = min(half, 256)
    before = [] if partial is None else [partial]

    def kernel(ours_ref, theirs_ref, *refs):
        refs, out = refs[:-1], refs[-1]
        blocks = [filled(ref, 0, 0) for ref in refs[len(before) : -1]] + [filled(refs[-1], 0, rest)]
        for number, w_ref in enumerate((ours_ref, theirs_ref)):
            for row in range(0, half, step):
                product = chunk_product(w_ref, blocks, first, pl.ds(row, step))
                at = pl.ds(number * half + row, step)
                out[at, :] = product + refs[0][at, :] if before else product

    return pl.pallas_call(
        kernel,
        in_specs=[VMEM] * (2 + len(before) + len(chunks)),
        out_specs=VMEM,
        out_shape=jax.ShapeDtypeStruct((2 * half, 2 * samples), jnp.float32),
        compiler_params=PARAMS,
        cost_estimate=SHORT,
        name="early_beams",
    )(*weights, *before, *chunks)


def two_parts(x):
    high = x.astype(jnp.bfloat16)
    return high, (x - high.astype(jnp.float32)).astype(jnp.bfloat16)


def message(blocks, width, extra):
    return jax.ShapeDtypeStruct((blocks * width // 128 + 16 * extra, 128), jnp.bfloat16)


def put(ref, first, value):
    bins, width = value.shape
    for lane in range(0, width, 128):
        ref[pl.ds(first, bins), :] = value[:, lane : lane + 128].astype(ref.dtype)
        first += bins
    return first


def take(ref, number, bins, width):
    first = number * bins * width // 128
    pieces = [ref[pl.ds(first + lane // 128 * bins, bins), :] for lane in range(0, width, 128)]
    return jnp.concatenate(pieces, axis=1)


def pad(ref, first):
    if first < ref.shape[0]:
        ref[pl.ds(first, ref.shape[0] - first), :] = jnp.zeros((ref.shape[0] - first, 128), ref.dtype)


def last_levels(weights, chunk, partial, total):
    _, half, ants = weights[0].shape
    samples = chunk.shape[2]
    bins = samples // INTEG
    count = chunk.shape[1]
    first = ants - count

    def kernel(ours_ref, theirs_ref, part_ref, chunk_ref, high_ref, low_ref, *sent_refs):
        re, im = chunk_ref[0], chunk_ref[1]
        antennas = jnp.concatenate(
            [jnp.concatenate([re, im], axis=1), jnp.concatenate([-im, re], axis=1)], axis=0
        )
        bin_no = lax.broadcasted_iota(jnp.int32, (bins, samples), 0)
        time = lax.broadcasted_iota(jnp.int32, (bins, samples), 1)
        centre = jnp.where(time // INTEG == bin_no, 1.0 / INTEG, 0.0) - 1.0 / samples
        centre = jnp.concatenate([centre, centre], axis=1).astype(jnp.bfloat16)
        beams = []
        for number, w_ref in enumerate((ours_ref, theirs_ref)):
            both = jnp.concatenate([w_ref[0, :, pl.ds(first, count)], w_ref[1, :, pl.ds(first, count)]], axis=1)
            product = jnp.dot(both, antennas, preferred_element_type=jnp.float32)
            beams.append(part_ref[pl.ds(number * half, half), :] + product)
        for number, beam in enumerate(beams):
            re, im = beam[:, :samples], beam[:, samples:]
            parts = jnp.concatenate(two_parts(re * re + im * im), axis=1)
            level = lax.dot_general(centre, parts, (((1,), (1,)), ((), ())), preferred_element_type=jnp.float32)
            high, low = two_parts(level * (1.0 / math.sqrt(total)))
            if number == 0:
                pad(high_ref, put(high_ref, 0, high))
                put(low_ref, 0, low)
            else:
                for sent_ref in sent_refs:
                    pad(sent_ref, put(sent_ref, 0, high))

    return pl.pallas_call(
        kernel,
        in_specs=[VMEM] * 4,
        out_specs=[VMEM] * 4,
        out_shape=[message(bins, half, extra) for extra in (HIGH_EXTRA, 0, *OTHER_EXTRA)],
        compiler_params=PARAMS,
        name="last_levels",
    )(*weights, partial, chunk)


def tree_stage(matrix, states, bins, width, first, final):
    slots, rows, _ = matrix.shape
    targets = rows // bins
    blocks = bins * slots
    if final:
        shapes = [jax.ShapeDtypeStruct((slots, bins, width), jnp.float32)]
        shapes += [message(blocks, width, extra) for extra in SUM_EXTRA[: targets - 1]]
    else:
        shapes = [message(blocks, width, 0)] * 2

    def kernel(map_ref, *refs):
        ins, outs = refs[: len(states)], refs[len(states) :]
        row = 0
        for slot in range(slots):
            column = [take(ref, 0 if first else slot, bins, width) for ref in ins]
            value = jnp.dot(map_ref[slot], jnp.concatenate(column, axis=0), preferred_element_type=jnp.float32)
            if final:
                outs[0][slot] = value[:bins]
                parts = [value[t * bins : t * bins + bins] for t in range(1, targets)]
            else:
                parts = two_parts(value)
            for out, part in zip(outs[-len(parts) :], parts):
                after = put(out, row, part)
            row = after
        for out in outs[-len(parts) :]:
            pad(out, row)

    return pl.pallas_call(
        kernel,
        in_specs=[VMEM] * (1 + len(states)),
        out_specs=[VMEM] * len(shapes),
        out_shape=shapes,
        compiler_params=PARAMS,
        name="tree_stage",
    )(matrix, *states)


def tree_sum(own, received):
    slots, bins, width = own.shape

    def kernel(own_ref, *refs):
        out, total, sems = refs[-3:]
        copies = [pltpu.make_async_copy(total.at[slot], out.at[slot], sems.at[slot]) for slot in range(slots)]
        for slot, copy in enumerate(copies):
            value = own_ref[slot]
            for ref in refs[:-3]:
                value = value + take(ref, slot, bins, width).astype(jnp.float32)
            total[slot] = value
            copy.start()
        for copy in copies:
            copy.wait()

    return pl.pallas_call(
        kernel,
        in_specs=[VMEM] * (1 + len(received)),
        out_specs=pl.BlockSpec(memory_space=pltpu.HBM),
        out_shape=jax.ShapeDtypeStruct(own.shape, jnp.float32),
        scratch_shapes=[pltpu.VMEM(own.shape, jnp.float32), pltpu.SemaphoreType.DMA((slots,))],
        compiler_params=PARAMS,
        name="tree_sum",
    )(own, *received)


def shards(voltages, gains, positions, directions, antenna_row_lookup, chan_order, delays):
    chan_count = lax.axis_size("chan")
    band_count = lax.axis_size("band")
    per_dev = gains.shape[2]
    assert per_dev == lax.axis_size("beam") == 2
    in_band = per_dev * chan_count
    total = in_band * band_count
    ants, samples = voltages.shape[1], voltages.shape[4]
    bins = samples // INTEG

    middle = chan_count // 2
    near = list(range(middle))
    distant = list(range(chan_count - 2, middle - 1, -1))
    middle = chan_count - 1
    masks = distant + near[1:] + [0, middle]
    cut = ants // 2
    first = split_channels(voltages, [(middle, 0, cut)], True)
    across = split_channels(voltages, [(m, 0, ants) for m in distant], True, first[0])
    *beside, rest = split_channels(voltages, [(m, 0, ants) for m in near] + [(middle, cut, ants)], True, across[0])
    first = [chan_partner(first[0], middle)]
    across = [chan_partner(v, m) for v, m in zip(across, distant)]
    rest = chan_partner(rest, middle)
    beside = [beside[0]] + [chan_partner(v, m) for v, m in zip(beside[1:], near[1:])]

    bits = [("beam", 0)]
    for axis, count in (("chan", chan_count), ("band", band_count)):
        bits += [(axis, bit) for bit in range(count.bit_length() - 1)]
    last = bits[-4:]
    got = [bit for bit in last if bit in (("beam", 0), ("chan", chan_count.bit_length() - 2))]
    got += [bit for bit in last[::-1] if bit not in got][: 2 - len(got)]
    stages = [(pair, pair, []) for pair in (bits[:-4][i : i + 2] for i in range(0, len(bits) - 4, 2))]
    stages.append((last, got, [bit for bit in last if bit not in got]))

    lookup = antenna_row_lookup.reshape(1, -1)
    placed, _ = lax.optimization_barrier((positions, beside[0]))
    ours, right, length, dirs, *maps = our_weights(
        placed, lookup, gains[:, 0], directions, chan_order, delays, masks, stages, bins
    )
    weights = [ours, their_weights(right, length, partner(dirs, [("beam", 0)]))]
    partial = early_beams(weights, [beside[0]] + first, ants * (chan_count - 2), ants - cut)
    partial = early_beams(weights, across + beside[1:], 0, 0, partial)

    high, low, *other = last_levels(weights, rest, partial, total)
    for number, ((_, got, sent), matrix) in enumerate(zip(stages, maps)):
        states = [high, low]
        for flips in subsets(got)[1:]:
            states.append(partner(other[len(flips) - 1] if ("beam", 0) in flips else high, flips))
        result = tree_stage(matrix, states, bins, directions.shape[1], number == 0, bool(sent))
        if not sent:
            high, low = result
    received = [partner(value, flips) for value, flips in zip(result[1:], subsets(sent)[1:])]
    return tree_sum(result[0], received).reshape(1, per_dev, bins, directions.shape[1])


def solution(mesh):
    placed = (
        P(None, "chan", "band", None, "group"),
        P(None, "band", "chan", None),
        P(),
        P(None, ("group", "beam")),
        P(),
        P(),
        P(),
    )
    return jax.shard_map(
        shards,
        mesh=mesh,
        in_specs=placed,
        out_specs=P("band", "chan", None, ("group", "beam")),
        check_vma=False,
    )
```

```python
import math

import jax
import jax.numpy as jnp
from jax import lax
from jax.experimental import pallas as pl
from jax.experimental.pallas import tpu as pltpu
from jax.sharding import PartitionSpec as P

INTEG = 8
VMEM = pl.BlockSpec(memory_space=pltpu.VMEM)
SMEM = pl.BlockSpec(memory_space=pltpu.SMEM)
PARAMS = pltpu.CompilerParams(vmem_limit_bytes=40 * 1024 * 1024)
SIN = (6.283184915580925, -41.34158901325128, 81.59993513909575, -76.61436771142901, 41.342343389037076, -12.470285565721209)
COS = (0.9999992089426497, -19.738979914331107, 64.92864094416844, -85.27141067260794, 58.789407905427666, -21.069178520245686)
PHASE_ROWS = 32
LONG = pl.CostEstimate(flops=10**10, bytes_accessed=10**8, transcendentals=10**8)
SHORT = pl.CostEstimate(flops=0, bytes_accessed=0, transcendentals=0)


def partner(value, flips):
    axes = tuple(axis for axis in ("chan", "band", "beam") if axis in dict(flips))
    sizes = [lax.axis_size(axis) for axis in axes]
    flip = 0
    for axis, bit in flips:
        flip ^= (1 << bit) * math.prod(sizes[axes.index(axis) + 1 :])
    pairs = [(source, source ^ flip) for source in range(math.prod(sizes))]
    return lax.ppermute(value, axes, pairs)


def chan_partner(value, mask):
    return partner(value, [("chan", bit) for bit in range(mask.bit_length()) if mask >> bit & 1])


def split_channels(voltages, pieces, from_hbm, token=None):
    parts, ants, _, chans, samples = voltages.shape
    per_dev = lax.axis_size("beam")
    start = min(first for _, first, _ in pieces)
    stop = max(last for _, _, last in pieces)
    group = max(16, (stop - start) // 4)
    jobs = [(p, first) for first in range(start, stop, group) for p in range(parts)]
    lanes = range(0, samples, 128)
    tokens = [] if token is None else [token]

    def kernel(v_ref, *refs):
        refs = refs[len(tokens) :]
        outs, wide, (raw, sems) = refs[: len(pieces)], refs[len(pieces) : -2], refs[-2:]
        z = lax.axis_index("chan")
        e = lax.axis_index("beam")

        def rows(number):
            p, first = jobs[number]
            return v_ref.at[p, pl.ds(first * chans, group * chans), :]

        def fetch(number):
            return pltpu.make_async_copy(rows(number), raw.at[number], sems.at[number])

        if from_hbm:
            for number in range(len(jobs)):
                fetch(number).start()
        for number, (p, first) in enumerate(jobs):
            if from_hbm:
                fetch(number).wait()
            block = raw.at[number] if from_hbm else rows(number)
            slot = number % 2
            for lane, half in zip(lanes, wide):
                half[slot, pl.ds(0, group * chans), :] = block[:, pl.ds(lane, 128)].astype(jnp.float32)
            for (mask, piece_first, piece_last), out in zip(pieces, outs):
                if piece_first <= first < piece_last:
                    chan = (z ^ mask) * per_dev + e
                    at = pl.ds(first - piece_first, group)
                    for lane, half in zip(lanes, wide):
                        out[p, at, pl.ds(lane, 128)] = half[slot, pl.ds(chan, group, stride=chans), :].astype(jnp.bfloat16)

    place = pltpu.HBM if from_hbm else pltpu.VMEM
    raw_slots = len(jobs) if from_hbm else 1
    return pl.pallas_call(
        kernel,
        in_specs=[pl.BlockSpec(memory_space=place)] + [pl.BlockSpec(memory_space=pl.ANY)] * len(tokens),
        out_specs=[VMEM] * len(pieces),
        out_shape=[
            jax.ShapeDtypeStruct((parts, last - first, samples), jnp.bfloat16) for _, first, last in pieces
        ],
        scratch_shapes=[pltpu.VMEM((2, (group + 1) * chans, 128), jnp.float32)] * len(lanes)
        + [
            pltpu.VMEM((raw_slots, group * chans, samples), jnp.bfloat16),
            pltpu.SemaphoreType.DMA((raw_slots,)),
        ],
        compiler_params=PARAMS,
        name="split_channels",
    )(pltpu.with_memory_space_constraint(voltages.reshape(parts, ants * chans, samples), place), *tokens)


def horner(coefs, u):
    total = coefs[-1] * u + coefs[-2]
    for coef in coefs[-3::-1]:
        total = total * u + coef
    return total


def bf16_parts(x):
    first = x.astype(jnp.bfloat16).astype(jnp.float32)
    rest = x - first
    second = rest.astype(jnp.bfloat16).astype(jnp.float32)
    return first, second, rest - second


def xor_blocks(x, index, count):
    size = x.shape[-1] // count
    for bit in range(count.bit_length() - 1):
        swapped = [x[..., (i ^ (1 << bit)) * size : (i ^ (1 << bit)) * size + size] for i in range(count)]
        x = jnp.where((index >> bit) & 1 == 1, jnp.concatenate(swapped, axis=-1), x)
    return x


def phase_rows(dirs):
    parts = jnp.concatenate(bf16_parts(dirs), axis=0)
    rows = [parts, parts, parts, jnp.ones((3, dirs.shape[1]), jnp.float32)]
    rows.append(jnp.zeros((PHASE_ROWS - 30, dirs.shape[1]), jnp.float32))
    return jnp.concatenate(rows, axis=0).astype(jnp.bfloat16)


def fill_weights(left_ref, right_ref, length_ref, turns, out):
    _, beams, ants = out.shape
    block = turns.shape[0]
    lanes = min(ants, 512)

    def block_of_beams(number, carry):
        start = pl.multiple_of(number * block, block)
        turns[...] = lax.dot_general(
            left_ref[:, pl.ds(start, block)],
            right_ref[...],
            (((0,), (0,)), ((), ())),
            preferred_element_type=jnp.float32,
        )

        def rows(step, carry):
            at = pl.ds(pl.multiple_of(step * 16, 16), 16)
            to = pl.ds(pl.multiple_of(start + step * 16, 16), 16)
            for lane in range(0, ants, lanes):
                cols = pl.ds(lane, lanes)
                x = turns[at, cols]
                t = x - jnp.round(x)
                u = t * t
                scale = length_ref[:, cols]
                out[0, to, cols] = (horner(COS, u) * scale).astype(jnp.bfloat16)
                out[1, to, cols] = (horner(SIN, u) * (t * scale)).astype(jnp.bfloat16)
            return carry

        return lax.fori_loop(0, block // 16, rows, carry)

    lax.fori_loop(0, beams // block, block_of_beams, 0)


def subsets(bits):
    return [[bit for k, bit in enumerate(bits) if pick >> k & 1] for pick in range(1 << len(bits))]


def map_shapes(stages, per_dev, bins):
    return [(per_dev, bins << len(sent), bins * (1 + (1 << len(got)))) for _, got, sent in stages]


def fill_maps(delay_ref, outs, stages, bins):
    per_dev = lax.axis_size("beam")

    def place(flips):
        at = {axis: lax.axis_index(axis) for axis in ("band", "chan", "beam")}
        for axis, bit in flips:
            at[axis] = at[axis] ^ (1 << bit)
        return at

    def total_delay(bits, first_round, target, source, slot):
        moved = 0
        for k, (axis, bit) in enumerate(bits):
            later = [b for b in bits[k + 1 :] if b in target or b in source]
            end = place(target + later)
            start = place(target + later + [b for b in bits[k : k + 1] if b in target or b in source])
            delay = delay_ref[first_round + k, end["band"], end["chan"] * per_dev + slot]
            moved = moved + ((start[axis] >> bit) & 1) * delay
        return moved

    first_round = 0
    for (bits, got, sent), out in zip(stages, outs):
        sources = [[]] + subsets(got)
        shape = (bins, out.shape[2])
        row = lax.broadcasted_iota(jnp.int32, shape, 0)
        col = lax.broadcasted_iota(jnp.int32, shape, 1)
        for slot in range(per_dev):
            for number, target in enumerate(subsets(sent)):
                shift = jnp.zeros_like(col)
                for place_no, source in enumerate(sources):
                    moved = total_delay(bits, first_round, target, source, slot)
                    shift = jnp.where(col // bins == place_no, moved, shift)
                hit = lax.rem(row - col + len(bits) * bins + shape[1] - shift, bins) == 0
                out[slot, pl.ds(number * bins, bins), :] = jnp.where(hit, 1.0, 0.0).astype(jnp.bfloat16)
        first_round += len(bits)


def our_weights(positions, lookup, gains, dirs, chan_order, delays, masks, stages, bins):
    ants, beams = positions.shape[1], dirs.shape[1]
    per_dev = lax.axis_size("beam")
    size = ants // len(masks)
    lanes = min(ants, 512)
    _, band_count, in_band = delays.shape
    shapes = map_shapes(stages, per_dev, bins)

    def in_order(x, z):
        x = xor_blocks(x, z, len(masks))
        return jnp.concatenate([x[..., m * size : m * size + size] for m in masks], axis=-1)

    def kernel(order_ref, delay_ref, pos_ref, look_ref, gain_ref, dir_ref, out, right_ref, length_ref, copy_ref, *refs):
        maps, (left, turns) = refs[:-2], refs[-2:]
        copy_ref[...] = dir_ref[...]
        z = lax.axis_index("chan")
        e = lax.axis_index("beam")
        slot = lax.axis_index("band") * in_band + z * per_dev + e
        freq = 1.0 + order_ref[slot].astype(jnp.float32) * (1.0 / (band_count * in_band))

        g_re = in_order(jnp.where(e == 0, gain_ref[0, 0:1, :], gain_ref[0, 1:2, :]), z)
        g_im = in_order(jnp.where(e == 0, gain_ref[1, 0:1, :], gain_ref[1, 1:2, :]), z)
        top = jnp.maximum(jnp.abs(g_re), jnp.abs(g_im))
        low = jnp.minimum(jnp.abs(g_re), jnp.abs(g_im))
        ratio = low / jnp.where(top > 0.0, top, 1.0)
        length_ref[...] = top * jnp.sqrt(1.0 + ratio * ratio) * (1.0 / math.sqrt(ants))

        parts = [jnp.concatenate([part] * 3, axis=0) for part in bf16_parts(pos_ref[...] * -freq)]
        parts.append(jnp.zeros((PHASE_ROWS - 27, ants), jnp.float32))
        table = jnp.concatenate(parts, axis=0).astype(jnp.bfloat16)
        look = in_order(look_ref[...], z)
        antenna = lax.broadcasted_iota(jnp.int32, (ants, lanes), 0)
        turn_parts = jnp.concatenate(
            [jnp.zeros((27, ants), jnp.float32)]
            + list(bf16_parts(jnp.arctan2(g_im, g_re) * (0.5 / math.pi)))
            + [jnp.zeros((PHASE_ROWS - 30, ants), jnp.float32)],
            axis=0,
        )
        for lane in range(0, ants, lanes):
            chosen = jnp.where(antenna == look[:, lane : lane + lanes], 1.0, 0.0).astype(jnp.bfloat16)
            rows = jnp.dot(table, chosen, preferred_element_type=jnp.float32)
            right_ref[:, pl.ds(lane, lanes)] = (rows + turn_parts[:, lane : lane + lanes]).astype(jnp.bfloat16)
        left[...] = phase_rows(dir_ref[...])
        fill_weights(left, right_ref, length_ref, turns, out)
        fill_maps(delay_ref, maps, stages, bins)

    return pl.pallas_call(
        kernel,
        in_specs=[SMEM] * 2 + [VMEM] * 4,
        out_specs=[VMEM] * (4 + len(shapes)),
        out_shape=[
            jax.ShapeDtypeStruct((2, beams, ants), jnp.bfloat16),
            jax.ShapeDtypeStruct((PHASE_ROWS, ants), jnp.bfloat16),
            jax.ShapeDtypeStruct((1, ants), jnp.float32),
            jax.ShapeDtypeStruct(dirs.shape, jnp.float32),
        ]
        + [jax.ShapeDtypeStruct(shape, jnp.bfloat16) for shape in shapes],
        scratch_shapes=[
            pltpu.VMEM((PHASE_ROWS, beams), jnp.bfloat16),
            pltpu.VMEM((min(beams, 128), ants), jnp.float32),
        ],
        compiler_params=PARAMS,
        cost_estimate=LONG,
        name="our_weights",
    )(chan_order, delays, positions, lookup, gains, dirs)


def their_weights(right, length, dirs):
    ants, beams = right.shape[1], dirs.shape[1]

    def kernel(right_ref, length_ref, dir_ref, out, left, turns):
        left[...] = phase_rows(dir_ref[...])
        fill_weights(left, right_ref, length_ref, turns, out)

    return pl.pallas_call(
        kernel,
        in_specs=[VMEM] * 3,
        out_specs=VMEM,
        out_shape=jax.ShapeDtypeStruct((2, beams, ants), jnp.bfloat16),
        scratch_shapes=[
            pltpu.VMEM((PHASE_ROWS, beams), jnp.bfloat16),
            pltpu.VMEM((min(beams, 128), ants), jnp.float32),
        ],
        compiler_params=PARAMS,
        cost_estimate=SHORT,
        name="their_weights",
    )(right, length, dirs)


def chunk_product(w_ref, blocks, first, beam_rows):
    re = jnp.concatenate([re for re, _ in blocks], axis=0)
    im = jnp.concatenate([im for _, im in blocks], axis=0)
    straight = jnp.concatenate([re, im], axis=1)
    turned = jnp.concatenate([-im, re], axis=1)
    cols = pl.ds(first, re.shape[0])
    dot = lambda a, b: jnp.dot(a, b, preferred_element_type=jnp.float32)
    return dot(w_ref[0, beam_rows, cols], straight) + dot(w_ref[1, beam_rows, cols], turned)


HIGH_EXTRA, OTHER_EXTRA = 1, (0, 2)
SUM_EXTRA = (1, 0, 2)


def filled(ref, before, after):
    zeros = lambda count: [jnp.zeros((count, ref.shape[2]), ref.dtype)] if count else []
    return [jnp.concatenate(zeros(before) + [ref[p]] + zeros(after), axis=0) for p in range(2)]


def early_beams(weights, chunks, first, rest, partial=None):
    half = weights[0].shape[1]
    samples = chunks[0].shape[2]
    step = min(half, 256)
    before = [] if partial is None else [partial]

    def kernel(ours_ref, theirs_ref, *refs):
        refs, out = refs[:-1], refs[-1]
        blocks = [filled(ref, 0, 0) for ref in refs[len(before) : -1]] + [filled(refs[-1], 0, rest)]
        for number, w_ref in enumerate((ours_ref, theirs_ref)):
            for row in range(0, half, step):
                product = chunk_product(w_ref, blocks, first, pl.ds(row, step))
                at = pl.ds(number * half + row, step)
                out[at, :] = product + refs[0][at, :] if before else product

    return pl.pallas_call(
        kernel,
        in_specs=[VMEM] * (2 + len(before) + len(chunks)),
        out_specs=VMEM,
        out_shape=jax.ShapeDtypeStruct((2 * half, 2 * samples), jnp.float32),
        compiler_params=PARAMS,
        cost_estimate=SHORT,
        name="early_beams",
    )(*weights, *before, *chunks)


def two_parts(x):
    high = x.astype(jnp.bfloat16)
    return high, (x - high.astype(jnp.float32)).astype(jnp.bfloat16)


def message(blocks, width, extra):
    return jax.ShapeDtypeStruct((blocks * width // 128 + 16 * extra, 128), jnp.bfloat16)


def put(ref, first, value):
    bins, width = value.shape
    for lane in range(0, width, 128):
        ref[pl.ds(first, bins), :] = value[:, lane : lane + 128].astype(ref.dtype)
        first += bins
    return first


def take(ref, number, bins, width):
    first = number * bins * width // 128
    pieces = [ref[pl.ds(first + lane // 128 * bins, bins), :] for lane in range(0, width, 128)]
    return jnp.concatenate(pieces, axis=1)


def pad(ref, first):
    if first < ref.shape[0]:
        ref[pl.ds(first, ref.shape[0] - first), :] = jnp.zeros((ref.shape[0] - first, 128), ref.dtype)


def last_levels(weights, chunk, partial, total):
    _, half, ants = weights[0].shape
    samples = chunk.shape[2]
    bins = samples // INTEG
    count = chunk.shape[1]
    first = ants - count

    def kernel(ours_ref, theirs_ref, part_ref, chunk_ref, high_ref, low_ref, *sent_refs):
        re, im = chunk_ref[0], chunk_ref[1]
        antennas = jnp.concatenate(
            [jnp.concatenate([re, im], axis=1), jnp.concatenate([-im, re], axis=1)], axis=0
        )
        bin_no = lax.broadcasted_iota(jnp.int32, (bins, samples), 0)
        time = lax.broadcasted_iota(jnp.int32, (bins, samples), 1)
        centre = jnp.where(time // INTEG == bin_no, 1.0 / INTEG, 0.0) - 1.0 / samples
        centre = jnp.concatenate([centre, centre], axis=1).astype(jnp.bfloat16)
        beams = []
        for number, w_ref in enumerate((ours_ref, theirs_ref)):
            both = jnp.concatenate([w_ref[0, :, pl.ds(first, count)], w_ref[1, :, pl.ds(first, count)]], axis=1)
            product = jnp.dot(both, antennas, preferred_element_type=jnp.float32)
            beams.append(part_ref[pl.ds(number * half, half), :] + product)
        for number, beam in enumerate(beams):
            re, im = beam[:, :samples], beam[:, samples:]
            parts = jnp.concatenate(two_parts(re * re + im * im), axis=1)
            level = lax.dot_general(centre, parts, (((1,), (1,)), ((), ())), preferred_element_type=jnp.float32)
            high, low = two_parts(level * (1.0 / math.sqrt(total)))
            if number == 0:
                pad(high_ref, put(high_ref, 0, high))
                put(low_ref, 0, low)
            else:
                for sent_ref in sent_refs:
                    pad(sent_ref, put(sent_ref, 0, high))

    return pl.pallas_call(
        kernel,
        in_specs=[VMEM] * 4,
        out_specs=[VMEM] * 4,
        out_shape=[message(bins, half, extra) for extra in (HIGH_EXTRA, 0, *OTHER_EXTRA)],
        compiler_params=PARAMS,
        name="last_levels",
    )(*weights, partial, chunk)


def tree_stage(matrix, states, bins, width, first, final):
    slots, rows, _ = matrix.shape
    targets = rows // bins
    blocks = bins * slots
    if final:
        shapes = [jax.ShapeDtypeStruct((slots, bins, width), jnp.float32)]
        shapes += [message(blocks, width, extra) for extra in SUM_EXTRA[: targets - 1]]
    else:
        shapes = [message(blocks, width, 0)] * 2

    def kernel(map_ref, *refs):
        ins, outs = refs[: len(states)], refs[len(states) :]
        row = 0
        for slot in range(slots):
            column = [take(ref, 0 if first else slot, bins, width) for ref in ins]
            value = jnp.dot(map_ref[slot], jnp.concatenate(column, axis=0), preferred_element_type=jnp.float32)
            if final:
                outs[0][slot] = value[:bins]
                parts = [value[t * bins : t * bins + bins] for t in range(1, targets)]
            else:
                parts = two_parts(value)
            for out, part in zip(outs[-len(parts) :], parts):
                after = put(out, row, part)
            row = after
        for out in outs[-len(parts) :]:
            pad(out, row)

    return pl.pallas_call(
        kernel,
        in_specs=[VMEM] * (1 + len(states)),
        out_specs=[VMEM] * len(shapes),
        out_shape=shapes,
        compiler_params=PARAMS,
        name="tree_stage",
    )(matrix, *states)


def tree_sum(own, received):
    slots, bins, width = own.shape

    def kernel(own_ref, *refs):
        out, total, sems = refs[-3:]
        copies = [pltpu.make_async_copy(total.at[slot], out.at[slot], sems.at[slot]) for slot in range(slots)]
        for slot, copy in enumerate(copies):
            value = own_ref[slot]
            for ref in refs[:-3]:
                value = value + take(ref, slot, bins, width).astype(jnp.float32)
            total[slot] = value
            copy.start()
        for copy in copies:
            copy.wait()

    return pl.pallas_call(
        kernel,
        in_specs=[VMEM] * (1 + len(received)),
        out_specs=pl.BlockSpec(memory_space=pltpu.HBM),
        out_shape=jax.ShapeDtypeStruct(own.shape, jnp.float32),
        scratch_shapes=[pltpu.VMEM(own.shape, jnp.float32), pltpu.SemaphoreType.DMA((slots,))],
        compiler_params=PARAMS,
        name="tree_sum",
    )(own, *received)


def shards(voltages, gains, positions, directions, antenna_row_lookup, chan_order, delays):
    chan_count = lax.axis_size("chan")
    band_count = lax.axis_size("band")
    per_dev = gains.shape[2]
    assert per_dev == lax.axis_size("beam") == 2
    in_band = per_dev * chan_count
    total = in_band * band_count
    ants, samples = voltages.shape[1], voltages.shape[4]
    bins = samples // INTEG

    middle = chan_count // 2
    near = list(range(middle))
    distant = list(range(chan_count - 2, middle - 1, -1))
    middle = chan_count - 1
    masks = distant + near[1:] + [0, middle]
    cut = ants // 2
    first = split_channels(voltages, [(middle, 0, cut)], True)
    across = split_channels(voltages, [(m, 0, ants) for m in distant], True, first[0])
    *beside, rest = split_channels(voltages, [(m, 0, ants) for m in near] + [(middle, cut, ants)], True, across[0])
    first = [chan_partner(first[0], middle)]
    across = [chan_partner(v, m) for v, m in zip(across, distant)]
    rest = chan_partner(rest, middle)
    beside = [beside[0]] + [chan_partner(v, m) for v, m in zip(beside[1:], near[1:])]

    bits = [("beam", 0)]
    for axis, count in (("chan", chan_count), ("band", band_count)):
        bits += [(axis, bit) for bit in range(count.bit_length() - 1)]
    last = bits[-4:]
    got = [bit for bit in last if bit in (("beam", 0), ("chan", chan_count.bit_length() - 2))]
    got += [bit for bit in last[::-1] if bit not in got][: 2 - len(got)]
    stages = [(pair, pair, []) for pair in (bits[:-4][i : i + 2] for i in range(0, len(bits) - 4, 2))]
    stages.append((last, got, [bit for bit in last if bit not in got]))

    lookup = antenna_row_lookup.reshape(1, -1)
    placed, _ = lax.optimization_barrier((positions, beside[0]))
    ours, right, length, dirs, *maps = our_weights(
        placed, lookup, gains[:, 0], directions, chan_order, delays, masks, stages, bins
    )
    weights = [ours, their_weights(right, length, partner(dirs, [("beam", 0)]))]
    partial = early_beams(weights, [beside[0]] + first, ants * (chan_count - 2), ants - cut)
    partial = early_beams(weights, across + beside[1:], 0, 0, partial)

    high, low, *other = last_levels(weights, rest, partial, total)
    for number, ((_, got, sent), matrix) in enumerate(zip(stages, maps)):
        states = [high, low]
        for flips in subsets(got)[1:]:
            states.append(partner(other[len(flips) - 1] if ("beam", 0) in flips else high, flips))
        result = tree_stage(matrix, states, bins, directions.shape[1], number == 0, bool(sent))
        if not sent:
            high, low = result
    received = [partner(value, flips) for value, flips in zip(result[1:], subsets(sent)[1:])]
    return tree_sum(result[0], received).reshape(1, per_dev, bins, directions.shape[1])


def solution(mesh):
    placed = (
        P(None, "chan", "band", None, "group"),
        P(None, "band", "chan", None),
        P(),
        P(None, ("group", "beam")),
        P(),
        P(),
        P(),
    )
    return jax.shard_map(
        shards,
        mesh=mesh,
        in_specs=placed,
        out_specs=P("band", "chan", None, ("group", "beam")),
        check_vma=False,
    )
```

```python
import math

import jax
import jax.numpy as jnp
from jax import lax
from jax.experimental import pallas as pl
from jax.experimental.pallas import tpu as pltpu
from jax.sharding import PartitionSpec as P

INTEG = 8
VMEM = pl.BlockSpec(memory_space=pltpu.VMEM)
SMEM = pl.BlockSpec(memory_space=pltpu.SMEM)
PARAMS = pltpu.CompilerParams(vmem_limit_bytes=40 * 1024 * 1024)
SIN = (6.283184915580925, -41.34158901325128, 81.59993513909575, -76.61436771142901, 41.342343389037076, -12.470285565721209)
COS = (0.9999992089426497, -19.738979914331107, 64.92864094416844, -85.27141067260794, 58.789407905427666, -21.069178520245686)
PHASE_ROWS = 32
LONG = pl.CostEstimate(flops=10**10, bytes_accessed=10**8, transcendentals=10**8)
SHORT = pl.CostEstimate(flops=0, bytes_accessed=0, transcendentals=0)


def partner(value, flips):
    axes = tuple(axis for axis in ("chan", "band", "beam") if axis in dict(flips))
    sizes = [lax.axis_size(axis) for axis in axes]
    flip = 0
    for axis, bit in flips:
        flip ^= (1 << bit) * math.prod(sizes[axes.index(axis) + 1 :])
    pairs = [(source, source ^ flip) for source in range(math.prod(sizes))]
    return lax.ppermute(value, axes, pairs)


def chan_partner(value, mask):
    return partner(value, [("chan", bit) for bit in range(mask.bit_length()) if mask >> bit & 1])


def split_channels(voltages, pieces, from_hbm, token=None):
    parts, ants, _, chans, samples = voltages.shape
    per_dev = lax.axis_size("beam")
    start = min(first for _, first, _ in pieces)
    stop = max(last for _, _, last in pieces)
    group = max(16, (stop - start) // 2)
    jobs = [(p, first) for first in range(start, stop, group) for p in range(parts)]
    lanes = range(0, samples, 128)
    tokens = [] if token is None else [token]

    def kernel(v_ref, *refs):
        refs = refs[len(tokens) :]
        outs, wide, (raw, sems) = refs[: len(pieces)], refs[len(pieces) : -2], refs[-2:]
        z = lax.axis_index("chan")
        e = lax.axis_index("beam")

        def rows(number):
            p, first = jobs[number]
            return v_ref.at[p, pl.ds(first * chans, group * chans), :]

        def fetch(number):
            return pltpu.make_async_copy(rows(number), raw.at[number], sems.at[number])

        if from_hbm:
            for number in range(len(jobs)):
                fetch(number).start()
        for number, (p, first) in enumerate(jobs):
            if from_hbm:
                fetch(number).wait()
            block = raw.at[number] if from_hbm else rows(number)
            slot = number % 2
            for lane, half in zip(lanes, wide):
                half[slot, pl.ds(0, group * chans), :] = block[:, pl.ds(lane, 128)].astype(jnp.float32)
            for (mask, piece_first, piece_last), out in zip(pieces, outs):
                if piece_first <= first < piece_last:
                    chan = (z ^ mask) * per_dev + e
                    at = pl.ds(first - piece_first, group)
                    for lane, half in zip(lanes, wide):
                        out[p, at, pl.ds(lane, 128)] = half[slot, pl.ds(chan, group, stride=chans), :].astype(jnp.bfloat16)

    place = pltpu.HBM if from_hbm else pltpu.VMEM
    raw_slots = len(jobs) if from_hbm else 1
    return pl.pallas_call(
        kernel,
        in_specs=[pl.BlockSpec(memory_space=place)] + [pl.BlockSpec(memory_space=pl.ANY)] * len(tokens),
        out_specs=[VMEM] * len(pieces),
        out_shape=[
            jax.ShapeDtypeStruct((parts, last - first, samples), jnp.bfloat16) for _, first, last in pieces
        ],
        scratch_shapes=[pltpu.VMEM((2, (group + 1) * chans, 128), jnp.float32)] * len(lanes)
        + [
            pltpu.VMEM((raw_slots, group * chans, samples), jnp.bfloat16),
            pltpu.SemaphoreType.DMA((raw_slots,)),
        ],
        compiler_params=PARAMS,
        name="split_channels",
    )(pltpu.with_memory_space_constraint(voltages.reshape(parts, ants * chans, samples), place), *tokens)


def horner(coefs, u):
    total = coefs[-1] * u + coefs[-2]
    for coef in coefs[-3::-1]:
        total = total * u + coef
    return total


def bf16_parts(x):
    first = x.astype(jnp.bfloat16).astype(jnp.float32)
    rest = x - first
    second = rest.astype(jnp.bfloat16).astype(jnp.float32)
    return first, second, rest - second


def xor_blocks(x, index, count):
    size = x.shape[-1] // count
    for bit in range(count.bit_length() - 1):
        swapped = [x[..., (i ^ (1 << bit)) * size : (i ^ (1 << bit)) * size + size] for i in range(count)]
        x = jnp.where((index >> bit) & 1 == 1, jnp.concatenate(swapped, axis=-1), x)
    return x


def phase_rows(dirs):
    parts = jnp.concatenate(bf16_parts(dirs), axis=0)
    rows = [parts, parts, parts, jnp.ones((3, dirs.shape[1]), jnp.float32)]
    rows.append(jnp.zeros((PHASE_ROWS - 30, dirs.shape[1]), jnp.float32))
    return jnp.concatenate(rows, axis=0).astype(jnp.bfloat16)


def fill_weights(left_ref, right_ref, length_ref, turns, out):
    _, beams, ants = out.shape
    block = turns.shape[0]
    lanes = min(ants, 512)

    def block_of_beams(number, carry):
        start = pl.multiple_of(number * block, block)
        turns[...] = lax.dot_general(
            left_ref[:, pl.ds(start, block)],
            right_ref[...],
            (((0,), (0,)), ((), ())),
            preferred_element_type=jnp.float32,
        )

        def rows(step, carry):
            at = pl.ds(pl.multiple_of(step * 16, 16), 16)
            to = pl.ds(pl.multiple_of(start + step * 16, 16), 16)
            for lane in range(0, ants, lanes):
                cols = pl.ds(lane, lanes)
                x = turns[at, cols]
                t = x - jnp.round(x)
                u = t * t
                scale = length_ref[:, cols]
                out[0, to, cols] = (horner(COS, u) * scale).astype(jnp.bfloat16)
                out[1, to, cols] = (horner(SIN, u) * (t * scale)).astype(jnp.bfloat16)
            return carry

        return lax.fori_loop(0, block // 16, rows, carry)

    lax.fori_loop(0, beams // block, block_of_beams, 0)


def subsets(bits):
    return [[bit for k, bit in enumerate(bits) if pick >> k & 1] for pick in range(1 << len(bits))]


def map_shapes(stages, per_dev, bins):
    return [(per_dev, bins << len(sent), bins * (1 + (1 << len(got)))) for _, got, sent in stages]


def fill_maps(delay_ref, outs, stages, bins):
    per_dev = lax.axis_size("beam")

    def place(flips):
        at = {axis: lax.axis_index(axis) for axis in ("band", "chan", "beam")}
        for axis, bit in flips:
            at[axis] = at[axis] ^ (1 << bit)
        return at

    def total_delay(bits, first_round, target, source, slot):
        moved = 0
        for k, (axis, bit) in enumerate(bits):
            later = [b for b in bits[k + 1 :] if b in target or b in source]
            end = place(target + later)
            start = place(target + later + [b for b in bits[k : k + 1] if b in target or b in source])
            delay = delay_ref[first_round + k, end["band"], end["chan"] * per_dev + slot]
            moved = moved + ((start[axis] >> bit) & 1) * delay
        return moved

    first_round = 0
    for (bits, got, sent), out in zip(stages, outs):
        sources = [[]] + subsets(got)
        shape = (bins, out.shape[2])
        row = lax.broadcasted_iota(jnp.int32, shape, 0)
        col = lax.broadcasted_iota(jnp.int32, shape, 1)
        for slot in range(per_dev):
            for number, target in enumerate(subsets(sent)):
                shift = jnp.zeros_like(col)
                for place_no, source in enumerate(sources):
                    moved = total_delay(bits, first_round, target, source, slot)
                    shift = jnp.where(col // bins == place_no, moved, shift)
                hit = lax.rem(row - col + len(bits) * bins + shape[1] - shift, bins) == 0
                out[slot, pl.ds(number * bins, bins), :] = jnp.where(hit, 1.0, 0.0).astype(jnp.bfloat16)
        first_round += len(bits)


def our_weights(positions, lookup, gains, dirs, chan_order, delays, masks, stages, bins):
    ants, beams = positions.shape[1], dirs.shape[1]
    per_dev = lax.axis_size("beam")
    size = ants // len(masks)
    lanes = min(ants, 512)
    _, band_count, in_band = delays.shape
    shapes = map_shapes(stages, per_dev, bins)

    def in_order(x, z):
        x = xor_blocks(x, z, len(masks))
        return jnp.concatenate([x[..., m * size : m * size + size] for m in masks], axis=-1)

    def kernel(order_ref, delay_ref, pos_ref, look_ref, gain_ref, dir_ref, out, right_ref, length_ref, copy_ref, *refs):
        maps, (left, turns) = refs[:-2], refs[-2:]
        copy_ref[...] = dir_ref[...]
        z = lax.axis_index("chan")
        e = lax.axis_index("beam")
        slot = lax.axis_index("band") * in_band + z * per_dev + e
        freq = 1.0 + order_ref[slot].astype(jnp.float32) * (1.0 / (band_count * in_band))

        g_re = in_order(jnp.where(e == 0, gain_ref[0, 0:1, :], gain_ref[0, 1:2, :]), z)
        g_im = in_order(jnp.where(e == 0, gain_ref[1, 0:1, :], gain_ref[1, 1:2, :]), z)
        top = jnp.maximum(jnp.abs(g_re), jnp.abs(g_im))
        low = jnp.minimum(jnp.abs(g_re), jnp.abs(g_im))
        ratio = low / jnp.where(top > 0.0, top, 1.0)
        length_ref[...] = top * jnp.sqrt(1.0 + ratio * ratio) * (1.0 / math.sqrt(ants))

        parts = [jnp.concatenate([part] * 3, axis=0) for part in bf16_parts(pos_ref[...] * -freq)]
        parts.append(jnp.zeros((PHASE_ROWS - 27, ants), jnp.float32))
        table = jnp.concatenate(parts, axis=0).astype(jnp.bfloat16)
        look = in_order(look_ref[...], z)
        antenna = lax.broadcasted_iota(jnp.int32, (ants, lanes), 0)
        turn_parts = jnp.concatenate(
            [jnp.zeros((27, ants), jnp.float32)]
            + list(bf16_parts(jnp.arctan2(g_im, g_re) * (0.5 / math.pi)))
            + [jnp.zeros((PHASE_ROWS - 30, ants), jnp.float32)],
            axis=0,
        )
        for lane in range(0, ants, lanes):
            chosen = jnp.where(antenna == look[:, lane : lane + lanes], 1.0, 0.0).astype(jnp.bfloat16)
            rows = jnp.dot(table, chosen, preferred_element_type=jnp.float32)
            right_ref[:, pl.ds(lane, lanes)] = (rows + turn_parts[:, lane : lane + lanes]).astype(jnp.bfloat16)
        left[...] = phase_rows(dir_ref[...])
        fill_weights(left, right_ref, length_ref, turns, out)
        fill_maps(delay_ref, maps, stages, bins)

    return pl.pallas_call(
        kernel,
        in_specs=[SMEM] * 2 + [VMEM] * 4,
        out_specs=[VMEM] * (4 + len(shapes)),
        out_shape=[
            jax.ShapeDtypeStruct((2, beams, ants), jnp.bfloat16),
            jax.ShapeDtypeStruct((PHASE_ROWS, ants), jnp.bfloat16),
            jax.ShapeDtypeStruct((1, ants), jnp.float32),
            jax.ShapeDtypeStruct(dirs.shape, jnp.float32),
        ]
        + [jax.ShapeDtypeStruct(shape, jnp.bfloat16) for shape in shapes],
        scratch_shapes=[
            pltpu.VMEM((PHASE_ROWS, beams), jnp.bfloat16),
            pltpu.VMEM((min(beams, 128), ants), jnp.float32),
        ],
        compiler_params=PARAMS,
        cost_estimate=LONG,
        name="our_weights",
    )(chan_order, delays, positions, lookup, gains, dirs)


def their_weights(right, length, dirs):
    ants, beams = right.shape[1], dirs.shape[1]

    def kernel(right_ref, length_ref, dir_ref, out, left, turns):
        left[...] = phase_rows(dir_ref[...])
        fill_weights(left, right_ref, length_ref, turns, out)

    return pl.pallas_call(
        kernel,
        in_specs=[VMEM] * 3,
        out_specs=VMEM,
        out_shape=jax.ShapeDtypeStruct((2, beams, ants), jnp.bfloat16),
        scratch_shapes=[
            pltpu.VMEM((PHASE_ROWS, beams), jnp.bfloat16),
            pltpu.VMEM((min(beams, 128), ants), jnp.float32),
        ],
        compiler_params=PARAMS,
        cost_estimate=SHORT,
        name="their_weights",
    )(right, length, dirs)


def chunk_product(w_ref, blocks, first, beam_rows):
    re = jnp.concatenate([re for re, _ in blocks], axis=0)
    im = jnp.concatenate([im for _, im in blocks], axis=0)
    straight = jnp.concatenate([re, im], axis=1)
    turned = jnp.concatenate([-im, re], axis=1)
    cols = pl.ds(first, re.shape[0])
    dot = lambda a, b: jnp.dot(a, b, preferred_element_type=jnp.float32)
    return dot(w_ref[0, beam_rows, cols], straight) + dot(w_ref[1, beam_rows, cols], turned)


HIGH_EXTRA, OTHER_EXTRA = 1, (0, 2)
SUM_EXTRA = (1, 0, 2)


def filled(ref, before, after):
    zeros = lambda count: [jnp.zeros((count, ref.shape[2]), ref.dtype)] if count else []
    return [jnp.concatenate(zeros(before) + [ref[p]] + zeros(after), axis=0) for p in range(2)]


def early_beams(weights, chunks, first, rest, partial=None):
    half = weights[0].shape[1]
    samples = chunks[0].shape[2]
    step = min(half, 256)
    before = [] if partial is None else [partial]

    def kernel(ours_ref, theirs_ref, *refs):
        refs, out = refs[:-1], refs[-1]
        blocks = [filled(ref, 0, 0) for ref in refs[len(before) : -1]] + [filled(refs[-1], 0, rest)]
        for number, w_ref in enumerate((ours_ref, theirs_ref)):
            for row in range(0, half, step):
                product = chunk_product(w_ref, blocks, first, pl.ds(row, step))
                at = pl.ds(number * half + row, step)
                out[at, :] = product + refs[0][at, :] if before else product

    return pl.pallas_call(
        kernel,
        in_specs=[VMEM] * (2 + len(before) + len(chunks)),
        out_specs=VMEM,
        out_shape=jax.ShapeDtypeStruct((2 * half, 2 * samples), jnp.float32),
        compiler_params=PARAMS,
        cost_estimate=SHORT,
        name="early_beams",
    )(*weights, *before, *chunks)


def two_parts(x):
    high = x.astype(jnp.bfloat16)
    return high, (x - high.astype(jnp.float32)).astype(jnp.bfloat16)


def message(blocks, width, extra):
    return jax.ShapeDtypeStruct((blocks * width // 128 + 16 * extra, 128), jnp.bfloat16)


def put(ref, first, value):
    bins, width = value.shape
    for lane in range(0, width, 128):
        ref[pl.ds(first, bins), :] = value[:, lane : lane + 128].astype(ref.dtype)
        first += bins
    return first


def take(ref, number, bins, width):
    first = number * bins * width // 128
    pieces = [ref[pl.ds(first + lane // 128 * bins, bins), :] for lane in range(0, width, 128)]
    return jnp.concatenate(pieces, axis=1)


def pad(ref, first):
    if first < ref.shape[0]:
        ref[pl.ds(first, ref.shape[0] - first), :] = jnp.zeros((ref.shape[0] - first, 128), ref.dtype)


def last_levels(weights, chunk, partial, total):
    _, half, ants = weights[0].shape
    samples = chunk.shape[2]
    bins = samples // INTEG
    count = chunk.shape[1]
    first = ants - count

    def kernel(ours_ref, theirs_ref, part_ref, chunk_ref, high_ref, low_ref, *sent_refs):
        re, im = chunk_ref[0], chunk_ref[1]
        antennas = jnp.concatenate(
            [jnp.concatenate([re, im], axis=1), jnp.concatenate([-im, re], axis=1)], axis=0
        )
        bin_no = lax.broadcasted_iota(jnp.int32, (bins, samples), 0)
        time = lax.broadcasted_iota(jnp.int32, (bins, samples), 1)
        centre = jnp.where(time // INTEG == bin_no, 1.0 / INTEG, 0.0) - 1.0 / samples
        centre = jnp.concatenate([centre, centre], axis=1).astype(jnp.bfloat16)
        beams = []
        for number, w_ref in enumerate((ours_ref, theirs_ref)):
            both = jnp.concatenate([w_ref[0, :, pl.ds(first, count)], w_ref[1, :, pl.ds(first, count)]], axis=1)
            product = jnp.dot(both, antennas, preferred_element_type=jnp.float32)
            beams.append(part_ref[pl.ds(number * half, half), :] + product)
        for number, beam in enumerate(beams):
            re, im = beam[:, :samples], beam[:, samples:]
            parts = jnp.concatenate(two_parts(re * re + im * im), axis=1)
            level = lax.dot_general(centre, parts, (((1,), (1,)), ((), ())), preferred_element_type=jnp.float32)
            high, low = two_parts(level * (1.0 / math.sqrt(total)))
            if number == 0:
                pad(high_ref, put(high_ref, 0, high))
                put(low_ref, 0, low)
            else:
                for sent_ref in sent_refs:
                    pad(sent_ref, put(sent_ref, 0, high))

    return pl.pallas_call(
        kernel,
        in_specs=[VMEM] * 4,
        out_specs=[VMEM] * 4,
        out_shape=[message(bins, half, extra) for extra in (HIGH_EXTRA, 0, *OTHER_EXTRA)],
        compiler_params=PARAMS,
        name="last_levels",
    )(*weights, partial, chunk)


def tree_stage(matrix, states, bins, width, first, final):
    slots, rows, _ = matrix.shape
    targets = rows // bins
    blocks = bins * slots
    if final:
        shapes = [jax.ShapeDtypeStruct((slots, bins, width), jnp.float32)]
        shapes += [message(blocks, width, extra) for extra in SUM_EXTRA[: targets - 1]]
    else:
        shapes = [message(blocks, width, 0)] * 2

    def kernel(map_ref, *refs):
        ins, outs = refs[: len(states)], refs[len(states) :]
        row = 0
        for slot in range(slots):
            column = [take(ref, 0 if first else slot, bins, width) for ref in ins]
            value = jnp.dot(map_ref[slot], jnp.concatenate(column, axis=0), preferred_element_type=jnp.float32)
            if final:
                outs[0][slot] = value[:bins]
                parts = [value[t * bins : t * bins + bins] for t in range(1, targets)]
            else:
                parts = two_parts(value)
            for out, part in zip(outs[-len(parts) :], parts):
                after = put(out, row, part)
            row = after
        for out in outs[-len(parts) :]:
            pad(out, row)

    return pl.pallas_call(
        kernel,
        in_specs=[VMEM] * (1 + len(states)),
        out_specs=[VMEM] * len(shapes),
        out_shape=shapes,
        compiler_params=PARAMS,
        name="tree_stage",
    )(matrix, *states)


def tree_sum(own, received):
    slots, bins, width = own.shape

    def kernel(own_ref, *refs):
        out, total, sems = refs[-3:]
        copies = [pltpu.make_async_copy(total.at[slot], out.at[slot], sems.at[slot]) for slot in range(slots)]
        for slot, copy in enumerate(copies):
            value = own_ref[slot]
            for ref in refs[:-3]:
                value = value + take(ref, slot, bins, width).astype(jnp.float32)
            total[slot] = value
            copy.start()
        for copy in copies:
            copy.wait()

    return pl.pallas_call(
        kernel,
        in_specs=[VMEM] * (1 + len(received)),
        out_specs=pl.BlockSpec(memory_space=pltpu.HBM),
        out_shape=jax.ShapeDtypeStruct(own.shape, jnp.float32),
        scratch_shapes=[pltpu.VMEM(own.shape, jnp.float32), pltpu.SemaphoreType.DMA((slots,))],
        compiler_params=PARAMS,
        name="tree_sum",
    )(own, *received)


def shards(voltages, gains, positions, directions, antenna_row_lookup, chan_order, delays):
    chan_count = lax.axis_size("chan")
    band_count = lax.axis_size("band")
    per_dev = gains.shape[2]
    assert per_dev == lax.axis_size("beam") == 2
    in_band = per_dev * chan_count
    total = in_band * band_count
    ants, samples = voltages.shape[1], voltages.shape[4]
    bins = samples // INTEG

    middle = chan_count // 2
    near = list(range(middle))
    distant = list(range(chan_count - 2, middle - 1, -1))
    middle = chan_count - 1
    masks = distant + near[1:] + [0, middle]
    cut = ants // 2
    first = split_channels(voltages, [(middle, 0, cut)], True)
    across = split_channels(voltages, [(m, 0, ants) for m in distant], True, first[0])
    *beside, rest = split_channels(voltages, [(m, 0, ants) for m in near] + [(middle, cut, ants)], True, across[0])
    first = [chan_partner(first[0], middle)]
    across = [chan_partner(v, m) for v, m in zip(across, distant)]
    rest = chan_partner(rest, middle)
    beside = [beside[0]] + [chan_partner(v, m) for v, m in zip(beside[1:], near[1:])]

    bits = [("beam", 0)]
    for axis, count in (("chan", chan_count), ("band", band_count)):
        bits += [(axis, bit) for bit in range(count.bit_length() - 1)]
    last = bits[-4:]
    got = [bit for bit in last if bit in (("beam", 0), ("chan", chan_count.bit_length() - 2))]
    got += [bit for bit in last[::-1] if bit not in got][: 2 - len(got)]
    stages = [(pair, pair, []) for pair in (bits[:-4][i : i + 2] for i in range(0, len(bits) - 4, 2))]
    stages.append((last, got, [bit for bit in last if bit not in got]))

    lookup = antenna_row_lookup.reshape(1, -1)
    placed, _ = lax.optimization_barrier((positions, beside[0]))
    ours, right, length, dirs, *maps = our_weights(
        placed, lookup, gains[:, 0], directions, chan_order, delays, masks, stages, bins
    )
    weights = [ours, their_weights(right, length, partner(dirs, [("beam", 0)]))]
    partial = early_beams(weights, [beside[0]] + first, ants * (chan_count - 2), ants - cut)
    partial = early_beams(weights, across + beside[1:], 0, 0, partial)

    high, low, *other = last_levels(weights, rest, partial, total)
    for number, ((_, got, sent), matrix) in enumerate(zip(stages, maps)):
        states = [high, low]
        for flips in subsets(got)[1:]:
            states.append(partner(other[len(flips) - 1] if ("beam", 0) in flips else high, flips))
        result = tree_stage(matrix, states, bins, directions.shape[1], number == 0, bool(sent))
        if not sent:
            high, low = result
    received = [partner(value, flips) for value, flips in zip(result[1:], subsets(sent)[1:])]
    return tree_sum(result[0], received).reshape(1, per_dev, bins, directions.shape[1])


def solution(mesh):
    placed = (
        P(None, "chan", "band", None, "group"),
        P(None, "band", "chan", None),
        P(),
        P(None, ("group", "beam")),
        P(),
        P(),
        P(),
    )
    return jax.shard_map(
        shards,
        mesh=mesh,
        in_specs=placed,
        out_specs=P("band", "chan", None, ("group", "beam")),
        check_vma=False,
    )
```

```python
import math

import jax
import jax.numpy as jnp
from jax import lax
from jax.experimental import pallas as pl
from jax.experimental.pallas import tpu as pltpu
from jax.sharding import PartitionSpec as P

INTEG = 8
VMEM = pl.BlockSpec(memory_space=pltpu.VMEM)
SMEM = pl.BlockSpec(memory_space=pltpu.SMEM)
PARAMS = pltpu.CompilerParams(vmem_limit_bytes=40 * 1024 * 1024)
SIN = (6.283184915580925, -41.34158901325128, 81.59993513909575, -76.61436771142901, 41.342343389037076, -12.470285565721209)
COS = (0.9999992089426497, -19.738979914331107, 64.92864094416844, -85.27141067260794, 58.789407905427666, -21.069178520245686)
PHASE_ROWS = 32
LONG = pl.CostEstimate(flops=10**10, bytes_accessed=10**8, transcendentals=10**8)
SHORT = pl.CostEstimate(flops=0, bytes_accessed=0, transcendentals=0)


def partner(value, flips):
    axes = tuple(axis for axis in ("chan", "band", "beam") if axis in dict(flips))
    sizes = [lax.axis_size(axis) for axis in axes]
    flip = 0
    for axis, bit in flips:
        flip ^= (1 << bit) * math.prod(sizes[axes.index(axis) + 1 :])
    pairs = [(source, source ^ flip) for source in range(math.prod(sizes))]
    return lax.ppermute(value, axes, pairs)


def chan_partner(value, mask):
    return partner(value, [("chan", bit) for bit in range(mask.bit_length()) if mask >> bit & 1])


def split_channels(voltages, pieces, from_hbm, token=None):
    parts, ants, _, chans, samples = voltages.shape
    per_dev = lax.axis_size("beam")
    start = min(first for _, first, _ in pieces)
    stop = max(last for _, _, last in pieces)
    group = max(16, (stop - start) // 2)
    jobs = [(p, first) for first in range(start, stop, group) for p in range(parts)]
    lanes = range(0, samples, 128)
    tokens = [] if token is None else [token]

    def kernel(v_ref, *refs):
        refs = refs[len(tokens) :]
        outs, wide, (raw, sems) = refs[: len(pieces)], refs[len(pieces) : -2], refs[-2:]
        z = lax.axis_index("chan")
        e = lax.axis_index("beam")

        def rows(number):
            p, first = jobs[number]
            return v_ref.at[p, pl.ds(first * chans, group * chans), :]

        def fetch(number):
            return pltpu.make_async_copy(rows(number), raw.at[number], sems.at[number])

        if from_hbm:
            for number in range(len(jobs)):
                fetch(number).start()
        for number, (p, first) in enumerate(jobs):
            if from_hbm:
                fetch(number).wait()
            block = raw.at[number] if from_hbm else rows(number)
            slot = number % 2
            for lane, half in zip(lanes, wide):
                half[slot, pl.ds(0, group * chans), :] = block[:, pl.ds(lane, 128)].astype(jnp.float32)
            for (mask, piece_first, piece_last), out in zip(pieces, outs):
                if piece_first <= first < piece_last:
                    chan = (z ^ mask) * per_dev + e
                    at = pl.ds(first - piece_first, group)
                    for lane, half in zip(lanes, wide):
                        out[p, at, pl.ds(lane, 128)] = half[slot, pl.ds(chan, group, stride=chans), :].astype(jnp.bfloat16)

    place = pltpu.HBM if from_hbm else pltpu.VMEM
    raw_slots = len(jobs) if from_hbm else 1
    return pl.pallas_call(
        kernel,
        in_specs=[pl.BlockSpec(memory_space=place)] + [pl.BlockSpec(memory_space=pl.ANY)] * len(tokens),
        out_specs=[VMEM] * len(pieces),
        out_shape=[
            jax.ShapeDtypeStruct((parts, last - first, samples), jnp.bfloat16) for _, first, last in pieces
        ],
        scratch_shapes=[pltpu.VMEM((2, (group + 1) * chans, 128), jnp.float32)] * len(lanes)
        + [
            pltpu.VMEM((raw_slots, group * chans, samples), jnp.bfloat16),
            pltpu.SemaphoreType.DMA((raw_slots,)),
        ],
        compiler_params=PARAMS,
        name="split_channels",
    )(pltpu.with_memory_space_constraint(voltages.reshape(parts, ants * chans, samples), place), *tokens)


def horner(coefs, u):
    total = coefs[-1] * u + coefs[-2]
    for coef in coefs[-3::-1]:
        total = total * u + coef
    return total


def bf16_parts(x):
    first = x.astype(jnp.bfloat16).astype(jnp.float32)
    rest = x - first
    second = rest.astype(jnp.bfloat16).astype(jnp.float32)
    return first, second, rest - second


def xor_blocks(x, index, count):
    size = x.shape[-1] // count
    for bit in range(count.bit_length() - 1):
        swapped = [x[..., (i ^ (1 << bit)) * size : (i ^ (1 << bit)) * size + size] for i in range(count)]
        x = jnp.where((index >> bit) & 1 == 1, jnp.concatenate(swapped, axis=-1), x)
    return x


def phase_rows(dirs):
    parts = jnp.concatenate(bf16_parts(dirs), axis=0)
    rows = [parts, parts, parts, jnp.ones((3, dirs.shape[1]), jnp.float32)]
    rows.append(jnp.zeros((PHASE_ROWS - 30, dirs.shape[1]), jnp.float32))
    return jnp.concatenate(rows, axis=0).astype(jnp.bfloat16)


def fill_weights(left_ref, right_ref, length_ref, turns, out):
    _, beams, ants = out.shape
    block = turns.shape[0]
    lanes = min(ants, 512)

    def block_of_beams(number, carry):
        start = pl.multiple_of(number * block, block)
        turns[...] = lax.dot_general(
            left_ref[:, pl.ds(start, block)],
            right_ref[...],
            (((0,), (0,)), ((), ())),
            preferred_element_type=jnp.float32,
        )

        def rows(step, carry):
            at = pl.ds(pl.multiple_of(step * 16, 16), 16)
            to = pl.ds(pl.multiple_of(start + step * 16, 16), 16)
            for lane in range(0, ants, lanes):
                cols = pl.ds(lane, lanes)
                x = turns[at, cols]
                t = x - jnp.round(x)
                u = t * t
                scale = length_ref[:, cols]
                out[0, to, cols] = (horner(COS, u) * scale).astype(jnp.bfloat16)
                out[1, to, cols] = (horner(SIN, u) * (t * scale)).astype(jnp.bfloat16)
            return carry

        return lax.fori_loop(0, block // 16, rows, carry)

    lax.fori_loop(0, beams // block, block_of_beams, 0)


def subsets(bits):
    return [[bit for k, bit in enumerate(bits) if pick >> k & 1] for pick in range(1 << len(bits))]


def map_shapes(stages, per_dev, bins):
    return [(per_dev, bins << len(sent), bins * (1 + (1 << len(got)))) for _, got, sent in stages]


def fill_maps(delay_ref, outs, stages, bins):
    per_dev = lax.axis_size("beam")

    def place(flips):
        at = {axis: lax.axis_index(axis) for axis in ("band", "chan", "beam")}
        for axis, bit in flips:
            at[axis] = at[axis] ^ (1 << bit)
        return at

    def total_delay(bits, first_round, target, source, slot):
        moved = 0
        for k, (axis, bit) in enumerate(bits):
            later = [b for b in bits[k + 1 :] if b in target or b in source]
            end = place(target + later)
            start = place(target + later + [b for b in bits[k : k + 1] if b in target or b in source])
            delay = delay_ref[first_round + k, end["band"], end["chan"] * per_dev + slot]
            moved = moved + ((start[axis] >> bit) & 1) * delay
        return moved

    first_round = 0
    for (bits, got, sent), out in zip(stages, outs):
        sources = [[]] + subsets(got)
        shape = (bins, out.shape[2])
        row = lax.broadcasted_iota(jnp.int32, shape, 0)
        col = lax.broadcasted_iota(jnp.int32, shape, 1)
        for slot in range(per_dev):
            for number, target in enumerate(subsets(sent)):
                shift = jnp.zeros_like(col)
                for place_no, source in enumerate(sources):
                    moved = total_delay(bits, first_round, target, source, slot)
                    shift = jnp.where(col // bins == place_no, moved, shift)
                hit = lax.rem(row - col + len(bits) * bins + shape[1] - shift, bins) == 0
                out[slot, pl.ds(number * bins, bins), :] = jnp.where(hit, 1.0, 0.0).astype(jnp.bfloat16)
        first_round += len(bits)


def our_weights(positions, lookup, gains, dirs, chan_order, delays, masks, stages, bins):
    ants, beams = positions.shape[1], dirs.shape[1]
    per_dev = lax.axis_size("beam")
    size = ants // len(masks)
    lanes = min(ants, 512)
    _, band_count, in_band = delays.shape
    shapes = map_shapes(stages, per_dev, bins)

    def in_order(x, z):
        x = xor_blocks(x, z, len(masks))
        return jnp.concatenate([x[..., m * size : m * size + size] for m in masks], axis=-1)

    def kernel(order_ref, delay_ref, pos_ref, look_ref, gain_ref, dir_ref, out, right_ref, length_ref, copy_ref, *refs):
        maps, (left, turns) = refs[:-2], refs[-2:]
        copy_ref[...] = dir_ref[...]
        z = lax.axis_index("chan")
        e = lax.axis_index("beam")
        slot = lax.axis_index("band") * in_band + z * per_dev + e
        freq = 1.0 + order_ref[slot].astype(jnp.float32) * (1.0 / (band_count * in_band))

        g_re = in_order(jnp.where(e == 0, gain_ref[0, 0:1, :], gain_ref[0, 1:2, :]), z)
        g_im = in_order(jnp.where(e == 0, gain_ref[1, 0:1, :], gain_ref[1, 1:2, :]), z)
        top = jnp.maximum(jnp.abs(g_re), jnp.abs(g_im))
        low = jnp.minimum(jnp.abs(g_re), jnp.abs(g_im))
        ratio = low / jnp.where(top > 0.0, top, 1.0)
        length_ref[...] = top * jnp.sqrt(1.0 + ratio * ratio) * (1.0 / math.sqrt(ants))

        parts = [jnp.concatenate([part] * 3, axis=0) for part in bf16_parts(pos_ref[...] * -freq)]
        parts.append(jnp.zeros((PHASE_ROWS - 27, ants), jnp.float32))
        table = jnp.concatenate(parts, axis=0).astype(jnp.bfloat16)
        look = in_order(look_ref[...], z)
        antenna = lax.broadcasted_iota(jnp.int32, (ants, lanes), 0)
        turn_parts = jnp.concatenate(
            [jnp.zeros((27, ants), jnp.float32)]
            + list(bf16_parts(jnp.arctan2(g_im, g_re) * (0.5 / math.pi)))
            + [jnp.zeros((PHASE_ROWS - 30, ants), jnp.float32)],
            axis=0,
        )
        for lane in range(0, ants, lanes):
            chosen = jnp.where(antenna == look[:, lane : lane + lanes], 1.0, 0.0).astype(jnp.bfloat16)
            rows = jnp.dot(table, chosen, preferred_element_type=jnp.float32)
            right_ref[:, pl.ds(lane, lanes)] = (rows + turn_parts[:, lane : lane + lanes]).astype(jnp.bfloat16)
        left[...] = phase_rows(dir_ref[...])
        fill_weights(left, right_ref, length_ref, turns, out)
        fill_maps(delay_ref, maps, stages, bins)

    return pl.pallas_call(
        kernel,
        in_specs=[SMEM] * 2 + [VMEM] * 4,
        out_specs=[VMEM] * (4 + len(shapes)),
        out_shape=[
            jax.ShapeDtypeStruct((2, beams, ants), jnp.bfloat16),
            jax.ShapeDtypeStruct((PHASE_ROWS, ants), jnp.bfloat16),
            jax.ShapeDtypeStruct((1, ants), jnp.float32),
            jax.ShapeDtypeStruct(dirs.shape, jnp.float32),
        ]
        + [jax.ShapeDtypeStruct(shape, jnp.bfloat16) for shape in shapes],
        scratch_shapes=[
            pltpu.VMEM((PHASE_ROWS, beams), jnp.bfloat16),
            pltpu.VMEM((min(beams, 128), ants), jnp.float32),
        ],
        compiler_params=PARAMS,
        cost_estimate=LONG,
        name="our_weights",
    )(chan_order, delays, positions, lookup, gains, dirs)


def their_weights(right, length, dirs):
    ants, beams = right.shape[1], dirs.shape[1]

    def kernel(right_ref, length_ref, dir_ref, out, left, turns):
        left[...] = phase_rows(dir_ref[...])
        fill_weights(left, right_ref, length_ref, turns, out)

    return pl.pallas_call(
        kernel,
        in_specs=[VMEM] * 3,
        out_specs=VMEM,
        out_shape=jax.ShapeDtypeStruct((2, beams, ants), jnp.bfloat16),
        scratch_shapes=[
            pltpu.VMEM((PHASE_ROWS, beams), jnp.bfloat16),
            pltpu.VMEM((min(beams, 128), ants), jnp.float32),
        ],
        compiler_params=PARAMS,
        cost_estimate=SHORT,
        name="their_weights",
    )(right, length, dirs)


def chunk_product(w_ref, blocks, first, beam_rows):
    re = jnp.concatenate([re for re, _ in blocks], axis=0)
    im = jnp.concatenate([im for _, im in blocks], axis=0)
    straight = jnp.concatenate([re, im], axis=1)
    turned = jnp.concatenate([-im, re], axis=1)
    cols = pl.ds(first, re.shape[0])
    dot = lambda a, b: jnp.dot(a, b, preferred_element_type=jnp.float32)
    return dot(w_ref[0, beam_rows, cols], straight) + dot(w_ref[1, beam_rows, cols], turned)


HIGH_EXTRA, OTHER_EXTRA = 1, (1, 0)
SUM_EXTRA = (0, 0, 1)


def filled(ref, before, after):
    zeros = lambda count: [jnp.zeros((count, ref.shape[2]), ref.dtype)] if count else []
    return [jnp.concatenate(zeros(before) + [ref[p]] + zeros(after), axis=0) for p in range(2)]


def early_beams(weights, chunks, first, rest, partial=None):
    half = weights[0].shape[1]
    samples = chunks[0].shape[2]
    step = min(half, 256)
    before = [] if partial is None else [partial]

    def kernel(ours_ref, theirs_ref, *refs):
        refs, out = refs[:-1], refs[-1]
        blocks = [filled(ref, 0, 0) for ref in refs[len(before) : -1]] + [filled(refs[-1], 0, rest)]
        for number, w_ref in enumerate((ours_ref, theirs_ref)):
            for row in range(0, half, step):
                product = chunk_product(w_ref, blocks, first, pl.ds(row, step))
                at = pl.ds(number * half + row, step)
                out[at, :] = product + refs[0][at, :] if before else product

    return pl.pallas_call(
        kernel,
        in_specs=[VMEM] * (2 + len(before) + len(chunks)),
        out_specs=VMEM,
        out_shape=jax.ShapeDtypeStruct((2 * half, 2 * samples), jnp.float32),
        compiler_params=PARAMS,
        cost_estimate=SHORT,
        name="early_beams",
    )(*weights, *before, *chunks)


def two_parts(x):
    high = x.astype(jnp.bfloat16)
    return high, (x - high.astype(jnp.float32)).astype(jnp.bfloat16)


def message(blocks, width, extra):
    return jax.ShapeDtypeStruct((blocks * width // 128 + 16 * extra, 128), jnp.bfloat16)


def put(ref, first, value):
    bins, width = value.shape
    for lane in range(0, width, 128):
        ref[pl.ds(first, bins), :] = value[:, lane : lane + 128].astype(ref.dtype)
        first += bins
    return first


def take(ref, number, bins, width):
    first = number * bins * width // 128
    pieces = [ref[pl.ds(first + lane // 128 * bins, bins), :] for lane in range(0, width, 128)]
    return jnp.concatenate(pieces, axis=1)


def pad(ref, first):
    if first < ref.shape[0]:
        ref[pl.ds(first, ref.shape[0] - first), :] = jnp.zeros((ref.shape[0] - first, 128), ref.dtype)


def last_levels(weights, chunk, partial, total):
    _, half, ants = weights[0].shape
    samples = chunk.shape[2]
    bins = samples // INTEG
    count = chunk.shape[1]
    first = ants - count

    def kernel(ours_ref, theirs_ref, part_ref, chunk_ref, high_ref, low_ref, *sent_refs):
        re, im = chunk_ref[0], chunk_ref[1]
        antennas = jnp.concatenate(
            [jnp.concatenate([re, im], axis=1), jnp.concatenate([-im, re], axis=1)], axis=0
        )
        bin_no = lax.broadcasted_iota(jnp.int32, (bins, samples), 0)
        time = lax.broadcasted_iota(jnp.int32, (bins, samples), 1)
        centre = jnp.where(time // INTEG == bin_no, 1.0 / INTEG, 0.0) - 1.0 / samples
        centre = jnp.concatenate([centre, centre], axis=1).astype(jnp.bfloat16)
        beams = []
        for number, w_ref in enumerate((ours_ref, theirs_ref)):
            both = jnp.concatenate([w_ref[0, :, pl.ds(first, count)], w_ref[1, :, pl.ds(first, count)]], axis=1)
            product = jnp.dot(both, antennas, preferred_element_type=jnp.float32)
            beams.append(part_ref[pl.ds(number * half, half), :] + product)
        for number, beam in enumerate(beams):
            re, im = beam[:, :samples], beam[:, samples:]
            parts = jnp.concatenate(two_parts(re * re + im * im), axis=1)
            level = lax.dot_general(centre, parts, (((1,), (1,)), ((), ())), preferred_element_type=jnp.float32)
            high, low = two_parts(level * (1.0 / math.sqrt(total)))
            if number == 0:
                pad(high_ref, put(high_ref, 0, high))
                put(low_ref, 0, low)
            else:
                for sent_ref in sent_refs:
                    pad(sent_ref, put(sent_ref, 0, high))

    return pl.pallas_call(
        kernel,
        in_specs=[VMEM] * 4,
        out_specs=[VMEM] * 4,
        out_shape=[message(bins, half, extra) for extra in (HIGH_EXTRA, 0, *OTHER_EXTRA)],
        compiler_params=PARAMS,
        name="last_levels",
    )(*weights, partial, chunk)


def tree_stage(matrix, states, bins, width, first, final):
    slots, rows, _ = matrix.shape
    targets = rows // bins
    blocks = bins * slots
    if final:
        shapes = [jax.ShapeDtypeStruct((slots, bins, width), jnp.float32)]
        shapes += [message(blocks, width, extra) for extra in SUM_EXTRA[: targets - 1]]
    else:
        shapes = [message(blocks, width, 0)] * 2

    def kernel(map_ref, *refs):
        ins, outs = refs[: len(states)], refs[len(states) :]
        row = 0
        for slot in range(slots):
            column = [take(ref, 0 if first else slot, bins, width) for ref in ins]
            value = jnp.dot(map_ref[slot], jnp.concatenate(column, axis=0), preferred_element_type=jnp.float32)
            if final:
                outs[0][slot] = value[:bins]
                parts = [value[t * bins : t * bins + bins] for t in range(1, targets)]
            else:
                parts = two_parts(value)
            for out, part in zip(outs[-len(parts) :], parts):
                after = put(out, row, part)
            row = after
        for out in outs[-len(parts) :]:
            pad(out, row)

    return pl.pallas_call(
        kernel,
        in_specs=[VMEM] * (1 + len(states)),
        out_specs=[VMEM] * len(shapes),
        out_shape=shapes,
        compiler_params=PARAMS,
        name="tree_stage",
    )(matrix, *states)


def tree_sum(own, received):
    slots, bins, width = own.shape

    def kernel(own_ref, *refs):
        out, total, sems = refs[-3:]
        copies = [pltpu.make_async_copy(total.at[slot], out.at[slot], sems.at[slot]) for slot in range(slots)]
        for slot, copy in enumerate(copies):
            value = own_ref[slot]
            for ref in refs[:-3]:
                value = value + take(ref, slot, bins, width).astype(jnp.float32)
            total[slot] = value
            copy.start()
        for copy in copies:
            copy.wait()

    return pl.pallas_call(
        kernel,
        in_specs=[VMEM] * (1 + len(received)),
        out_specs=pl.BlockSpec(memory_space=pltpu.HBM),
        out_shape=jax.ShapeDtypeStruct(own.shape, jnp.float32),
        scratch_shapes=[pltpu.VMEM(own.shape, jnp.float32), pltpu.SemaphoreType.DMA((slots,))],
        compiler_params=PARAMS,
        name="tree_sum",
    )(own, *received)


def shards(voltages, gains, positions, directions, antenna_row_lookup, chan_order, delays):
    chan_count = lax.axis_size("chan")
    band_count = lax.axis_size("band")
    per_dev = gains.shape[2]
    assert per_dev == lax.axis_size("beam") == 2
    in_band = per_dev * chan_count
    total = in_band * band_count
    ants, samples = voltages.shape[1], voltages.shape[4]
    bins = samples // INTEG

    middle = chan_count // 2
    near = list(range(middle))
    distant = list(range(chan_count - 2, middle - 1, -1))
    middle = chan_count - 1
    masks = distant + near[1:] + [0, middle]
    cut = ants // 2
    first = split_channels(voltages, [(middle, 0, cut)], True)
    across = split_channels(voltages, [(m, 0, ants) for m in distant], True, first[0])
    *beside, rest = split_channels(voltages, [(m, 0, ants) for m in near] + [(middle, cut, ants)], True, across[0])
    first = [chan_partner(first[0], middle)]
    across = [chan_partner(v, m) for v, m in zip(across, distant)]
    rest = chan_partner(rest, middle)
    beside = [beside[0]] + [chan_partner(v, m) for v, m in zip(beside[1:], near[1:])]

    bits = [("beam", 0)]
    for axis, count in (("chan", chan_count), ("band", band_count)):
        bits += [(axis, bit) for bit in range(count.bit_length() - 1)]
    last = bits[-4:]
    got = [bit for bit in last if bit in (("beam", 0), ("chan", chan_count.bit_length() - 2))]
    got += [bit for bit in last[::-1] if bit not in got][: 2 - len(got)]
    stages = [(pair, pair, []) for pair in (bits[:-4][i : i + 2] for i in range(0, len(bits) - 4, 2))]
    stages.append((last, got, [bit for bit in last if bit not in got]))

    lookup = antenna_row_lookup.reshape(1, -1)
    placed, _ = lax.optimization_barrier((positions, beside[0]))
    ours, right, length, dirs, *maps = our_weights(
        placed, lookup, gains[:, 0], directions, chan_order, delays, masks, stages, bins
    )
    weights = [ours, their_weights(right, length, partner(dirs, [("beam", 0)]))]
    partial = early_beams(weights, [beside[0]] + first, ants * (chan_count - 2), ants - cut)
    partial = early_beams(weights, across + beside[1:], 0, 0, partial)

    high, low, *other = last_levels(weights, rest, partial, total)
    for number, ((_, got, sent), matrix) in enumerate(zip(stages, maps)):
        states = [high, low]
        for flips in subsets(got)[1:]:
            states.append(partner(other[len(flips) - 1] if ("beam", 0) in flips else high, flips))
        result = tree_stage(matrix, states, bins, directions.shape[1], number == 0, bool(sent))
        if not sent:
            high, low = result
    received = [partner(value, flips) for value, flips in zip(result[1:], subsets(sent)[1:])]
    return tree_sum(result[0], received).reshape(1, per_dev, bins, directions.shape[1])


def solution(mesh):
    placed = (
        P(None, "chan", "band", None, "group"),
        P(None, "band", "chan", None),
        P(),
        P(None, ("group", "beam")),
        P(),
        P(),
        P(),
    )
    return jax.shard_map(
        shards,
        mesh=mesh,
        in_specs=placed,
        out_specs=P("band", "chan", None, ("group", "beam")),
        check_vma=False,
    )
```

```python
import math

import jax
import jax.numpy as jnp
from jax import lax
from jax.experimental import pallas as pl
from jax.experimental.pallas import tpu as pltpu
from jax.sharding import PartitionSpec as P

INTEG = 8
VMEM = pl.BlockSpec(memory_space=pltpu.VMEM)
SMEM = pl.BlockSpec(memory_space=pltpu.SMEM)
PARAMS = pltpu.CompilerParams(vmem_limit_bytes=40 * 1024 * 1024)
SIN = (6.283184915580925, -41.34158901325128, 81.59993513909575, -76.61436771142901, 41.342343389037076, -12.470285565721209)
COS = (0.9999992089426497, -19.738979914331107, 64.92864094416844, -85.27141067260794, 58.789407905427666, -21.069178520245686)
PHASE_ROWS = 32
LONG = pl.CostEstimate(flops=10**10, bytes_accessed=10**8, transcendentals=10**8)
SHORT = pl.CostEstimate(flops=0, bytes_accessed=0, transcendentals=0)


def partner(value, flips):
    axes = tuple(axis for axis in ("chan", "band", "beam") if axis in dict(flips))
    sizes = [lax.axis_size(axis) for axis in axes]
    flip = 0
    for axis, bit in flips:
        flip ^= (1 << bit) * math.prod(sizes[axes.index(axis) + 1 :])
    pairs = [(source, source ^ flip) for source in range(math.prod(sizes))]
    return lax.ppermute(value, axes, pairs)


def chan_partner(value, mask):
    return partner(value, [("chan", bit) for bit in range(mask.bit_length()) if mask >> bit & 1])


def split_channels(voltages, pieces, from_hbm, token=None):
    parts, ants, _, chans, samples = voltages.shape
    per_dev = lax.axis_size("beam")
    start = min(first for _, first, _ in pieces)
    stop = max(last for _, _, last in pieces)
    group = max(16, (stop - start) // 2)
    jobs = [(p, first) for first in range(start, stop, group) for p in range(parts)]
    lanes = range(0, samples, 128)
    tokens = [] if token is None else [token]

    def kernel(v_ref, *refs):
        refs = refs[len(tokens) :]
        outs, wide, (raw, sems) = refs[: len(pieces)], refs[len(pieces) : -2], refs[-2:]
        z = lax.axis_index("chan")
        e = lax.axis_index("beam")

        def rows(number):
            p, first = jobs[number]
            return v_ref.at[p, pl.ds(first * chans, group * chans), :]

        def fetch(number):
            return pltpu.make_async_copy(rows(number), raw.at[number], sems.at[number])

        if from_hbm:
            for number in range(len(jobs)):
                fetch(number).start()
        for number, (p, first) in enumerate(jobs):
            if from_hbm:
                fetch(number).wait()
            block = raw.at[number] if from_hbm else rows(number)
            slot = number % 2
            for lane, half in zip(lanes, wide):
                half[slot, pl.ds(0, group * chans), :] = block[:, pl.ds(lane, 128)].astype(jnp.float32)
            for (mask, piece_first, piece_last), out in zip(pieces, outs):
                if piece_first <= first < piece_last:
                    chan = (z ^ mask) * per_dev + e
                    at = pl.ds(first - piece_first, group)
                    for lane, half in zip(lanes, wide):
                        out[p, at, pl.ds(lane, 128)] = half[slot, pl.ds(chan, group, stride=chans), :].astype(jnp.bfloat16)

    place = pltpu.HBM if from_hbm else pltpu.VMEM
    raw_slots = len(jobs) if from_hbm else 1
    return pl.pallas_call(
        kernel,
        in_specs=[pl.BlockSpec(memory_space=place)] + [pl.BlockSpec(memory_space=pl.ANY)] * len(tokens),
        out_specs=[VMEM] * len(pieces),
        out_shape=[
            jax.ShapeDtypeStruct((parts, last - first, samples), jnp.bfloat16) for _, first, last in pieces
        ],
        scratch_shapes=[pltpu.VMEM((2, (group + 1) * chans, 128), jnp.float32)] * len(lanes)
        + [
            pltpu.VMEM((raw_slots, group * chans, samples), jnp.bfloat16),
            pltpu.SemaphoreType.DMA((raw_slots,)),
        ],
        compiler_params=PARAMS,
        name="split_channels",
    )(pltpu.with_memory_space_constraint(voltages.reshape(parts, ants * chans, samples), place), *tokens)


def horner(coefs, u):
    total = coefs[-1] * u + coefs[-2]
    for coef in coefs[-3::-1]:
        total = total * u + coef
    return total


def bf16_parts(x):
    first = x.astype(jnp.bfloat16).astype(jnp.float32)
    rest = x - first
    second = rest.astype(jnp.bfloat16).astype(jnp.float32)
    return first, second, rest - second


def xor_blocks(x, index, count):
    size = x.shape[-1] // count
    for bit in range(count.bit_length() - 1):
        swapped = [x[..., (i ^ (1 << bit)) * size : (i ^ (1 << bit)) * size + size] for i in range(count)]
        x = jnp.where((index >> bit) & 1 == 1, jnp.concatenate(swapped, axis=-1), x)
    return x


def phase_rows(dirs):
    parts = jnp.concatenate(bf16_parts(dirs), axis=0)
    rows = [parts, parts, parts, jnp.ones((3, dirs.shape[1]), jnp.float32)]
    rows.append(jnp.zeros((PHASE_ROWS - 30, dirs.shape[1]), jnp.float32))
    return jnp.concatenate(rows, axis=0).astype(jnp.bfloat16)


def fill_weights(left_ref, right_ref, length_ref, turns, out):
    _, beams, ants = out.shape
    block = turns.shape[0]
    lanes = min(ants, 512)

    def block_of_beams(number, carry):
        start = pl.multiple_of(number * block, block)
        turns[...] = lax.dot_general(
            left_ref[:, pl.ds(start, block)],
            right_ref[...],
            (((0,), (0,)), ((), ())),
            preferred_element_type=jnp.float32,
        )

        def rows(step, carry):
            at = pl.ds(pl.multiple_of(step * 16, 16), 16)
            to = pl.ds(pl.multiple_of(start + step * 16, 16), 16)
            for lane in range(0, ants, lanes):
                cols = pl.ds(lane, lanes)
                x = turns[at, cols]
                t = x - jnp.round(x)
                u = t * t
                scale = length_ref[:, cols]
                out[0, to, cols] = (horner(COS, u) * scale).astype(jnp.bfloat16)
                out[1, to, cols] = (horner(SIN, u) * (t * scale)).astype(jnp.bfloat16)
            return carry

        return lax.fori_loop(0, block // 16, rows, carry)

    lax.fori_loop(0, beams // block, block_of_beams, 0)


def subsets(bits):
    return [[bit for k, bit in enumerate(bits) if pick >> k & 1] for pick in range(1 << len(bits))]


def map_shapes(stages, per_dev, bins):
    return [(per_dev, bins << len(sent), bins * (1 + (1 << len(got)))) for _, got, sent in stages]


def fill_maps(delay_ref, outs, stages, bins):
    per_dev = lax.axis_size("beam")

    def place(flips):
        at = {axis: lax.axis_index(axis) for axis in ("band", "chan", "beam")}
        for axis, bit in flips:
            at[axis] = at[axis] ^ (1 << bit)
        return at

    def total_delay(bits, first_round, target, source, slot):
        moved = 0
        for k, (axis, bit) in enumerate(bits):
            later = [b for b in bits[k + 1 :] if b in target or b in source]
            end = place(target + later)
            start = place(target + later + [b for b in bits[k : k + 1] if b in target or b in source])
            delay = delay_ref[first_round + k, end["band"], end["chan"] * per_dev + slot]
            moved = moved + ((start[axis] >> bit) & 1) * delay
        return moved

    first_round = 0
    for (bits, got, sent), out in zip(stages, outs):
        sources = [[]] + subsets(got)
        shape = (bins, out.shape[2])
        row = lax.broadcasted_iota(jnp.int32, shape, 0)
        col = lax.broadcasted_iota(jnp.int32, shape, 1)
        for slot in range(per_dev):
            for number, target in enumerate(subsets(sent)):
                shift = jnp.zeros_like(col)
                for place_no, source in enumerate(sources):
                    moved = total_delay(bits, first_round, target, source, slot)
                    shift = jnp.where(col // bins == place_no, moved, shift)
                hit = lax.rem(row - col + len(bits) * bins + shape[1] - shift, bins) == 0
                out[slot, pl.ds(number * bins, bins), :] = jnp.where(hit, 1.0, 0.0).astype(jnp.bfloat16)
        first_round += len(bits)


def our_weights(positions, lookup, gains, dirs, chan_order, delays, masks, stages, bins):
    ants, beams = positions.shape[1], dirs.shape[1]
    per_dev = lax.axis_size("beam")
    size = ants // len(masks)
    lanes = min(ants, 512)
    _, band_count, in_band = delays.shape
    shapes = map_shapes(stages, per_dev, bins)

    def in_order(x, z):
        x = xor_blocks(x, z, len(masks))
        return jnp.concatenate([x[..., m * size : m * size + size] for m in masks], axis=-1)

    def kernel(order_ref, delay_ref, pos_ref, look_ref, gain_ref, dir_ref, out, right_ref, length_ref, copy_ref, *refs):
        maps, (left, turns) = refs[:-2], refs[-2:]
        copy_ref[...] = dir_ref[...]
        z = lax.axis_index("chan")
        e = lax.axis_index("beam")
        slot = lax.axis_index("band") * in_band + z * per_dev + e
        freq = 1.0 + order_ref[slot].astype(jnp.float32) * (1.0 / (band_count * in_band))

        g_re = in_order(jnp.where(e == 0, gain_ref[0, 0:1, :], gain_ref[0, 1:2, :]), z)
        g_im = in_order(jnp.where(e == 0, gain_ref[1, 0:1, :], gain_ref[1, 1:2, :]), z)
        top = jnp.maximum(jnp.abs(g_re), jnp.abs(g_im))
        low = jnp.minimum(jnp.abs(g_re), jnp.abs(g_im))
        ratio = low / jnp.where(top > 0.0, top, 1.0)
        length_ref[...] = top * jnp.sqrt(1.0 + ratio * ratio) * (1.0 / math.sqrt(ants))

        parts = [jnp.concatenate([part] * 3, axis=0) for part in bf16_parts(pos_ref[...] * -freq)]
        parts.append(jnp.zeros((PHASE_ROWS - 27, ants), jnp.float32))
        table = jnp.concatenate(parts, axis=0).astype(jnp.bfloat16)
        look = in_order(look_ref[...], z)
        antenna = lax.broadcasted_iota(jnp.int32, (ants, lanes), 0)
        turn_parts = jnp.concatenate(
            [jnp.zeros((27, ants), jnp.float32)]
            + list(bf16_parts(jnp.arctan2(g_im, g_re) * (0.5 / math.pi)))
            + [jnp.zeros((PHASE_ROWS - 30, ants), jnp.float32)],
            axis=0,
        )
        for lane in range(0, ants, lanes):
            chosen = jnp.where(antenna == look[:, lane : lane + lanes], 1.0, 0.0).astype(jnp.bfloat16)
            rows = jnp.dot(table, chosen, preferred_element_type=jnp.float32)
            right_ref[:, pl.ds(lane, lanes)] = (rows + turn_parts[:, lane : lane + lanes]).astype(jnp.bfloat16)
        left[...] = phase_rows(dir_ref[...])
        fill_weights(left, right_ref, length_ref, turns, out)
        fill_maps(delay_ref, maps, stages, bins)

    return pl.pallas_call(
        kernel,
        in_specs=[SMEM] * 2 + [VMEM] * 4,
        out_specs=[VMEM] * (4 + len(shapes)),
        out_shape=[
            jax.ShapeDtypeStruct((2, beams, ants), jnp.bfloat16),
            jax.ShapeDtypeStruct((PHASE_ROWS, ants), jnp.bfloat16),
            jax.ShapeDtypeStruct((1, ants), jnp.float32),
            jax.ShapeDtypeStruct(dirs.shape, jnp.float32),
        ]
        + [jax.ShapeDtypeStruct(shape, jnp.bfloat16) for shape in shapes],
        scratch_shapes=[
            pltpu.VMEM((PHASE_ROWS, beams), jnp.bfloat16),
            pltpu.VMEM((min(beams, 128), ants), jnp.float32),
        ],
        compiler_params=PARAMS,
        cost_estimate=LONG,
        name="our_weights",
    )(chan_order, delays, positions, lookup, gains, dirs)


def their_weights(right, length, dirs):
    ants, beams = right.shape[1], dirs.shape[1]

    def kernel(right_ref, length_ref, dir_ref, out, left, turns):
        left[...] = phase_rows(dir_ref[...])
        fill_weights(left, right_ref, length_ref, turns, out)

    return pl.pallas_call(
        kernel,
        in_specs=[VMEM] * 3,
        out_specs=VMEM,
        out_shape=jax.ShapeDtypeStruct((2, beams, ants), jnp.bfloat16),
        scratch_shapes=[
            pltpu.VMEM((PHASE_ROWS, beams), jnp.bfloat16),
            pltpu.VMEM((min(beams, 128), ants), jnp.float32),
        ],
        compiler_params=PARAMS,
        cost_estimate=SHORT,
        name="their_weights",
    )(right, length, dirs)


def chunk_product(w_ref, blocks, first, beam_rows):
    re = jnp.concatenate([re for re, _ in blocks], axis=0)
    im = jnp.concatenate([im for _, im in blocks], axis=0)
    straight = jnp.concatenate([re, im], axis=1)
    turned = jnp.concatenate([-im, re], axis=1)
    cols = pl.ds(first, re.shape[0])
    dot = lambda a, b: jnp.dot(a, b, preferred_element_type=jnp.float32)
    return dot(w_ref[0, beam_rows, cols], straight) + dot(w_ref[1, beam_rows, cols], turned)


HIGH_EXTRA, OTHER_EXTRA = 1, (0, 2)
SUM_EXTRA = (0, 0, 1)


def filled(ref, before, after):
    zeros = lambda count: [jnp.zeros((count, ref.shape[2]), ref.dtype)] if count else []
    return [jnp.concatenate(zeros(before) + [ref[p]] + zeros(after), axis=0) for p in range(2)]


def early_beams(weights, chunks, first, rest, partial=None):
    half = weights[0].shape[1]
    samples = chunks[0].shape[2]
    step = min(half, 256)
    before = [] if partial is None else [partial]

    def kernel(ours_ref, theirs_ref, *refs):
        refs, out = refs[:-1], refs[-1]
        blocks = [filled(ref, 0, 0) for ref in refs[len(before) : -1]] + [filled(refs[-1], 0, rest)]
        for number, w_ref in enumerate((ours_ref, theirs_ref)):
            for row in range(0, half, step):
                product = chunk_product(w_ref, blocks, first, pl.ds(row, step))
                at = pl.ds(number * half + row, step)
                out[at, :] = product + refs[0][at, :] if before else product

    return pl.pallas_call(
        kernel,
        in_specs=[VMEM] * (2 + len(before) + len(chunks)),
        out_specs=VMEM,
        out_shape=jax.ShapeDtypeStruct((2 * half, 2 * samples), jnp.float32),
        compiler_params=PARAMS,
        cost_estimate=SHORT,
        name="early_beams",
    )(*weights, *before, *chunks)


def two_parts(x):
    high = x.astype(jnp.bfloat16)
    return high, (x - high.astype(jnp.float32)).astype(jnp.bfloat16)


def message(blocks, width, extra):
    return jax.ShapeDtypeStruct((blocks * width // 128 + 16 * extra, 128), jnp.bfloat16)


def put(ref, first, value):
    bins, width = value.shape
    for lane in range(0, width, 128):
        ref[pl.ds(first, bins), :] = value[:, lane : lane + 128].astype(ref.dtype)
        first += bins
    return first


def take(ref, number, bins, width):
    first = number * bins * width // 128
    pieces = [ref[pl.ds(first + lane // 128 * bins, bins), :] for lane in range(0, width, 128)]
    return jnp.concatenate(pieces, axis=1)


def pad(ref, first):
    if first < ref.shape[0]:
        ref[pl.ds(first, ref.shape[0] - first), :] = jnp.zeros((ref.shape[0] - first, 128), ref.dtype)


def last_levels(weights, chunk, partial, total):
    _, half, ants = weights[0].shape
    samples = chunk.shape[2]
    bins = samples // INTEG
    count = chunk.shape[1]
    first = ants - count

    def kernel(ours_ref, theirs_ref, part_ref, chunk_ref, high_ref, low_ref, *sent_refs):
        re, im = chunk_ref[0], chunk_ref[1]
        antennas = jnp.concatenate(
            [jnp.concatenate([re, im], axis=1), jnp.concatenate([-im, re], axis=1)], axis=0
        )
        bin_no = lax.broadcasted_iota(jnp.int32, (bins, samples), 0)
        time = lax.broadcasted_iota(jnp.int32, (bins, samples), 1)
        centre = jnp.where(time // INTEG == bin_no, 1.0 / INTEG, 0.0) - 1.0 / samples
        centre = jnp.concatenate([centre, centre], axis=1).astype(jnp.bfloat16)
        beams = []
        for number, w_ref in enumerate((ours_ref, theirs_ref)):
            both = jnp.concatenate([w_ref[0, :, pl.ds(first, count)], w_ref[1, :, pl.ds(first, count)]], axis=1)
            product = jnp.dot(both, antennas, preferred_element_type=jnp.float32)
            beams.append(part_ref[pl.ds(number * half, half), :] + product)
        for number, beam in enumerate(beams):
            re, im = beam[:, :samples], beam[:, samples:]
            parts = jnp.concatenate(two_parts(re * re + im * im), axis=1)
            level = lax.dot_general(centre, parts, (((1,), (1,)), ((), ())), preferred_element_type=jnp.float32)
            high, low = two_parts(level * (1.0 / math.sqrt(total)))
            if number == 0:
                pad(high_ref, put(high_ref, 0, high))
                put(low_ref, 0, low)
            else:
                for sent_ref in sent_refs:
                    pad(sent_ref, put(sent_ref, 0, high))

    return pl.pallas_call(
        kernel,
        in_specs=[VMEM] * 4,
        out_specs=[VMEM] * 4,
        out_shape=[message(bins, half, extra) for extra in (HIGH_EXTRA, 0, *OTHER_EXTRA)],
        compiler_params=PARAMS,
        name="last_levels",
    )(*weights, partial, chunk)


def tree_stage(matrix, states, bins, width, first, final):
    slots, rows, _ = matrix.shape
    targets = rows // bins
    blocks = bins * slots
    if final:
        shapes = [jax.ShapeDtypeStruct((slots, bins, width), jnp.float32)]
        shapes += [message(blocks, width, extra) for extra in SUM_EXTRA[: targets - 1]]
    else:
        shapes = [message(blocks, width, 0)] * 2

    def kernel(map_ref, *refs):
        ins, outs = refs[: len(states)], refs[len(states) :]
        row = 0
        for slot in range(slots):
            column = [take(ref, 0 if first else slot, bins, width) for ref in ins]
            value = jnp.dot(map_ref[slot], jnp.concatenate(column, axis=0), preferred_element_type=jnp.float32)
            if final:
                outs[0][slot] = value[:bins]
                parts = [value[t * bins : t * bins + bins] for t in range(1, targets)]
            else:
                parts = two_parts(value)
            for out, part in zip(outs[-len(parts) :], parts):
                after = put(out, row, part)
            row = after
        for out in outs[-len(parts) :]:
            pad(out, row)

    return pl.pallas_call(
        kernel,
        in_specs=[VMEM] * (1 + len(states)),
        out_specs=[VMEM] * len(shapes),
        out_shape=shapes,
        compiler_params=PARAMS,
        name="tree_stage",
    )(matrix, *states)


def tree_sum(own, received):
    slots, bins, width = own.shape

    def kernel(own_ref, *refs):
        out, total, sems = refs[-3:]
        copies = [pltpu.make_async_copy(total.at[slot], out.at[slot], sems.at[slot]) for slot in range(slots)]
        for slot, copy in enumerate(copies):
            value = own_ref[slot]
            for ref in refs[:-3]:
                value = value + take(ref, slot, bins, width).astype(jnp.float32)
            total[slot] = value
            copy.start()
        for copy in copies:
            copy.wait()

    return pl.pallas_call(
        kernel,
        in_specs=[VMEM] * (1 + len(received)),
        out_specs=pl.BlockSpec(memory_space=pltpu.HBM),
        out_shape=jax.ShapeDtypeStruct(own.shape, jnp.float32),
        scratch_shapes=[pltpu.VMEM(own.shape, jnp.float32), pltpu.SemaphoreType.DMA((slots,))],
        compiler_params=PARAMS,
        name="tree_sum",
    )(own, *received)


def shards(voltages, gains, positions, directions, antenna_row_lookup, chan_order, delays):
    chan_count = lax.axis_size("chan")
    band_count = lax.axis_size("band")
    per_dev = gains.shape[2]
    assert per_dev == lax.axis_size("beam") == 2
    in_band = per_dev * chan_count
    total = in_band * band_count
    ants, samples = voltages.shape[1], voltages.shape[4]
    bins = samples // INTEG

    middle = chan_count // 2
    near = list(range(middle))
    distant = list(range(chan_count - 2, middle - 1, -1))
    middle = chan_count - 1
    masks = distant + near[1:] + [0, middle]
    cut = ants // 2
    first = split_channels(voltages, [(middle, 0, cut)], True)
    across = split_channels(voltages, [(m, 0, ants) for m in distant], True, first[0])
    *beside, rest = split_channels(voltages, [(m, 0, ants) for m in near] + [(middle, cut, ants)], True, across[0])
    first = [chan_partner(first[0], middle)]
    across = [chan_partner(v, m) for v, m in zip(across, distant)]
    rest = chan_partner(rest, middle)
    beside = [beside[0]] + [chan_partner(v, m) for v, m in zip(beside[1:], near[1:])]

    bits = [("beam", 0)]
    for axis, count in (("chan", chan_count), ("band", band_count)):
        bits += [(axis, bit) for bit in range(count.bit_length() - 1)]
    last = bits[-4:]
    got = [bit for bit in last if bit in (("beam", 0), ("chan", chan_count.bit_length() - 2))]
    got += [bit for bit in last[::-1] if bit not in got][: 2 - len(got)]
    stages = [(pair, pair, []) for pair in (bits[:-4][i : i + 2] for i in range(0, len(bits) - 4, 2))]
    stages.append((last, got, [bit for bit in last if bit not in got]))

    lookup = antenna_row_lookup.reshape(1, -1)
    placed, _ = lax.optimization_barrier((positions, beside[0]))
    ours, right, length, dirs, *maps = our_weights(
        placed, lookup, gains[:, 0], directions, chan_order, delays, masks, stages, bins
    )
    weights = [ours, their_weights(right, length, partner(dirs, [("beam", 0)]))]
    partial = early_beams(weights, [beside[0]] + first, ants * (chan_count - 2), ants - cut)
    partial = early_beams(weights, across + beside[1:], 0, 0, partial)

    high, low, *other = last_levels(weights, rest, partial, total)
    for number, ((_, got, sent), matrix) in enumerate(zip(stages, maps)):
        states = [high, low]
        for flips in subsets(got)[1:]:
            states.append(partner(other[len(flips) - 1] if ("beam", 0) in flips else high, flips))
        result = tree_stage(matrix, states, bins, directions.shape[1], number == 0, bool(sent))
        if not sent:
            high, low = result
    received = [partner(value, flips) for value, flips in zip(result[1:], subsets(sent)[1:])]
    return tree_sum(result[0], received).reshape(1, per_dev, bins, directions.shape[1])


def solution(mesh):
    placed = (
        P(None, "chan", "band", None, "group"),
        P(None, "band", "chan", None),
        P(),
        P(None, ("group", "beam")),
        P(),
        P(),
        P(),
    )
    return jax.shard_map(
        shards,
        mesh=mesh,
        in_specs=placed,
        out_specs=P("band", "chan", None, ("group", "beam")),
        check_vma=False,
    )
```
